32 devices in a mesh: groups: 2 (over y), seq: 4 (over z), tp: 2 (over x), rep: 2 (over core).
Axes of the slice: x: 2, y: 2, z: 4, core: 2. Of those that a mesh axis runs over, the one named last changes fastest.
Arguments:
- queries: bfloat16 [1024, 8192], P(('groups', 'seq'), ('tp', 'rep')), parts along dimension 0, may hold values from -8 to 8
- keys: bfloat16 [1024, 1024], P(('groups', 'seq'), ('tp', 'rep')), parts along dimension 0, may hold values from -5 to 5
- values: bfloat16 [1024, 1024], P(('groups', 'seq'), ('tp', 'rep')), parts along dimension 0, may hold values from -6 to 6
- query_owner: int32 [1024, 1], P(('groups', 'seq')), parts along dimension 0, may hold values from 0 to 3; in each aligned block of 128 rows (0 to 127, 128 to 255, ...) at most 48 rows name the same one
- cache_owner: int32 [1024, 1], P(('groups', 'seq')), parts along dimension 0, may hold values from 0 to 3; in each aligned block of 128 rows (0 to 127, 128 to 255, ...) at most 48 rows name the same one
Outputs:
- attended: bfloat16 [1536, 8192], P(('groups', 'seq'), ('tp', 'rep')), parts along dimension 0
- key_cache: bfloat16 [1536, 1024], P(('groups', 'seq'), ('tp', 'rep')), parts along dimension 0
- value_cache: bfloat16 [1536, 1024], P(('groups', 'seq'), ('tp', 'rep')), parts along dimension 0
The draws below stay inside these ranges and needn't reach their ends.
There are 2 independent parts, one for each index of `groups`. The reference program is written for one: setup_inputs(seed, part) draws one part's arguments, and reference() takes and returns one part's arrays. A program takes and returns all parts, laid end to end along the dimension named above; each array names one. Nothing has to cross between parts.
Inputs may be any that keep to these rules, and one draw needn't show every extreme that they name: `query_owner`: among the rows of one instance no instance is named more than 48 times. `cache_owner`: among the rows of one instance no instance is named more than 48 times.
All inputs are finite; a program needn't handle non-finite values.
Results may differ from the reference program's by a relative error of at most 0.0045.
Values may be sent and summed in bfloat16 or wider, within the bound.
No kernel may reach another device: no remote copies, remote signals or barrier semaphores. Data moves between devices by JAX's collectives and lax.ppermute only.
A program may use at most 64 MiB of HBM per device.

```python
import math
import jax
import jax.numpy as jnp
import numpy as np
from jax import lax

HQ = 64
KVH = 8
HD = 128
TOK_DEV = 128
TOKENS = 512
CAP = 48
SLOTS = 768
N_SEQ = 4


def draw_queries(key, part):
    key = jax.random.fold_in(key, 1)
    base = jnp.clip(2.0 * jax.random.normal(key, (TOKENS, HQ * HD), jnp.float32), -8.0, 8.0)
    return base.astype(jnp.bfloat16)


def draw_keys(key, part):
    key = jax.random.fold_in(key, 2)
    base = jnp.clip(jax.random.normal(key, (TOKENS, KVH * HD), jnp.float32), -5.0, 5.0)
    return base.astype(jnp.bfloat16)


def shard_levels(stream_key, shape, pieces, least, high):
    gain, own = 1.0, jax.random.fold_in(stream_key, 6)
    for position, blocks in pieces:
        draws = jnp.exp(jax.random.uniform(jax.random.fold_in(own, position), (blocks,), jnp.float32, least / len(pieces), high / len(pieces)))
        gain = gain * jnp.repeat(draws, shape[position] // blocks).reshape([-1 if axis == position else 1 for axis in range(len(shape))])
    return gain


def shared_out(own_key, own, number, rows, count, top, limit, lean):
    sequence = jax.random.permutation(own_key, count)
    packed, common = shares(count, rows * top, limit, lean, True), shares(count, rows * top, limit, lean, False)
    places = jnp.arange(count)

    def named(sizes, offset_by):
        used = int((sizes > 0).sum())
        fixed = max(1, used // 4)
        passed = fixed + (places - fixed + offset_by * (used - fixed)) % max(1, count - fixed)
        return jnp.zeros((count,), jnp.int32).at[sequence[jnp.where(places < fixed, places, passed)]].set(jnp.asarray(sizes, jnp.int32))

    sizes = jnp.where(number % 4 == 0, named(packed, number // 4), named(common, number - number // 4 - 1))
    mixed = jax.random.permutation(jax.random.fold_in(own, 3), count)
    donor, receiver = mixed[0:count // 2 * 2:2], mixed[1:count // 2 * 2:2]
    margin = jnp.minimum(sizes[donor] - 1, limit - sizes[receiver]) // 2
    margin = jnp.where((donor == sequence[0]) | (receiver == sequence[0]) | (sizes[receiver] == 0), 0, jnp.maximum(margin, 0))
    passed = jax.random.randint(jax.random.fold_in(own, 4), (count // 2,), 0, 1 << 20) % (margin + 1)
    sizes = sizes.at[donor].add(-passed).at[receiver].add(passed)
    labels = jnp.searchsorted(jnp.cumsum(sizes), jnp.arange(rows * top), side="right").astype(jnp.int32)
    table = labels.reshape(top, rows).T
    table = table[jax.random.permutation(jax.random.fold_in(own, 1), rows)]
    offset_by = jax.random.randint(jax.random.fold_in(own, 2), (rows, 1), 0, top)
    return jnp.take_along_axis(table, (jnp.arange(top)[None, :] + offset_by) % top, axis=1)


def shares(count, total, limit, skew, full):
    weights = [(1 << 20) // math.isqrt(standing ** skew) + 1 for standing in range(1, count + 1)]
    largest = limit if full else min(limit, max(-(-total // count), total * weights[0] // sum(weights)))
    least = 1 if total - largest >= count - 1 else 0
    counts, spare = [largest] + [least] * (count - 1), total - largest - least * (count - 1)
    while spare > 0:
        free = [i for i in range(1, count) if counts[i] < largest] or [i for i in range(1, count) if counts[i] < limit]
        pool, budget = sum([weights[i] for i in free]), spare
        for i in free:
            addition = min(limit - counts[i], max(1, budget * weights[i] // pool), spare)
            counts[i] = counts[i] + addition
            spare = spare - addition
    return np.array(counts)


def normal_values(rng, shape, deviation, most, pieces=(), kind=jnp.bfloat16):
    factor_of = shard_levels(rng, shape, pieces, -0.22, 0.18) if pieces else 1.0
    values = jax.random.normal(rng, shape, jnp.float32) * deviation * factor_of
    return jnp.minimum(jnp.maximum(values, -most), most).astype(kind)


def setup_inputs(seed: int = 0, part: int = 0) -> dict:
    splits = jax.random.split(jax.random.key(seed), 6)
    part_keys = jax.random.split(jax.random.fold_in(splits[5], part), 6)
    queries = draw_queries(jax.random.fold_in(jax.random.fold_in(splits[5], part), 71), part)
    keys = draw_keys(jax.random.fold_in(jax.random.fold_in(splits[5], part), 71), part)
    values = normal_values(part_keys[2], (TOKENS, KVH * HD), 1.0, 6.0, ((0, 4), (1, 4)))
    query_owner_keys = jax.random.split(jax.random.fold_in(part_keys[3], 1), TOKENS // TOK_DEV)
    query_owner_turns = jax.random.permutation(jax.random.fold_in(part_keys[3], 3), TOKENS // TOK_DEV)
    query_owner = jax.vmap(lambda own, number: shared_out(jax.random.fold_in(part_keys[3], 2), own, number, TOK_DEV, N_SEQ, 1, CAP, 2))(query_owner_keys, query_owner_turns).reshape((TOKENS, 1))
    cache_owner_keys = jax.random.split(jax.random.fold_in(part_keys[4], 1), TOKENS // TOK_DEV)
    cache_owner_turns = jax.random.permutation(jax.random.fold_in(part_keys[4], 3), TOKENS // TOK_DEV)
    cache_owner = jax.vmap(lambda own, number: shared_out(jax.random.fold_in(part_keys[4], 2), own, number, TOK_DEV, N_SEQ, 1, CAP, 2))(cache_owner_keys, cache_owner_turns).reshape((TOKENS, 1))
    return {"queries": queries, "keys": keys, "values": values, "query_owner": query_owner, "cache_owner": cache_owner}


neg_big = -1e+30

def slot_rows(owner_list):
    owners = owner_list[:, 0].reshape(N_SEQ, TOK_DEV)
    onehot = (owners[:, :, None] == jnp.arange(N_SEQ, dtype=jnp.int32)[None, None, :]).astype(jnp.int32)
    earlier = jnp.cumsum(onehot, axis=1) - onehot
    ranking = lax.optimization_barrier(jnp.sum(earlier * onehot, axis=2))
    sources = jnp.arange(N_SEQ, dtype=jnp.int32)[:, None]
    return (owners * (N_SEQ * CAP) + sources * CAP + ranking).reshape(-1).astype(jnp.int32)

def causal_attention(queries, keys, values):
    per_group = HQ // KVH
    block_rows = min(512, TOKENS)
    scale = 1.0 / math.sqrt(HD)
    query_heads = jnp.transpose(queries.reshape(TOKENS, KVH, per_group, HD), (1, 0, 2, 3))
    key_heads = jnp.transpose(keys.reshape(TOKENS, KVH, HD), (1, 0, 2))
    value_heads = jnp.transpose(values.reshape(TOKENS, KVH, HD), (1, 0, 2))
    key_pos = jnp.arange(TOKENS, dtype=jnp.int32)

    def one_head(operands):
        query_one, key_one, value_one = operands
        key_wide = key_one.astype(jnp.float32)
        value_wide = value_one.astype(jnp.float32)
        blocks = query_one.reshape(TOKENS // block_rows, block_rows, per_group, HD)

        def one_block(block_args):
            query_block, block_index = block_args
            scores = jnp.einsum('rgd,nd->grn', query_block.astype(jnp.float32), key_wide) * scale
            query_pos = block_index * block_rows + jnp.arange(block_rows, dtype=jnp.int32)
            allowed = key_pos[None, :] <= query_pos[:, None]
            scores = jnp.where(allowed, scores, neg_big)
            row_max = lax.optimization_barrier(jnp.max(scores, axis=-1, keepdims=True))
            weights = jnp.where(allowed, jnp.exp(scores - row_max), 0.0).astype(jnp.bfloat16)
            wide_weights = weights.astype(jnp.float32)
            weight_sum = lax.optimization_barrier(jnp.sum(wide_weights, axis=-1))
            mixed = jnp.einsum('grn,nd->grd', wide_weights, value_wide)
            return (mixed / weight_sum[..., None]).astype(jnp.bfloat16)
        result = lax.map(one_block, (blocks, jnp.arange(TOKENS // block_rows, dtype=jnp.int32)))
        return jnp.transpose(result, (0, 2, 1, 3)).reshape(TOKENS, per_group, HD)
    per_head = lax.map(one_head, (query_heads, key_heads, value_heads))
    return jnp.transpose(per_head, (1, 0, 2, 3)).reshape(TOKENS, HQ * HD)

def reference(queries, keys, values, query_owner, cache_owner):
    attention = causal_attention(queries, keys, values)
    query_slot = slot_rows(query_owner)
    cache_slot = slot_rows(cache_owner)
    attended = jnp.zeros((SLOTS, HQ * HD), jnp.bfloat16).at[query_slot].set(attention)
    key_cache = jnp.zeros((SLOTS, KVH * HD), jnp.bfloat16).at[cache_slot].set(keys)
    value_cache = jnp.zeros((SLOTS, KVH * HD), jnp.bfloat16).at[cache_slot].set(values)
    return (attended, key_cache, value_cache)
```

```python
import functools
import math

import jax
import jax.numpy as jnp
from jax import lax
from jax.experimental import pallas as pl
from jax.experimental.pallas import tpu as pltpu
from jax.sharding import PartitionSpec as P

HD = 128


neg_big = -1e30


def slot_select(owner_list, instances, capacity):
    owners = owner_list[:, 0]
    onehot = (owners[:, None] == jnp.arange(instances, dtype=jnp.int32)[None, :]).astype(jnp.int32)
    earlier = jnp.cumsum(onehot, axis=0) - onehot
    ranking = jnp.sum(earlier * onehot, axis=1)
    target = owners * capacity + ranking
    return target[None, :] == jnp.arange(instances * capacity, dtype=jnp.int32)[:, None]


def pack_rows(select, table_rows, instances):
    selected = jnp.dot(
        select.astype(table_rows.dtype), table_rows, preferred_element_type=jnp.float32
    )
    return selected.astype(table_rows.dtype).reshape(instances, -1, table_rows.shape[1])


def start_state(heads_kv, per_group, slot_count):
    running_max = jnp.full((heads_kv, per_group, slot_count), neg_big, jnp.float32)
    running_sum = jnp.zeros((heads_kv, per_group, slot_count), jnp.float32)
    weighted = jnp.zeros((heads_kv, per_group, slot_count, HD), jnp.float32)
    return (running_max, running_sum, weighted)


def key_block(current, grouped, query_pos, key_piece, value_piece, key_start):
    running_max, running_sum, weighted = current
    key_count = key_piece.shape[0]
    heads_kv = grouped.shape[1]
    key_heads = key_piece.reshape(key_count, heads_kv, HD)
    value_heads = value_piece.reshape(key_count, heads_kv, HD)
    scores = jnp.einsum("rkgd,nkd->kgrn", grouped, key_heads, preferred_element_type=jnp.float32)
    scores = scores * (1.0 / math.sqrt(HD))
    key_pos = key_start + jnp.arange(key_count, dtype=jnp.int32)
    allowed = key_pos[None, :] <= query_pos[:, None]
    scores = jnp.where(allowed, scores, neg_big)
    new_max = jnp.maximum(running_max, jnp.max(scores, axis=-1))
    weights = jnp.where(allowed, jnp.exp(scores - new_max[..., None]), 0.0).astype(jnp.bfloat16)
    rescale = jnp.exp(running_max - new_max)
    running_sum = running_sum * rescale + jnp.sum(weights, axis=-1, dtype=jnp.float32)
    weighted = weighted * rescale[..., None] + jnp.einsum(
        "kgrn,nkd->kgrd", weights, value_heads, preferred_element_type=jnp.float32
    )
    return (new_max, running_sum, weighted)


def folder(grouped, query_pos, current, pieces):
    last_pos = jnp.max(query_pos)
    key_part, value_part = pieces
    key_count = key_part.shape[0]
    block_rows = math.gcd(512, key_count)
    block_count = key_count // block_rows
    key_blocks = key_part.reshape(block_count, block_rows, key_part.shape[1])
    value_blocks = value_part.reshape(block_count, block_rows, value_part.shape[1])

    def visit(carried, block_item):
        block_index, key_piece, value_piece = block_item
        key_start = block_index * block_rows
        updated = lax.cond(
            key_start <= last_pos,
            lambda inner: key_block(inner, grouped, query_pos, key_piece, value_piece, key_start),
            lambda inner: inner,
            carried,
        )
        return (updated, None)

    current, _ = lax.scan(
        visit, current, (jnp.arange(block_count, dtype=jnp.int32), key_blocks, value_blocks)
    )
    return current


def finish(current, slot_count):
    running_max, running_sum, weighted = current
    denominator = jnp.where(running_sum > 0.0, running_sum, 1.0)
    averaged = weighted / denominator[..., None]
    return jnp.transpose(averaged, (2, 0, 1, 3)).reshape(slot_count, -1).astype(jnp.bfloat16)


def many_instances(queries, keys, values, query_owner, cache_owner):
    instances = lax.axis_size("seq")
    own_index = lax.axis_index("seq")
    local_rows = queries.shape[0]
    capacity = 3 * local_rows // (2 * instances)
    slot_count = instances * capacity
    heads_kv = keys.shape[1] // HD
    per_group = queries.shape[1] // keys.shape[1]
    positions = own_index * local_rows + jnp.arange(local_rows, dtype=jnp.int32)
    cache_pick = slot_select(cache_owner, instances, capacity)
    key_slots = pack_rows(cache_pick, keys, instances)
    value_slots = pack_rows(cache_pick, values, instances)
    query_pick = slot_select(query_owner, instances, capacity)
    query_slots = pack_rows(query_pick, queries, instances)
    slot_pos = jnp.max(jnp.where(query_pick, positions[None, :], -1), axis=1).reshape(
        instances, capacity
    )
    query_got, pos_got, key_got, value_got = (
        lax.all_to_all(query_slots, "seq", split_axis=0, concat_axis=0, tiled=True),
        lax.all_to_all(slot_pos, "seq", split_axis=0, concat_axis=0, tiled=True),
        lax.all_to_all(key_slots, "seq", split_axis=0, concat_axis=0, tiled=True),
        lax.all_to_all(value_slots, "seq", split_axis=0, concat_axis=0, tiled=True),
    )
    arrived = query_got.reshape(slot_count, -1)
    arrived_pos = pos_got.reshape(slot_count)
    grouped = arrived.reshape(slot_count, heads_kv, per_group, HD)
    final_state = folder(
        grouped,
        arrived_pos,
        start_state(heads_kv, per_group, slot_count),
        (
            lax.all_gather(keys, "seq", axis=0, tiled=True),
            lax.all_gather(values, "seq", axis=0, tiled=True),
        ),
    )
    attended = finish(final_state, slot_count)
    key_cache = key_got.reshape(slot_count, -1)
    value_cache = value_got.reshape(slot_count, -1)
    return (attended, key_cache, value_cache)


def before(rows):
    r = lax.broadcasted_iota(jnp.int32, (rows, rows), 0)
    u = lax.broadcasted_iota(jnp.int32, (rows, rows), 1)
    return (r < u).astype(jnp.bfloat16)


def picks(marks, earlier, capacity):
    rows = marks.shape[1]
    slot = lax.broadcasted_iota(jnp.int32, (capacity, rows), 0).astype(jnp.float32)
    chosen = jnp.where(marks > 0.5, earlier, -1.0)
    return (chosen == slot).astype(jnp.bfloat16)


def pack_kernel(instances, capacity, q_ref, k_ref, v_ref, qo_ref, co_ref, send_ref):
    rows = q_ref.shape[0]
    heads = q_ref.shape[1] // HD
    heads_kv = k_ref.shape[1] // HD
    owners = qo_ref[...]
    lanes = max(16, instances)
    dest = lax.broadcasted_iota(jnp.int32, (lanes, rows), 0)
    marks = (jnp.broadcast_to(owners, (lanes, rows)) == dest).astype(jnp.bfloat16)
    earlier = jnp.dot(marks, before(rows), preferred_element_type=jnp.float32)
    wide = marks.astype(jnp.float32)
    select = jnp.concatenate(
        [picks(wide[d : d + 1], earlier[d : d + 1], capacity) for d in range(instances)], axis=0
    )
    for pair in range(heads // 2):
        packed = jnp.dot(
            select,
            q_ref[:, pair * 2 * HD : (pair + 1) * 2 * HD],
            preferred_element_type=jnp.float32,
        ).astype(jnp.bfloat16)
        for d in range(instances):
            for half in range(2):
                at = (2 * pair + half) * capacity
                send_ref[d, at : at + capacity, :] = packed[
                    d * capacity : (d + 1) * capacity, half * HD : (half + 1) * HD
                ]
    base = heads * capacity
    lists = jnp.concatenate(
        [owners, co_ref[...], jnp.full((14, rows), -1, jnp.int32)], axis=0
    ).astype(jnp.float32).astype(jnp.bfloat16)
    for d in range(instances):
        for g in range(heads_kv):
            send_ref[d, base + g * rows : base + (g + 1) * rows, :] = k_ref[:, g * HD : (g + 1) * HD]
            at = base + (heads_kv + g) * rows
            send_ref[d, at : at + rows, :] = v_ref[:, g * HD : (g + 1) * HD]
        at = base + 2 * heads_kv * rows
        send_ref[d, at : at + 16, :] = lists


def attend_kernel(
    instances, capacity, heads, heads_kv, me_ref, got_ref, att_ref, kc_ref, vc_ref, keys, vals
):
    rows = 128
    per_group = heads // heads_kv
    base = heads * capacity
    tail = base + 2 * heads_kv * rows
    me = me_ref[0].astype(jnp.float32)
    lists = jnp.concatenate([got_ref[s, tail : tail + 16, :] for s in range(instances)], axis=0)
    wide = (lists.astype(jnp.float32) == me).astype(jnp.float32)
    earlier = jnp.dot(wide.astype(jnp.bfloat16), before(rows), preferred_element_type=jnp.float32)
    r = lax.broadcasted_iota(jnp.int32, (rows, 2 * rows), 0)
    u = lax.broadcasted_iota(jnp.int32, (rows, 2 * rows), 1)
    reach = ((u <= r) | (u >= rows)).astype(jnp.bfloat16)
    for s in range(instances):
        for g in range(heads_kv):
            keys[g, s * rows : (s + 1) * rows, :] = got_ref[s, base + g * rows : base + (g + 1) * rows, :]
            at = base + (heads_kv + g) * rows
            vals[g, s * rows : (s + 1) * rows, :HD] = got_ref[s, at : at + rows, :]
            vals[g, s * rows : (s + 1) * rows, HD:] = jnp.ones((rows, HD), jnp.bfloat16)
    scale = 1.0 / math.sqrt(HD)
    for s in range(instances):
        q_at, c_at = 16 * s, 16 * s + 1
        cache_pick = picks(wide[c_at : c_at + 1], earlier[c_at : c_at + 1], capacity)
        query_pick = picks(wide[q_at : q_at + 1], earlier[q_at : q_at + 1], capacity)
        slots = slice(s * capacity, (s + 1) * capacity)
        for g in range(heads_kv):
            columns = slice(g * HD, (g + 1) * HD)
            both = jnp.concatenate(
                [
                    got_ref[s, base + g * rows : base + (g + 1) * rows, :],
                    got_ref[s, base + (heads_kv + g) * rows : base + (heads_kv + g + 1) * rows, :],
                ],
                axis=1,
            )
            cached = jnp.dot(cache_pick, both, preferred_element_type=jnp.float32).astype(jnp.bfloat16)
            kc_ref[slots, columns] = cached[:, :HD]
            vc_ref[slots, columns] = cached[:, HD:]
        allowed = jnp.dot(query_pick, reach, preferred_element_type=jnp.float32)
        near = jnp.concatenate([allowed[:, :rows]] * per_group, axis=0) > 0.5
        valid = jnp.concatenate([allowed[:, rows:]] * per_group, axis=0) > 0.5
        for g in range(heads_kv):
            wanted = got_ref[s, g * per_group * capacity : (g + 1) * per_group * capacity, :]
            scores = lax.dot_general(
                wanted,
                keys[g, : (s + 1) * rows, :],
                (((1,), (1,)), ((), ())),
                preferred_element_type=jnp.float32,
            )
            last = jnp.where(near, scores[:, s * rows :], neg_big)
            scores = jnp.concatenate([scores[:, : s * rows], last], axis=1) if s else last
            top = jnp.max(scores, axis=1, keepdims=True)
            weights = jnp.exp((scores - top) * scale).astype(jnp.bfloat16)
            mixed = jnp.dot(weights, vals[g, : (s + 1) * rows, :], preferred_element_type=jnp.float32)
            out = jnp.where(valid, mixed[:, :HD] / mixed[:, HD:], 0.0).astype(jnp.bfloat16)
            for h in range(per_group):
                column = (g * per_group + h) * HD
                att_ref[slots, column : column + HD] = out[h * capacity : (h + 1) * capacity, :]


def few_instances(queries, keys, values, query_owner, cache_owner):
    instances = lax.axis_size("seq")
    rows = queries.shape[0]
    capacity = 3 * rows // (2 * instances)
    heads, heads_kv = queries.shape[1] // HD, keys.shape[1] // HD
    height = heads * capacity + 2 * heads_kv * rows + 16
    vmem = pl.BlockSpec(memory_space=pltpu.VMEM)
    send = pl.pallas_call(
        functools.partial(pack_kernel, instances, capacity),
        out_shape=jax.ShapeDtypeStruct((instances, height, HD), jnp.bfloat16),
        in_specs=[vmem] * 5,
        out_specs=vmem,
        compiler_params=pltpu.CompilerParams(vmem_limit_bytes=16 << 20),
        name="pack",
    )(queries, keys, values, query_owner.reshape(1, rows), cache_owner.reshape(1, rows))
    got = lax.all_to_all(send, "seq", split_axis=0, concat_axis=0, tiled=True)
    me = lax.axis_index("seq").astype(jnp.int32).reshape(1)
    slots = instances * capacity
    return pl.pallas_call(
        functools.partial(attend_kernel, instances, capacity, heads, heads_kv),
        out_shape=(
            jax.ShapeDtypeStruct((slots, heads * HD), jnp.bfloat16),
            jax.ShapeDtypeStruct((slots, heads_kv * HD), jnp.bfloat16),
            jax.ShapeDtypeStruct((slots, heads_kv * HD), jnp.bfloat16),
        ),
        in_specs=[pl.BlockSpec(memory_space=pltpu.SMEM), vmem],
        out_specs=(vmem, vmem, vmem),
        scratch_shapes=[
            pltpu.VMEM((heads_kv, instances * rows, HD), jnp.bfloat16),
            pltpu.VMEM((heads_kv, instances * rows, 2 * HD), jnp.bfloat16),
        ],
        compiler_params=pltpu.CompilerParams(vmem_limit_bytes=24 << 20),
        name="attend",
    )(me, got)


def on_device(queries, keys, values, query_owner, cache_owner):
    instances = lax.axis_size("seq")
    rows = queries.shape[0]
    capacity = 3 * rows // (2 * instances)
    heads = queries.shape[1] // HD
    whole_tiles = capacity % 16 == 0 and rows == HD and heads % 2 == 0
    form = few_instances if whole_tiles else many_instances
    return form(queries, keys, values, query_owner, cache_owner)


def solution(mesh):
    return jax.shard_map(
        on_device,
        mesh=mesh,
        in_specs=(
            P(("groups", "seq"), ("tp", "rep")),
            P(("groups", "seq"), ("tp", "rep")),
            P(("groups", "seq"), ("tp", "rep")),
            P(("groups", "seq"), None),
            P(("groups", "seq"), None),
        ),
        out_specs=(
            P(("groups", "seq"), ("tp", "rep")),
            P(("groups", "seq"), ("tp", "rep")),
            P(("groups", "seq"), ("tp", "rep")),
        ),
        check_vma=False,
    )
```

```python
import functools
import math

import jax
import jax.numpy as jnp
from jax import lax
from jax.experimental import pallas as pl
from jax.experimental.pallas import tpu as pltpu
from jax.sharding import PartitionSpec as P

HD = 128


neg_big = -1e30


def slot_select(owner_list, instances, capacity):
    owners = owner_list[:, 0]
    onehot = (owners[:, None] == jnp.arange(instances, dtype=jnp.int32)[None, :]).astype(jnp.int32)
    earlier = jnp.cumsum(onehot, axis=0) - onehot
    ranking = jnp.sum(earlier * onehot, axis=1)
    target = owners * capacity + ranking
    return target[None, :] == jnp.arange(instances * capacity, dtype=jnp.int32)[:, None]


def pack_rows(select, table_rows, instances):
    selected = jnp.dot(
        select.astype(table_rows.dtype), table_rows, preferred_element_type=jnp.float32
    )
    return selected.astype(table_rows.dtype).reshape(instances, -1, table_rows.shape[1])


def start_state(heads_kv, per_group, slot_count):
    running_max = jnp.full((heads_kv, per_group, slot_count), neg_big, jnp.float32)
    running_sum = jnp.zeros((heads_kv, per_group, slot_count), jnp.float32)
    weighted = jnp.zeros((heads_kv, per_group, slot_count, HD), jnp.float32)
    return (running_max, running_sum, weighted)


def key_block(current, grouped, query_pos, key_piece, value_piece, key_start):
    running_max, running_sum, weighted = current
    key_count = key_piece.shape[0]
    heads_kv = grouped.shape[1]
    key_heads = key_piece.reshape(key_count, heads_kv, HD)
    value_heads = value_piece.reshape(key_count, heads_kv, HD)
    scores = jnp.einsum("rkgd,nkd->kgrn", grouped, key_heads, preferred_element_type=jnp.float32)
    scores = scores * (1.0 / math.sqrt(HD))
    key_pos = key_start + jnp.arange(key_count, dtype=jnp.int32)
    allowed = key_pos[None, :] <= query_pos[:, None]
    scores = jnp.where(allowed, scores, neg_big)
    new_max = jnp.maximum(running_max, jnp.max(scores, axis=-1))
    weights = jnp.where(allowed, jnp.exp(scores - new_max[..., None]), 0.0).astype(jnp.bfloat16)
    rescale = jnp.exp(running_max - new_max)
    running_sum = running_sum * rescale + jnp.sum(weights, axis=-1, dtype=jnp.float32)
    weighted = weighted * rescale[..., None] + jnp.einsum(
        "kgrn,nkd->kgrd", weights, value_heads, preferred_element_type=jnp.float32
    )
    return (new_max, running_sum, weighted)


def folder(grouped, query_pos, current, pieces):
    last_pos = jnp.max(query_pos)
    key_part, value_part = pieces
    key_count = key_part.shape[0]
    block_rows = math.gcd(512, key_count)
    block_count = key_count // block_rows
    key_blocks = key_part.reshape(block_count, block_rows, key_part.shape[1])
    value_blocks = value_part.reshape(block_count, block_rows, value_part.shape[1])

    def visit(carried, block_item):
        block_index, key_piece, value_piece = block_item
        key_start = block_index * block_rows
        updated = lax.cond(
            key_start <= last_pos,
            lambda inner: key_block(inner, grouped, query_pos, key_piece, value_piece, key_start),
            lambda inner: inner,
            carried,
        )
        return (updated, None)

    current, _ = lax.scan(
        visit, current, (jnp.arange(block_count, dtype=jnp.int32), key_blocks, value_blocks)
    )
    return current


def finish(current, slot_count):
    running_max, running_sum, weighted = current
    denominator = jnp.where(running_sum > 0.0, running_sum, 1.0)
    averaged = weighted / denominator[..., None]
    return jnp.transpose(averaged, (2, 0, 1, 3)).reshape(slot_count, -1).astype(jnp.bfloat16)


def many_instances(queries, keys, values, query_owner, cache_owner):
    instances = lax.axis_size("seq")
    own_index = lax.axis_index("seq")
    local_rows = queries.shape[0]
    capacity = 3 * local_rows // (2 * instances)
    slot_count = instances * capacity
    heads_kv = keys.shape[1] // HD
    per_group = queries.shape[1] // keys.shape[1]
    positions = own_index * local_rows + jnp.arange(local_rows, dtype=jnp.int32)
    cache_pick = slot_select(cache_owner, instances, capacity)
    key_slots = pack_rows(cache_pick, keys, instances)
    value_slots = pack_rows(cache_pick, values, instances)
    query_pick = slot_select(query_owner, instances, capacity)
    query_slots = pack_rows(query_pick, queries, instances)
    slot_pos = jnp.max(jnp.where(query_pick, positions[None, :], -1), axis=1).reshape(
        instances, capacity
    )
    query_got, pos_got, key_got, value_got = (
        lax.all_to_all(query_slots, "seq", split_axis=0, concat_axis=0, tiled=True),
        lax.all_to_all(slot_pos, "seq", split_axis=0, concat_axis=0, tiled=True),
        lax.all_to_all(key_slots, "seq", split_axis=0, concat_axis=0, tiled=True),
        lax.all_to_all(value_slots, "seq", split_axis=0, concat_axis=0, tiled=True),
    )
    arrived = query_got.reshape(slot_count, -1)
    arrived_pos = pos_got.reshape(slot_count)
    grouped = arrived.reshape(slot_count, heads_kv, per_group, HD)
    final_state = folder(
        grouped,
        arrived_pos,
        start_state(heads_kv, per_group, slot_count),
        (
            lax.all_gather(keys, "seq", axis=0, tiled=True),
            lax.all_gather(values, "seq", axis=0, tiled=True),
        ),
    )
    attended = finish(final_state, slot_count)
    key_cache = key_got.reshape(slot_count, -1)
    value_cache = value_got.reshape(slot_count, -1)
    return (attended, key_cache, value_cache)


def before(rows):
    r = lax.broadcasted_iota(jnp.int32, (rows, rows), 0)
    u = lax.broadcasted_iota(jnp.int32, (rows, rows), 1)
    return (r < u).astype(jnp.bfloat16)


def picks(marks, earlier, capacity):
    rows = marks.shape[1]
    slot = lax.broadcasted_iota(jnp.int32, (capacity, rows), 0).astype(jnp.float32)
    chosen = jnp.where(marks > 0.5, earlier, -1.0)
    return (chosen == slot).astype(jnp.bfloat16)


def pack_kernel(instances, capacity, me_ref, q_hbm, qo_ref, co_ref, *rest):
    sends, (q_ref, arrived) = rest[:instances], rest[instances:]
    rows = q_ref.shape[0]
    heads = q_ref.shape[1] // HD
    fetch = pltpu.make_async_copy(q_hbm, q_ref, arrived)
    fetch.start()
    me = me_ref[0]
    owners = qo_ref[...]
    lane = lax.broadcasted_iota(jnp.int32, (16, rows), 0)
    dest = jnp.bitwise_xor(lane, me)
    marks = (jnp.broadcast_to(owners, (16, rows)) == dest).astype(jnp.bfloat16)
    earlier = jnp.dot(marks, before(rows), preferred_element_type=jnp.float32)
    wide = marks.astype(jnp.float32)
    select = jnp.concatenate(
        [picks(wide[k : k + 1], earlier[k : k + 1], capacity) for k in range(instances)], axis=0
    )
    lists = jnp.concatenate(
        [owners, co_ref[...], jnp.full((14, rows), -1, jnp.int32)], axis=0
    ).astype(jnp.float32).astype(jnp.bfloat16)
    for k in range(instances):
        sends[k][heads * capacity :, :] = lists
    fetch.wait()
    for pair in range(heads // 2):
        packed = jnp.dot(
            select,
            q_ref[:, pair * 2 * HD : (pair + 1) * 2 * HD],
            preferred_element_type=jnp.float32,
        ).astype(jnp.bfloat16)
        for k in range(instances):
            for half in range(2):
                at = (2 * pair + half) * capacity
                sends[k][at : at + capacity, :] = packed[
                    k * capacity : (k + 1) * capacity, half * HD : (half + 1) * HD
                ]


def attend_kernel(instances, capacity, heads, heads_kv, me_ref, *rest):
    got, rest = rest[:instances], rest[instances:]
    got_k, rest = rest[:instances], rest[instances:]
    got_v, rest = rest[:instances], rest[instances:]
    att_ref, kc_ref, vc_ref, wanted_ref, keys, vals = rest
    rows = got_k[0].shape[0]
    per_group = heads // heads_kv
    tail = heads * capacity
    me = me_ref[0]
    for k in range(instances):
        source = jnp.bitwise_xor(me, k)
        wanted_ref[source] = got[k][...]
        at = pl.ds(pl.multiple_of(source * rows, rows), rows)
        for g in range(heads_kv):
            keys[g, at, :] = got_k[k][:, g * HD : (g + 1) * HD]
            vals[g, at, :HD] = got_v[k][:, g * HD : (g + 1) * HD]
        vals[:, k * rows : (k + 1) * rows, HD:] = jnp.ones((heads_kv, rows, HD), jnp.bfloat16)
    lists = jnp.concatenate([wanted_ref[s, tail : tail + 16, :] for s in range(instances)], axis=0)
    wide = (lists.astype(jnp.float32) == me.astype(jnp.float32)).astype(jnp.float32)
    earlier = jnp.dot(wide.astype(jnp.bfloat16), before(rows), preferred_element_type=jnp.float32)
    r = lax.broadcasted_iota(jnp.int32, (rows, 2 * rows), 0)
    u = lax.broadcasted_iota(jnp.int32, (rows, 2 * rows), 1)
    reach = ((u <= r) | (u >= rows)).astype(jnp.bfloat16)
    scale = 1.0 / math.sqrt(HD)
    for s in range(instances):
        q_at, c_at = 16 * s, 16 * s + 1
        cache_pick = picks(wide[c_at : c_at + 1], earlier[c_at : c_at + 1], capacity)
        query_pick = picks(wide[q_at : q_at + 1], earlier[q_at : q_at + 1], capacity)
        slots = slice(s * capacity, (s + 1) * capacity)
        block = slice(s * rows, (s + 1) * rows)
        for g in range(heads_kv):
            columns = slice(g * HD, (g + 1) * HD)
            both = jnp.concatenate([keys[g, block, :], vals[g, block, :HD]], axis=1)
            cached = jnp.dot(cache_pick, both, preferred_element_type=jnp.float32).astype(jnp.bfloat16)
            kc_ref[slots, columns] = cached[:, :HD]
            vc_ref[slots, columns] = cached[:, HD:]
        allowed = jnp.dot(query_pick, reach, preferred_element_type=jnp.float32)
        near = jnp.concatenate([allowed[:, :rows]] * per_group, axis=0) > 0.5
        valid = jnp.concatenate([allowed[:, rows:]] * per_group, axis=0) > 0.5
        for g in range(heads_kv):
            wanted = wanted_ref[s, g * per_group * capacity : (g + 1) * per_group * capacity, :]
            scores = lax.dot_general(
                wanted,
                keys[g, : (s + 1) * rows, :],
                (((1,), (1,)), ((), ())),
                preferred_element_type=jnp.float32,
            )
            last = jnp.where(near, scores[:, s * rows :], neg_big)
            scores = jnp.concatenate([scores[:, : s * rows], last], axis=1) if s else last
            top = jnp.max(scores, axis=1, keepdims=True)
            weights = jnp.exp((scores - top) * scale).astype(jnp.bfloat16)
            mixed = jnp.dot(weights, vals[g, : (s + 1) * rows, :], preferred_element_type=jnp.float32)
            out = jnp.where(valid, mixed[:, :HD] / mixed[:, HD:], 0.0).astype(jnp.bfloat16)
            for h in range(per_group):
                column = (g * per_group + h) * HD
                att_ref[slots, column : column + HD] = out[h * capacity : (h + 1) * capacity, :]


def few_instances(queries, keys, values, query_owner, cache_owner):
    instances = lax.axis_size("seq")
    rows = queries.shape[0]
    capacity = 3 * rows // (2 * instances)
    heads, heads_kv = queries.shape[1] // HD, keys.shape[1] // HD

    def swap(array, k):
        return lax.ppermute(array, "seq", [(i, i ^ k) for i in range(instances)])

    all_k, all_v = {0: keys}, {0: values}
    bit = instances // 2
    while bit:
        for k in list(all_k):
            all_k[k ^ bit] = swap(all_k[k], bit)
            all_v[k ^ bit] = swap(all_v[k], bit)
        bit //= 2
    height = heads * capacity + 16
    vmem = pl.BlockSpec(memory_space=pltpu.VMEM)
    smem = pl.BlockSpec(memory_space=pltpu.SMEM)
    me = lax.axis_index("seq").astype(jnp.int32).reshape(1)
    sends = pl.pallas_call(
        functools.partial(pack_kernel, instances, capacity),
        out_shape=(jax.ShapeDtypeStruct((height, HD), jnp.bfloat16),) * instances,
        in_specs=[smem, pl.BlockSpec(memory_space=pl.ANY), vmem, vmem],
        out_specs=(vmem,) * instances,
        scratch_shapes=[pltpu.VMEM(queries.shape, jnp.bfloat16), pltpu.SemaphoreType.DMA],
        compiler_params=pltpu.CompilerParams(vmem_limit_bytes=16 << 20),
        cost_estimate=pl.CostEstimate(flops=1 << 27, bytes_accessed=2 << 20, transcendentals=0),
        name="pack",
    )(me, queries, query_owner.reshape(1, rows), cache_owner.reshape(1, rows))
    got = [swap(sends[k], k) if k else sends[0] for k in range(instances)]
    slots = instances * capacity
    return pl.pallas_call(
        functools.partial(attend_kernel, instances, capacity, heads, heads_kv),
        out_shape=(
            jax.ShapeDtypeStruct((slots, heads * HD), jnp.bfloat16),
            jax.ShapeDtypeStruct((slots, heads_kv * HD), jnp.bfloat16),
            jax.ShapeDtypeStruct((slots, heads_kv * HD), jnp.bfloat16),
        ),
        in_specs=[smem] + [vmem] * (3 * instances),
        out_specs=(vmem, vmem, vmem),
        scratch_shapes=[
            pltpu.VMEM((instances, height, HD), jnp.bfloat16),
            pltpu.VMEM((heads_kv, instances * rows, HD), jnp.bfloat16),
            pltpu.VMEM((heads_kv, instances * rows, 2 * HD), jnp.bfloat16),
        ],
        compiler_params=pltpu.CompilerParams(vmem_limit_bytes=24 << 20),
        name="attend",
    )(
        me,
        *got,
        *[all_k[k] for k in range(instances)],
        *[all_v[k] for k in range(instances)],
    )


def on_device(queries, keys, values, query_owner, cache_owner):
    instances = lax.axis_size("seq")
    rows = queries.shape[0]
    capacity = 3 * rows // (2 * instances)
    heads = queries.shape[1] // HD
    whole_tiles = capacity % 16 == 0 and rows == HD and heads % 2 == 0 and instances & (instances - 1) == 0
    form = few_instances if whole_tiles else many_instances
    return form(queries, keys, values, query_owner, cache_owner)


def solution(mesh):
    return jax.shard_map(
        on_device,
        mesh=mesh,
        in_specs=(
            P(("groups", "seq"), ("tp", "rep")),
            P(("groups", "seq"), ("tp", "rep")),
            P(("groups", "seq"), ("tp", "rep")),
            P(("groups", "seq"), None),
            P(("groups", "seq"), None),
        ),
        out_specs=(
            P(("groups", "seq"), ("tp", "rep")),
            P(("groups", "seq"), ("tp", "rep")),
            P(("groups", "seq"), ("tp", "rep")),
        ),
        check_vma=False,
    )
```

```python
import functools
import math

import jax
import jax.numpy as jnp
from jax import lax
from jax.experimental import pallas as pl
from jax.experimental.pallas import tpu as pltpu
from jax.sharding import PartitionSpec as P

HD = 128


neg_big = -1e30


def slot_select(owner_list, instances, capacity):
    owners = owner_list[:, 0]
    onehot = (owners[:, None] == jnp.arange(instances, dtype=jnp.int32)[None, :]).astype(jnp.int32)
    earlier = jnp.cumsum(onehot, axis=0) - onehot
    ranking = jnp.sum(earlier * onehot, axis=1)
    target = owners * capacity + ranking
    return target[None, :] == jnp.arange(instances * capacity, dtype=jnp.int32)[:, None]


def pack_rows(select, table_rows, instances):
    selected = jnp.dot(
        select.astype(table_rows.dtype), table_rows, preferred_element_type=jnp.float32
    )
    return selected.astype(table_rows.dtype).reshape(instances, -1, table_rows.shape[1])


def start_state(heads_kv, per_group, slot_count):
    running_max = jnp.full((heads_kv, per_group, slot_count), neg_big, jnp.float32)
    running_sum = jnp.zeros((heads_kv, per_group, slot_count), jnp.float32)
    weighted = jnp.zeros((heads_kv, per_group, slot_count, HD), jnp.float32)
    return (running_max, running_sum, weighted)


def key_block(current, grouped, query_pos, key_piece, value_piece, key_start):
    running_max, running_sum, weighted = current
    key_count = key_piece.shape[0]
    heads_kv = grouped.shape[1]
    key_heads = key_piece.reshape(key_count, heads_kv, HD)
    value_heads = value_piece.reshape(key_count, heads_kv, HD)
    scores = jnp.einsum("rkgd,nkd->kgrn", grouped, key_heads, preferred_element_type=jnp.float32)
    scores = scores * (1.0 / math.sqrt(HD))
    key_pos = key_start + jnp.arange(key_count, dtype=jnp.int32)
    allowed = key_pos[None, :] <= query_pos[:, None]
    scores = jnp.where(allowed, scores, neg_big)
    new_max = jnp.maximum(running_max, jnp.max(scores, axis=-1))
    weights = jnp.where(allowed, jnp.exp(scores - new_max[..., None]), 0.0).astype(jnp.bfloat16)
    rescale = jnp.exp(running_max - new_max)
    running_sum = running_sum * rescale + jnp.sum(weights, axis=-1, dtype=jnp.float32)
    weighted = weighted * rescale[..., None] + jnp.einsum(
        "kgrn,nkd->kgrd", weights, value_heads, preferred_element_type=jnp.float32
    )
    return (new_max, running_sum, weighted)


def folder(grouped, query_pos, current, pieces):
    last_pos = jnp.max(query_pos)
    key_part, value_part = pieces
    key_count = key_part.shape[0]
    block_rows = math.gcd(512, key_count)
    block_count = key_count // block_rows
    key_blocks = key_part.reshape(block_count, block_rows, key_part.shape[1])
    value_blocks = value_part.reshape(block_count, block_rows, value_part.shape[1])

    def visit(carried, block_item):
        block_index, key_piece, value_piece = block_item
        key_start = block_index * block_rows
        updated = lax.cond(
            key_start <= last_pos,
            lambda inner: key_block(inner, grouped, query_pos, key_piece, value_piece, key_start),
            lambda inner: inner,
            carried,
        )
        return (updated, None)

    current, _ = lax.scan(
        visit, current, (jnp.arange(block_count, dtype=jnp.int32), key_blocks, value_blocks)
    )
    return current


def finish(current, slot_count):
    running_max, running_sum, weighted = current
    denominator = jnp.where(running_sum > 0.0, running_sum, 1.0)
    averaged = weighted / denominator[..., None]
    return jnp.transpose(averaged, (2, 0, 1, 3)).reshape(slot_count, -1).astype(jnp.bfloat16)


def many_instances(queries, keys, values, query_owner, cache_owner):
    instances = lax.axis_size("seq")
    own_index = lax.axis_index("seq")
    local_rows = queries.shape[0]
    capacity = 3 * local_rows // (2 * instances)
    slot_count = instances * capacity
    heads_kv = keys.shape[1] // HD
    per_group = queries.shape[1] // keys.shape[1]
    positions = own_index * local_rows + jnp.arange(local_rows, dtype=jnp.int32)
    cache_pick = slot_select(cache_owner, instances, capacity)
    key_slots = pack_rows(cache_pick, keys, instances)
    value_slots = pack_rows(cache_pick, values, instances)
    query_pick = slot_select(query_owner, instances, capacity)
    query_slots = pack_rows(query_pick, queries, instances)
    slot_pos = jnp.max(jnp.where(query_pick, positions[None, :], -1), axis=1).reshape(
        instances, capacity
    )
    query_got, pos_got, key_got, value_got = (
        lax.all_to_all(query_slots, "seq", split_axis=0, concat_axis=0, tiled=True),
        lax.all_to_all(slot_pos, "seq", split_axis=0, concat_axis=0, tiled=True),
        lax.all_to_all(key_slots, "seq", split_axis=0, concat_axis=0, tiled=True),
        lax.all_to_all(value_slots, "seq", split_axis=0, concat_axis=0, tiled=True),
    )
    arrived = query_got.reshape(slot_count, -1)
    arrived_pos = pos_got.reshape(slot_count)
    grouped = arrived.reshape(slot_count, heads_kv, per_group, HD)
    final_state = folder(
        grouped,
        arrived_pos,
        start_state(heads_kv, per_group, slot_count),
        (
            lax.all_gather(keys, "seq", axis=0, tiled=True),
            lax.all_gather(values, "seq", axis=0, tiled=True),
        ),
    )
    attended = finish(final_state, slot_count)
    key_cache = key_got.reshape(slot_count, -1)
    value_cache = value_got.reshape(slot_count, -1)
    return (attended, key_cache, value_cache)


def before(rows):
    r = lax.broadcasted_iota(jnp.int32, (rows, rows), 0)
    u = lax.broadcasted_iota(jnp.int32, (rows, rows), 1)
    return (r < u).astype(jnp.bfloat16)


def picks(marks, earlier, capacity):
    rows = marks.shape[1]
    slot = lax.broadcasted_iota(jnp.int32, (capacity, rows), 0).astype(jnp.float32)
    chosen = jnp.where(marks > 0.5, earlier, -1.0)
    return (chosen == slot).astype(jnp.bfloat16)


def pack_kernel(
    instances, capacity, me_ref, q_hbm, k_hbm, v_hbm, qo_ref, co_ref, kv_out, *rest
):
    sends, rest = rest[:instances], rest[instances:]
    q_ref, k_ref, v_ref, arrived = rest
    rows = q_ref.shape[0]
    heads = q_ref.shape[1] // HD
    heads_kv = k_ref.shape[1] // HD
    fetches = [
        pltpu.make_async_copy(k_hbm, k_ref, arrived.at[0]),
        pltpu.make_async_copy(v_hbm, v_ref, arrived.at[1]),
        pltpu.make_async_copy(q_hbm, q_ref, arrived.at[2]),
    ]
    for fetch in fetches:
        fetch.start()
    me = me_ref[0]
    owners = qo_ref[...]
    lane = lax.broadcasted_iota(jnp.int32, (16, rows), 0)
    dest = jnp.bitwise_xor(lane, me)
    marks = (jnp.broadcast_to(owners, (16, rows)) == dest).astype(jnp.bfloat16)
    earlier = jnp.dot(marks, before(rows), preferred_element_type=jnp.float32)
    wide = marks.astype(jnp.float32)
    select = jnp.concatenate(
        [picks(wide[k : k + 1], earlier[k : k + 1], capacity) for k in range(instances)], axis=0
    )
    query_list = jnp.broadcast_to(owners, (16, rows)).astype(jnp.float32).astype(jnp.bfloat16)
    cache_list = jnp.broadcast_to(co_ref[...], (16, rows)).astype(jnp.float32).astype(jnp.bfloat16)
    top = heads * capacity
    for k in range(instances):
        sends[k][top : top + 16, :] = query_list
    blocks = [(kv_out, 0)] + [(sends[1], top + 16)] * (instances > 1)
    for ref, at in blocks:
        ref[at : at + 16, :] = cache_list
    for index, source in ((0, k_ref), (1, v_ref)):
        fetches[index].wait()
        for g in range(heads_kv):
            piece = source[:, g * HD : (g + 1) * HD]
            for ref, at in blocks:
                at = at + 16 + (index * heads_kv + g) * rows
                ref[at : at + rows, :] = piece
    fetches[2].wait()
    for pair in range(heads // 2):
        packed = jnp.dot(
            select,
            q_ref[:, pair * 2 * HD : (pair + 1) * 2 * HD],
            preferred_element_type=jnp.float32,
        ).astype(jnp.bfloat16)
        for k in range(instances):
            for half in range(2):
                at = (2 * pair + half) * capacity
                sends[k][at : at + capacity, :] = packed[
                    k * capacity : (k + 1) * capacity, half * HD : (half + 1) * HD
                ]


def attend_kernel(instances, capacity, heads, heads_kv, kv_at, me_ref, *rest):
    got, rest = rest[:instances], rest[instances:]
    got_kv, rest = rest[:instances], rest[instances:]
    att_ref, kc_ref, vc_ref, wanted_ref, lists_ref, keys, vals = rest
    rows = HD
    per_group = heads // heads_kv
    tail = heads * capacity
    me = me_ref[0]
    for k in range(instances):
        source = jnp.bitwise_xor(me, k)
        wanted_ref[source] = got[k][: tail + 16, :]
        at = pl.ds(pl.multiple_of(source * rows, rows), rows)
        start = kv_at[k]
        lists_ref[source] = got_kv[k][start : start + 16, :]
        start = start + 16
        for g in range(heads_kv):
            keys[g, at, :] = got_kv[k][start + g * rows : start + (g + 1) * rows, :]
            there = start + (heads_kv + g) * rows
            vals[g, at, :HD] = got_kv[k][there : there + rows, :]
        vals[:, k * rows : (k + 1) * rows, HD:] = jnp.ones((heads_kv, rows, HD), jnp.bfloat16)
    lists = jnp.concatenate(
        [wanted_ref[s, tail : tail + 16, :] for s in range(instances)]
        + [lists_ref[s] for s in range(instances)],
        axis=0,
    )
    wide = (lists.astype(jnp.float32) == me.astype(jnp.float32)).astype(jnp.float32)
    earlier = jnp.dot(wide.astype(jnp.bfloat16), before(rows), preferred_element_type=jnp.float32)
    r = lax.broadcasted_iota(jnp.int32, (rows, 2 * rows), 0)
    u = lax.broadcasted_iota(jnp.int32, (rows, 2 * rows), 1)
    reach = ((u <= r) | (u >= rows)).astype(jnp.bfloat16)
    scale = 1.0 / math.sqrt(HD)
    for s in range(instances):
        q_at, c_at = 16 * s, 16 * (instances + s)
        cache_pick = picks(wide[c_at : c_at + 1], earlier[c_at : c_at + 1], capacity)
        query_pick = picks(wide[q_at : q_at + 1], earlier[q_at : q_at + 1], capacity)
        slots = slice(s * capacity, (s + 1) * capacity)
        block = slice(s * rows, (s + 1) * rows)
        for g in range(heads_kv):
            columns = slice(g * HD, (g + 1) * HD)
            both = jnp.concatenate([keys[g, block, :], vals[g, block, :HD]], axis=1)
            cached = jnp.dot(cache_pick, both, preferred_element_type=jnp.float32).astype(jnp.bfloat16)
            kc_ref[slots, columns] = cached[:, :HD]
            vc_ref[slots, columns] = cached[:, HD:]
        allowed = jnp.dot(query_pick, reach, preferred_element_type=jnp.float32)
        near = jnp.concatenate([allowed[:, :rows]] * per_group, axis=0) > 0.5
        valid = jnp.concatenate([allowed[:, rows:]] * per_group, axis=0) > 0.5
        for g in range(heads_kv):
            wanted = wanted_ref[s, g * per_group * capacity : (g + 1) * per_group * capacity, :]
            scores = lax.dot_general(
                wanted,
                keys[g, : (s + 1) * rows, :],
                (((1,), (1,)), ((), ())),
                preferred_element_type=jnp.float32,
            )
            last = jnp.where(near, scores[:, s * rows :], neg_big)
            scores = jnp.concatenate([scores[:, : s * rows], last], axis=1) if s else last
            top = jnp.max(scores, axis=1, keepdims=True)
            weights = jnp.exp((scores - top) * scale).astype(jnp.bfloat16)
            mixed = jnp.dot(weights, vals[g, : (s + 1) * rows, :], preferred_element_type=jnp.float32)
            out = jnp.where(valid, mixed[:, :HD] / mixed[:, HD:], 0.0).astype(jnp.bfloat16)
            for h in range(per_group):
                column = (g * per_group + h) * HD
                att_ref[slots, column : column + HD] = out[h * capacity : (h + 1) * capacity, :]


def few_instances(queries, keys, values, query_owner, cache_owner):
    instances = lax.axis_size("seq")
    rows = queries.shape[0]
    capacity = 3 * rows // (2 * instances)
    heads, heads_kv = queries.shape[1] // HD, keys.shape[1] // HD

    def swap(array, k):
        return lax.ppermute(array, "seq", [(i, i ^ k) for i in range(instances)])

    tall = heads * capacity + 16
    kv_tall = 2 * heads_kv * rows + 16
    vmem = pl.BlockSpec(memory_space=pltpu.VMEM)
    smem = pl.BlockSpec(memory_space=pltpu.SMEM)
    hbm = pl.BlockSpec(memory_space=pltpu.HBM)
    me = lax.axis_index("seq").astype(jnp.int32).reshape(1)
    heights = [kv_tall] + [tall + kv_tall * (k == 1) for k in range(instances)]
    own_kv, *sends = pl.pallas_call(
        functools.partial(pack_kernel, instances, capacity),
        out_shape=tuple(jax.ShapeDtypeStruct((h, HD), jnp.bfloat16) for h in heights),
        in_specs=[smem, hbm, hbm, hbm, vmem, vmem],
        out_specs=(vmem,) * (instances + 1),
        scratch_shapes=[
            pltpu.VMEM(queries.shape, jnp.bfloat16),
            pltpu.VMEM(keys.shape, jnp.bfloat16),
            pltpu.VMEM(values.shape, jnp.bfloat16),
            pltpu.SemaphoreType.DMA((3,)),
        ],
        compiler_params=pltpu.CompilerParams(vmem_limit_bytes=16 << 20),
        cost_estimate=pl.CostEstimate(flops=1 << 27, bytes_accessed=2 << 20, transcendentals=0),
        name="pack",
    )(me, queries, keys, values, query_owner.reshape(1, rows), cache_owner.reshape(1, rows))
    far_kv = swap(own_kv, 2)
    far_kv_beside = swap(far_kv, 1)
    got = [sends[0], swap(sends[1], 1), swap(sends[2], 2), swap(sends[3], 3)]
    got_kv, kv_at = (own_kv, got[1], far_kv, far_kv_beside), (0, tall, 0, 0)
    slots = instances * capacity
    return pl.pallas_call(
        functools.partial(attend_kernel, instances, capacity, heads, heads_kv, kv_at),
        out_shape=(
            jax.ShapeDtypeStruct((slots, heads * HD), jnp.bfloat16),
            jax.ShapeDtypeStruct((slots, heads_kv * HD), jnp.bfloat16),
            jax.ShapeDtypeStruct((slots, heads_kv * HD), jnp.bfloat16),
        ),
        in_specs=[smem] + [vmem] * (2 * instances),
        out_specs=(vmem, vmem, vmem),
        scratch_shapes=[
            pltpu.VMEM((instances, tall, HD), jnp.bfloat16),
            pltpu.VMEM((instances, 16, HD), jnp.bfloat16),
            pltpu.VMEM((heads_kv, instances * rows, HD), jnp.bfloat16),
            pltpu.VMEM((heads_kv, instances * rows, 2 * HD), jnp.bfloat16),
        ],
        compiler_params=pltpu.CompilerParams(vmem_limit_bytes=24 << 20),
        name="attend",
    )(me, *got, *got_kv)


def on_device(queries, keys, values, query_owner, cache_owner):
    instances = lax.axis_size("seq")
    rows = queries.shape[0]
    capacity = 3 * rows // (2 * instances)
    heads = queries.shape[1] // HD
    whole_tiles = instances == 4 and capacity % 16 == 0 and rows == HD and heads % 2 == 0
    form = few_instances if whole_tiles else many_instances
    return form(queries, keys, values, query_owner, cache_owner)


def solution(mesh):
    return jax.shard_map(
        on_device,
        mesh=mesh,
        in_specs=(
            P(("groups", "seq"), ("tp", "rep")),
            P(("groups", "seq"), ("tp", "rep")),
            P(("groups", "seq"), ("tp", "rep")),
            P(("groups", "seq"), None),
            P(("groups", "seq"), None),
        ),
        out_specs=(
            P(("groups", "seq"), ("tp", "rep")),
            P(("groups", "seq"), ("tp", "rep")),
            P(("groups", "seq"), ("tp", "rep")),
        ),
        check_vma=False,
    )
```

```python
import functools
import math

import jax
import jax.numpy as jnp
from jax import lax
from jax.experimental import pallas as pl
from jax.experimental.pallas import tpu as pltpu
from jax.sharding import PartitionSpec as P

HD = 128


neg_big = -1e30


def slot_select(owner_list, instances, capacity):
    owners = owner_list[:, 0]
    onehot = (owners[:, None] == jnp.arange(instances, dtype=jnp.int32)[None, :]).astype(jnp.int32)
    earlier = jnp.cumsum(onehot, axis=0) - onehot
    ranking = jnp.sum(earlier * onehot, axis=1)
    target = owners * capacity + ranking
    return target[None, :] == jnp.arange(instances * capacity, dtype=jnp.int32)[:, None]


def pack_rows(select, table_rows, instances):
    selected = jnp.dot(
        select.astype(table_rows.dtype), table_rows, preferred_element_type=jnp.float32
    )
    return selected.astype(table_rows.dtype).reshape(instances, -1, table_rows.shape[1])


def start_state(heads_kv, per_group, slot_count):
    running_max = jnp.full((heads_kv, per_group, slot_count), neg_big, jnp.float32)
    running_sum = jnp.zeros((heads_kv, per_group, slot_count), jnp.float32)
    weighted = jnp.zeros((heads_kv, per_group, slot_count, HD), jnp.float32)
    return (running_max, running_sum, weighted)


def key_block(current, grouped, query_pos, key_piece, value_piece, key_start):
    running_max, running_sum, weighted = current
    key_count = key_piece.shape[0]
    heads_kv = grouped.shape[1]
    key_heads = key_piece.reshape(key_count, heads_kv, HD)
    value_heads = value_piece.reshape(key_count, heads_kv, HD)
    scores = jnp.einsum("rkgd,nkd->kgrn", grouped, key_heads, preferred_element_type=jnp.float32)
    scores = scores * (1.0 / math.sqrt(HD))
    key_pos = key_start + jnp.arange(key_count, dtype=jnp.int32)
    allowed = key_pos[None, :] <= query_pos[:, None]
    scores = jnp.where(allowed, scores, neg_big)
    new_max = jnp.maximum(running_max, jnp.max(scores, axis=-1))
    weights = jnp.where(allowed, jnp.exp(scores - new_max[..., None]), 0.0).astype(jnp.bfloat16)
    rescale = jnp.exp(running_max - new_max)
    running_sum = running_sum * rescale + jnp.sum(weights, axis=-1, dtype=jnp.float32)
    weighted = weighted * rescale[..., None] + jnp.einsum(
        "kgrn,nkd->kgrd", weights, value_heads, preferred_element_type=jnp.float32
    )
    return (new_max, running_sum, weighted)


def folder(grouped, query_pos, current, pieces):
    last_pos = jnp.max(query_pos)
    key_part, value_part = pieces
    key_count = key_part.shape[0]
    block_rows = math.gcd(512, key_count)
    block_count = key_count // block_rows
    key_blocks = key_part.reshape(block_count, block_rows, key_part.shape[1])
    value_blocks = value_part.reshape(block_count, block_rows, value_part.shape[1])

    def visit(carried, block_item):
        block_index, key_piece, value_piece = block_item
        key_start = block_index * block_rows
        updated = lax.cond(
            key_start <= last_pos,
            lambda inner: key_block(inner, grouped, query_pos, key_piece, value_piece, key_start),
            lambda inner: inner,
            carried,
        )
        return (updated, None)

    current, _ = lax.scan(
        visit, current, (jnp.arange(block_count, dtype=jnp.int32), key_blocks, value_blocks)
    )
    return current


def finish(current, slot_count):
    running_max, running_sum, weighted = current
    denominator = jnp.where(running_sum > 0.0, running_sum, 1.0)
    averaged = weighted / denominator[..., None]
    return jnp.transpose(averaged, (2, 0, 1, 3)).reshape(slot_count, -1).astype(jnp.bfloat16)


def many_instances(queries, keys, values, query_owner, cache_owner):
    instances = lax.axis_size("seq")
    own_index = lax.axis_index("seq")
    local_rows = queries.shape[0]
    capacity = 3 * local_rows // (2 * instances)
    slot_count = instances * capacity
    heads_kv = keys.shape[1] // HD
    per_group = queries.shape[1] // keys.shape[1]
    positions = own_index * local_rows + jnp.arange(local_rows, dtype=jnp.int32)
    cache_pick = slot_select(cache_owner, instances, capacity)
    key_slots = pack_rows(cache_pick, keys, instances)
    value_slots = pack_rows(cache_pick, values, instances)
    query_pick = slot_select(query_owner, instances, capacity)
    query_slots = pack_rows(query_pick, queries, instances)
    slot_pos = jnp.max(jnp.where(query_pick, positions[None, :], -1), axis=1).reshape(
        instances, capacity
    )
    query_got, pos_got, key_got, value_got = (
        lax.all_to_all(query_slots, "seq", split_axis=0, concat_axis=0, tiled=True),
        lax.all_to_all(slot_pos, "seq", split_axis=0, concat_axis=0, tiled=True),
        lax.all_to_all(key_slots, "seq", split_axis=0, concat_axis=0, tiled=True),
        lax.all_to_all(value_slots, "seq", split_axis=0, concat_axis=0, tiled=True),
    )
    arrived = query_got.reshape(slot_count, -1)
    arrived_pos = pos_got.reshape(slot_count)
    grouped = arrived.reshape(slot_count, heads_kv, per_group, HD)
    final_state = folder(
        grouped,
        arrived_pos,
        start_state(heads_kv, per_group, slot_count),
        (
            lax.all_gather(keys, "seq", axis=0, tiled=True),
            lax.all_gather(values, "seq", axis=0, tiled=True),
        ),
    )
    attended = finish(final_state, slot_count)
    key_cache = key_got.reshape(slot_count, -1)
    value_cache = value_got.reshape(slot_count, -1)
    return (attended, key_cache, value_cache)


def before(rows):
    r = lax.broadcasted_iota(jnp.int32, (rows, rows), 0)
    u = lax.broadcasted_iota(jnp.int32, (rows, rows), 1)
    return (r < u).astype(jnp.bfloat16)


def picks(marks, earlier, capacity):
    rows = marks.shape[1]
    slot = lax.broadcasted_iota(jnp.int32, (capacity, rows), 0).astype(jnp.float32)
    chosen = jnp.where(marks > 0.5, earlier, -1.0)
    return (chosen == slot).astype(jnp.bfloat16)


def pack_kernel(instances, capacity, me_ref, q_hbm, qo_ref, co_ref, *rest):
    sends, (q_ref, arrived) = rest[:instances], rest[instances:]
    rows = q_ref.shape[0]
    heads = q_ref.shape[1] // HD
    fetch = pltpu.make_async_copy(q_hbm, q_ref, arrived)
    fetch.start()
    me = me_ref[0]
    owners = qo_ref[...]
    lane = lax.broadcasted_iota(jnp.int32, (16, rows), 0)
    dest = jnp.bitwise_xor(lane, me)
    marks = (jnp.broadcast_to(owners, (16, rows)) == dest).astype(jnp.bfloat16)
    earlier = jnp.dot(marks, before(rows), preferred_element_type=jnp.float32)
    wide = marks.astype(jnp.float32)
    select = jnp.concatenate(
        [picks(wide[k : k + 1], earlier[k : k + 1], capacity) for k in range(instances)], axis=0
    )
    lists = jnp.concatenate(
        [owners, co_ref[...], jnp.full((14, rows), -1, jnp.int32)], axis=0
    ).astype(jnp.float32).astype(jnp.bfloat16)
    for k in range(instances):
        sends[k][heads * capacity :, :] = lists
    fetch.wait()
    for pair in range(heads // 2):
        packed = jnp.dot(
            select,
            q_ref[:, pair * 2 * HD : (pair + 1) * 2 * HD],
            preferred_element_type=jnp.float32,
        ).astype(jnp.bfloat16)
        for k in range(instances):
            for half in range(2):
                at = (2 * pair + half) * capacity
                sends[k][at : at + capacity, :] = packed[
                    k * capacity : (k + 1) * capacity, half * HD : (half + 1) * HD
                ]


def gate_kernel(k_ref, v_ref, *rest):
    kv_ref = rest[-1]
    rows = k_ref.shape[0]
    at = 0
    for source in (k_ref, v_ref):
        for g in range(source.shape[1] // HD):
            kv_ref[at : at + rows, :] = source[:, g * HD : (g + 1) * HD]
            at += rows


def attend_kernel(instances, capacity, heads, heads_kv, me_ref, *rest):
    got, rest = rest[:instances], rest[instances:]
    k_own, v_own, k_near, v_near, k_far, v_far, both = rest[:7]
    att_ref, kc_ref, vc_ref, wanted_ref, keys, vals = rest[7:]
    rows = HD
    per_group = heads // heads_kv
    tail = heads * capacity
    me = me_ref[0]
    direct = ((k_own, v_own), (k_near, v_near), (k_far, v_far))
    for k in range(instances):
        source = jnp.bitwise_xor(me, k)
        wanted_ref[source] = got[k][...]
        at = pl.ds(pl.multiple_of(source * rows, rows), rows)
        for g in range(heads_kv):
            if k < len(direct):
                keys[g, at, :] = direct[k][0][:, g * HD : (g + 1) * HD]
                vals[g, at, :HD] = direct[k][1][:, g * HD : (g + 1) * HD]
            else:
                keys[g, at, :] = both[g * rows : (g + 1) * rows, :]
                vals[g, at, :HD] = both[(heads_kv + g) * rows : (heads_kv + g + 1) * rows, :]
        vals[:, k * rows : (k + 1) * rows, HD:] = jnp.ones((heads_kv, rows, HD), jnp.bfloat16)
    lists = jnp.concatenate([wanted_ref[s, tail : tail + 16, :] for s in range(instances)], axis=0)
    wide = (lists.astype(jnp.float32) == me.astype(jnp.float32)).astype(jnp.float32)
    earlier = jnp.dot(wide.astype(jnp.bfloat16), before(rows), preferred_element_type=jnp.float32)
    r = lax.broadcasted_iota(jnp.int32, (rows, 2 * rows), 0)
    u = lax.broadcasted_iota(jnp.int32, (rows, 2 * rows), 1)
    reach = ((u <= r) | (u >= rows)).astype(jnp.bfloat16)
    scale = 1.0 / math.sqrt(HD)
    for s in range(instances):
        q_at, c_at = 16 * s, 16 * s + 1
        cache_pick = picks(wide[c_at : c_at + 1], earlier[c_at : c_at + 1], capacity)
        query_pick = picks(wide[q_at : q_at + 1], earlier[q_at : q_at + 1], capacity)
        slots = slice(s * capacity, (s + 1) * capacity)
        block = slice(s * rows, (s + 1) * rows)
        for g in range(heads_kv):
            columns = slice(g * HD, (g + 1) * HD)
            both = jnp.concatenate([keys[g, block, :], vals[g, block, :HD]], axis=1)
            cached = jnp.dot(cache_pick, both, preferred_element_type=jnp.float32).astype(jnp.bfloat16)
            kc_ref[slots, columns] = cached[:, :HD]
            vc_ref[slots, columns] = cached[:, HD:]
        allowed = jnp.dot(query_pick, reach, preferred_element_type=jnp.float32)
        near = jnp.concatenate([allowed[:, :rows]] * per_group, axis=0) > 0.5
        valid = jnp.concatenate([allowed[:, rows:]] * per_group, axis=0) > 0.5
        for g in range(heads_kv):
            wanted = wanted_ref[s, g * per_group * capacity : (g + 1) * per_group * capacity, :]
            scores = lax.dot_general(
                wanted,
                keys[g, : (s + 1) * rows, :],
                (((1,), (1,)), ((), ())),
                preferred_element_type=jnp.float32,
            )
            last = jnp.where(near, scores[:, s * rows :], neg_big)
            scores = jnp.concatenate([scores[:, : s * rows], last], axis=1) if s else last
            top = jnp.max(scores, axis=1, keepdims=True)
            weights = jnp.exp((scores - top) * scale).astype(jnp.bfloat16)
            mixed = jnp.dot(weights, vals[g, : (s + 1) * rows, :], preferred_element_type=jnp.float32)
            out = jnp.where(valid, mixed[:, :HD] / mixed[:, HD:], 0.0).astype(jnp.bfloat16)
            for h in range(per_group):
                column = (g * per_group + h) * HD
                att_ref[slots, column : column + HD] = out[h * capacity : (h + 1) * capacity, :]


def few_instances(queries, keys, values, query_owner, cache_owner):
    instances = lax.axis_size("seq")
    rows = queries.shape[0]
    capacity = 3 * rows // (2 * instances)
    heads, heads_kv = queries.shape[1] // HD, keys.shape[1] // HD

    def swap(array, k):
        return lax.ppermute(array, "seq", [(i, i ^ k) for i in range(instances)])

    tall = heads * capacity + 16
    vmem = pl.BlockSpec(memory_space=pltpu.VMEM)
    smem = pl.BlockSpec(memory_space=pltpu.SMEM)
    hbm = pl.BlockSpec(memory_space=pltpu.HBM)
    me = lax.axis_index("seq").astype(jnp.int32).reshape(1)
    k_far, v_far = swap(keys, 2), swap(values, 2)
    k_near, v_near = swap(keys, 1), swap(values, 1)
    kv_tall = 2 * heads_kv * rows
    sends = pl.pallas_call(
        functools.partial(pack_kernel, instances, capacity),
        out_shape=(jax.ShapeDtypeStruct((tall, HD), jnp.bfloat16),) * instances,
        in_specs=[smem, hbm, vmem, vmem],
        out_specs=(vmem,) * instances,
        scratch_shapes=[pltpu.VMEM(queries.shape, jnp.bfloat16), pltpu.SemaphoreType.DMA],
        compiler_params=pltpu.CompilerParams(vmem_limit_bytes=16 << 20),
        cost_estimate=pl.CostEstimate(flops=1 << 27, bytes_accessed=2 << 20, transcendentals=0),
        name="pack",
    )(me, queries, query_owner.reshape(1, rows), cache_owner.reshape(1, rows))
    anyspace = pl.BlockSpec(memory_space=pl.ANY)
    through = [*sends[1:], k_near, v_near]
    *through, kv_far = pl.pallas_call(
        gate_kernel,
        out_shape=tuple(jax.ShapeDtypeStruct(x.shape, x.dtype) for x in through)
        + (jax.ShapeDtypeStruct((kv_tall, HD), jnp.bfloat16),),
        in_specs=[vmem, vmem] + [anyspace] * len(through),
        out_specs=(anyspace,) * len(through) + (vmem,),
        input_output_aliases={2 + i: i for i in range(len(through))},
        compiler_params=pltpu.CompilerParams(vmem_limit_bytes=16 << 20),
        cost_estimate=pl.CostEstimate(flops=0, bytes_accessed=1 << 18, transcendentals=0),
        name="gate",
    )(k_far, v_far, *through)
    k_near, v_near = through[-2:]
    sends = [sends[0], *through[:-2]]
    got = {0: sends[0]}
    for k in (2, 3, 1):
        got[k] = swap(sends[k], k)
    both = swap(kv_far, 1)
    slots = instances * capacity
    return pl.pallas_call(
        functools.partial(attend_kernel, instances, capacity, heads, heads_kv),
        out_shape=(
            jax.ShapeDtypeStruct((slots, heads * HD), jnp.bfloat16),
            jax.ShapeDtypeStruct((slots, heads_kv * HD), jnp.bfloat16),
            jax.ShapeDtypeStruct((slots, heads_kv * HD), jnp.bfloat16),
        ),
        in_specs=[smem] + [vmem] * (instances + 7),
        out_specs=(vmem, vmem, vmem),
        scratch_shapes=[
            pltpu.VMEM((instances, tall, HD), jnp.bfloat16),
            pltpu.VMEM((heads_kv, instances * rows, HD), jnp.bfloat16),
            pltpu.VMEM((heads_kv, instances * rows, 2 * HD), jnp.bfloat16),
        ],
        compiler_params=pltpu.CompilerParams(vmem_limit_bytes=24 << 20),
        name="attend",
    )(me, *[got[k] for k in range(instances)], keys, values, k_near, v_near, k_far, v_far, both)


def on_device(queries, keys, values, query_owner, cache_owner):
    instances = lax.axis_size("seq")
    rows = queries.shape[0]
    capacity = 3 * rows // (2 * instances)
    heads = queries.shape[1] // HD
    whole_tiles = instances == 4 and capacity % 16 == 0 and rows == HD and heads % 2 == 0
    form = few_instances if whole_tiles else many_instances
    return form(queries, keys, values, query_owner, cache_owner)


def solution(mesh):
    return jax.shard_map(
        on_device,
        mesh=mesh,
        in_specs=(
            P(("groups", "seq"), ("tp", "rep")),
            P(("groups", "seq"), ("tp", "rep")),
            P(("groups", "seq"), ("tp", "rep")),
            P(("groups", "seq"), None),
            P(("groups", "seq"), None),
        ),
        out_specs=(
            P(("groups", "seq"), ("tp", "rep")),
            P(("groups", "seq"), ("tp", "rep")),
            P(("groups", "seq"), ("tp", "rep")),
        ),
        check_vma=False,
    )
```

```python
import functools
import math

import jax
import jax.numpy as jnp
from jax import lax
from jax.experimental import pallas as pl
from jax.experimental.pallas import tpu as pltpu
from jax.sharding import PartitionSpec as P

HD = 128


neg_big = -1e30


def slot_select(owner_list, instances, capacity):
    owners = owner_list[:, 0]
    onehot = (owners[:, None] == jnp.arange(instances, dtype=jnp.int32)[None, :]).astype(jnp.int32)
    earlier = jnp.cumsum(onehot, axis=0) - onehot
    ranking = jnp.sum(earlier * onehot, axis=1)
    target = owners * capacity + ranking
    return target[None, :] == jnp.arange(instances * capacity, dtype=jnp.int32)[:, None]


def pack_rows(select, table_rows, instances):
    selected = jnp.dot(
        select.astype(table_rows.dtype), table_rows, preferred_element_type=jnp.float32
    )
    return selected.astype(table_rows.dtype).reshape(instances, -1, table_rows.shape[1])


def start_state(heads_kv, per_group, slot_count):
    running_max = jnp.full((heads_kv, per_group, slot_count), neg_big, jnp.float32)
    running_sum = jnp.zeros((heads_kv, per_group, slot_count), jnp.float32)
    weighted = jnp.zeros((heads_kv, per_group, slot_count, HD), jnp.float32)
    return (running_max, running_sum, weighted)


def key_block(current, grouped, query_pos, key_piece, value_piece, key_start):
    running_max, running_sum, weighted = current
    key_count = key_piece.shape[0]
    heads_kv = grouped.shape[1]
    key_heads = key_piece.reshape(key_count, heads_kv, HD)
    value_heads = value_piece.reshape(key_count, heads_kv, HD)
    scores = jnp.einsum("rkgd,nkd->kgrn", grouped, key_heads, preferred_element_type=jnp.float32)
    scores = scores * (1.0 / math.sqrt(HD))
    key_pos = key_start + jnp.arange(key_count, dtype=jnp.int32)
    allowed = key_pos[None, :] <= query_pos[:, None]
    scores = jnp.where(allowed, scores, neg_big)
    new_max = jnp.maximum(running_max, jnp.max(scores, axis=-1))
    weights = jnp.where(allowed, jnp.exp(scores - new_max[..., None]), 0.0).astype(jnp.bfloat16)
    rescale = jnp.exp(running_max - new_max)
    running_sum = running_sum * rescale + jnp.sum(weights, axis=-1, dtype=jnp.float32)
    weighted = weighted * rescale[..., None] + jnp.einsum(
        "kgrn,nkd->kgrd", weights, value_heads, preferred_element_type=jnp.float32
    )
    return (new_max, running_sum, weighted)


def folder(grouped, query_pos, current, pieces):
    last_pos = jnp.max(query_pos)
    key_part, value_part = pieces
    key_count = key_part.shape[0]
    block_rows = math.gcd(512, key_count)
    block_count = key_count // block_rows
    key_blocks = key_part.reshape(block_count, block_rows, key_part.shape[1])
    value_blocks = value_part.reshape(block_count, block_rows, value_part.shape[1])

    def visit(carried, block_item):
        block_index, key_piece, value_piece = block_item
        key_start = block_index * block_rows
        updated = lax.cond(
            key_start <= last_pos,
            lambda inner: key_block(inner, grouped, query_pos, key_piece, value_piece, key_start),
            lambda inner: inner,
            carried,
        )
        return (updated, None)

    current, _ = lax.scan(
        visit, current, (jnp.arange(block_count, dtype=jnp.int32), key_blocks, value_blocks)
    )
    return current


def finish(current, slot_count):
    running_max, running_sum, weighted = current
    denominator = jnp.where(running_sum > 0.0, running_sum, 1.0)
    averaged = weighted / denominator[..., None]
    return jnp.transpose(averaged, (2, 0, 1, 3)).reshape(slot_count, -1).astype(jnp.bfloat16)


def many_instances(queries, keys, values, query_owner, cache_owner):
    instances = lax.axis_size("seq")
    own_index = lax.axis_index("seq")
    local_rows = queries.shape[0]
    capacity = 3 * local_rows // (2 * instances)
    slot_count = instances * capacity
    heads_kv = keys.shape[1] // HD
    per_group = queries.shape[1] // keys.shape[1]
    positions = own_index * local_rows + jnp.arange(local_rows, dtype=jnp.int32)
    cache_pick = slot_select(cache_owner, instances, capacity)
    key_slots = pack_rows(cache_pick, keys, instances)
    value_slots = pack_rows(cache_pick, values, instances)
    query_pick = slot_select(query_owner, instances, capacity)
    query_slots = pack_rows(query_pick, queries, instances)
    slot_pos = jnp.max(jnp.where(query_pick, positions[None, :], -1), axis=1).reshape(
        instances, capacity
    )
    query_got, pos_got, key_got, value_got = (
        lax.all_to_all(query_slots, "seq", split_axis=0, concat_axis=0, tiled=True),
        lax.all_to_all(slot_pos, "seq", split_axis=0, concat_axis=0, tiled=True),
        lax.all_to_all(key_slots, "seq", split_axis=0, concat_axis=0, tiled=True),
        lax.all_to_all(value_slots, "seq", split_axis=0, concat_axis=0, tiled=True),
    )
    arrived = query_got.reshape(slot_count, -1)
    arrived_pos = pos_got.reshape(slot_count)
    grouped = arrived.reshape(slot_count, heads_kv, per_group, HD)
    final_state = folder(
        grouped,
        arrived_pos,
        start_state(heads_kv, per_group, slot_count),
        (
            lax.all_gather(keys, "seq", axis=0, tiled=True),
            lax.all_gather(values, "seq", axis=0, tiled=True),
        ),
    )
    attended = finish(final_state, slot_count)
    key_cache = key_got.reshape(slot_count, -1)
    value_cache = value_got.reshape(slot_count, -1)
    return (attended, key_cache, value_cache)


def before(rows):
    r = lax.broadcasted_iota(jnp.int32, (rows, rows), 0)
    u = lax.broadcasted_iota(jnp.int32, (rows, rows), 1)
    return (r < u).astype(jnp.bfloat16)


def picks(marks, earlier, capacity):
    rows = marks.shape[1]
    slot = lax.broadcasted_iota(jnp.int32, (capacity, rows), 0).astype(jnp.float32)
    chosen = jnp.where(marks > 0.5, earlier, -1.0)
    return (chosen == slot).astype(jnp.bfloat16)


def pack_kernel(instances, capacity, me_ref, q_hbm, qo_ref, co_ref, *rest):
    sends, (q_ref, arrived) = rest[:instances], rest[instances:]
    rows = q_ref.shape[0]
    heads = q_ref.shape[1] // HD
    fetch = pltpu.make_async_copy(q_hbm, q_ref, arrived)
    fetch.start()
    me = me_ref[0]
    owners = qo_ref[...]
    lane = lax.broadcasted_iota(jnp.int32, (16, rows), 0)
    dest = jnp.bitwise_xor(lane, me)
    marks = (jnp.broadcast_to(owners, (16, rows)) == dest).astype(jnp.bfloat16)
    earlier = jnp.dot(marks, before(rows), preferred_element_type=jnp.float32)
    wide = marks.astype(jnp.float32)
    select = jnp.concatenate(
        [picks(wide[k : k + 1], earlier[k : k + 1], capacity) for k in range(instances)], axis=0
    )
    lists = jnp.concatenate(
        [owners, co_ref[...], jnp.full((14, rows), -1, jnp.int32)], axis=0
    ).astype(jnp.float32).astype(jnp.bfloat16)
    for k in range(instances):
        sends[k][heads * capacity :, :] = lists
    fetch.wait()
    for pair in range(heads // 2):
        packed = jnp.dot(
            select,
            q_ref[:, pair * 2 * HD : (pair + 1) * 2 * HD],
            preferred_element_type=jnp.float32,
        ).astype(jnp.bfloat16)
        for k in range(instances):
            for half in range(2):
                at = (2 * pair + half) * capacity
                sends[k][at : at + capacity, :] = packed[
                    k * capacity : (k + 1) * capacity, half * HD : (half + 1) * HD
                ]


def gate_kernel(*refs):
    rows = refs[0].shape[0]
    for pair in range(2):
        at = 0
        for source in refs[2 * pair : 2 * pair + 2]:
            for g in range(source.shape[1] // HD):
                refs[len(refs) - 2 + pair][at : at + rows, :] = source[:, g * HD : (g + 1) * HD]
                at += rows


def attend_kernel(instances, capacity, heads, heads_kv, me_ref, *rest):
    got, rest = dict(zip((0, 2, 3, 1), rest)), rest[instances:]
    k_own, v_own, k_far, v_far, beside, both = rest[:6]
    att_ref, kc_ref, vc_ref, wanted_ref, keys, vals = rest[6:]
    rows = HD
    per_group = heads // heads_kv
    tail = heads * capacity
    me = me_ref[0]
    direct, joined = {0: (k_own, v_own), 2: (k_far, v_far)}, {1: beside, 3: both}
    for k in range(instances):
        source = jnp.bitwise_xor(me, k)
        wanted_ref[source] = got[k][...]
        at = pl.ds(pl.multiple_of(source * rows, rows), rows)
        for g in range(heads_kv):
            if k in direct:
                keys[g, at, :] = direct[k][0][:, g * HD : (g + 1) * HD]
                vals[g, at, :HD] = direct[k][1][:, g * HD : (g + 1) * HD]
            else:
                start = heads_kv * rows
                keys[g, at, :] = joined[k][g * rows : (g + 1) * rows, :]
                vals[g, at, :HD] = joined[k][start + g * rows : start + (g + 1) * rows, :]
        vals[:, k * rows : (k + 1) * rows, HD:] = jnp.ones((heads_kv, rows, HD), jnp.bfloat16)
    lists = jnp.concatenate([wanted_ref[s, tail : tail + 16, :] for s in range(instances)], axis=0)
    wide = (lists.astype(jnp.float32) == me.astype(jnp.float32)).astype(jnp.float32)
    earlier = jnp.dot(wide.astype(jnp.bfloat16), before(rows), preferred_element_type=jnp.float32)
    r = lax.broadcasted_iota(jnp.int32, (rows, 2 * rows), 0)
    u = lax.broadcasted_iota(jnp.int32, (rows, 2 * rows), 1)
    reach = ((u <= r) | (u >= rows)).astype(jnp.bfloat16)
    scale = 1.0 / math.sqrt(HD)
    for s in range(instances):
        q_at, c_at = 16 * s, 16 * s + 1
        cache_pick = picks(wide[c_at : c_at + 1], earlier[c_at : c_at + 1], capacity)
        query_pick = picks(wide[q_at : q_at + 1], earlier[q_at : q_at + 1], capacity)
        slots = slice(s * capacity, (s + 1) * capacity)
        block = slice(s * rows, (s + 1) * rows)
        for g in range(heads_kv):
            columns = slice(g * HD, (g + 1) * HD)
            both = jnp.concatenate([keys[g, block, :], vals[g, block, :HD]], axis=1)
            cached = jnp.dot(cache_pick, both, preferred_element_type=jnp.float32).astype(jnp.bfloat16)
            kc_ref[slots, columns] = cached[:, :HD]
            vc_ref[slots, columns] = cached[:, HD:]
        allowed = jnp.dot(query_pick, reach, preferred_element_type=jnp.float32)
        near = jnp.concatenate([allowed[:, :rows]] * per_group, axis=0) > 0.5
        valid = jnp.concatenate([allowed[:, rows:]] * per_group, axis=0) > 0.5
        for g in range(heads_kv):
            wanted = wanted_ref[s, g * per_group * capacity : (g + 1) * per_group * capacity, :]
            scores = lax.dot_general(
                wanted,
                keys[g, : (s + 1) * rows, :],
                (((1,), (1,)), ((), ())),
                preferred_element_type=jnp.float32,
            )
            last = jnp.where(near, scores[:, s * rows :], neg_big)
            scores = jnp.concatenate([scores[:, : s * rows], last], axis=1) if s else last
            top = jnp.max(scores, axis=1, keepdims=True)
            weights = jnp.exp((scores - top) * scale).astype(jnp.bfloat16)
            mixed = jnp.dot(weights, vals[g, : (s + 1) * rows, :], preferred_element_type=jnp.float32)
            out = jnp.where(valid, mixed[:, :HD] / mixed[:, HD:], 0.0).astype(jnp.bfloat16)
            for h in range(per_group):
                column = (g * per_group + h) * HD
                att_ref[slots, column : column + HD] = out[h * capacity : (h + 1) * capacity, :]


def few_instances(queries, keys, values, query_owner, cache_owner):
    instances = lax.axis_size("seq")
    rows = queries.shape[0]
    capacity = 3 * rows // (2 * instances)
    heads, heads_kv = queries.shape[1] // HD, keys.shape[1] // HD

    def swap(array, k):
        return lax.ppermute(array, "seq", [(i, i ^ k) for i in range(instances)])

    tall = heads * capacity + 16
    vmem = pl.BlockSpec(memory_space=pltpu.VMEM)
    smem = pl.BlockSpec(memory_space=pltpu.SMEM)
    hbm = pl.BlockSpec(memory_space=pltpu.HBM)
    me = lax.axis_index("seq").astype(jnp.int32).reshape(1)
    k_far, v_far = swap(keys, 2), swap(values, 2)
    kv_tall = 2 * heads_kv * rows
    sends = pl.pallas_call(
        functools.partial(pack_kernel, instances, capacity),
        out_shape=(jax.ShapeDtypeStruct((tall, HD), jnp.bfloat16),) * instances,
        in_specs=[smem, hbm, vmem, vmem],
        out_specs=(vmem,) * instances,
        scratch_shapes=[pltpu.VMEM(queries.shape, jnp.bfloat16), pltpu.SemaphoreType.DMA],
        compiler_params=pltpu.CompilerParams(vmem_limit_bytes=16 << 20),
        cost_estimate=pl.CostEstimate(flops=1 << 27, bytes_accessed=2 << 20, transcendentals=0),
        name="pack",
    )(me, queries, query_owner.reshape(1, rows), cache_owner.reshape(1, rows))
    anyspace = pl.BlockSpec(memory_space=pl.ANY)
    order = (2, 3, 1)
    through = [sends[k] for k in order]
    *through, own_kv, far_kv = pl.pallas_call(
        gate_kernel,
        out_shape=tuple(jax.ShapeDtypeStruct(x.shape, x.dtype) for x in through)
        + (jax.ShapeDtypeStruct((kv_tall, HD), jnp.bfloat16),) * 2,
        in_specs=[vmem] * 4 + [anyspace] * len(through),
        out_specs=(anyspace,) * len(through) + (vmem,) * 2,
        input_output_aliases={4 + i: i for i in range(len(through))},
        compiler_params=pltpu.CompilerParams(vmem_limit_bytes=16 << 20),
        cost_estimate=pl.CostEstimate(flops=0, bytes_accessed=1 << 18, transcendentals=0),
        name="gate",
    )(keys, values, k_far, v_far, *through)
    got = {0: sends[0]}
    for k, slots_of in zip(order, through):
        got[k] = swap(slots_of, k)
    beside, both = swap(own_kv, 1), swap(far_kv, 1)
    slots = instances * capacity
    return pl.pallas_call(
        functools.partial(attend_kernel, instances, capacity, heads, heads_kv),
        out_shape=(
            jax.ShapeDtypeStruct((slots, heads * HD), jnp.bfloat16),
            jax.ShapeDtypeStruct((slots, heads_kv * HD), jnp.bfloat16),
            jax.ShapeDtypeStruct((slots, heads_kv * HD), jnp.bfloat16),
        ),
        in_specs=[smem] + [vmem] * (instances + 6),
        out_specs=(vmem, vmem, vmem),
        scratch_shapes=[
            pltpu.VMEM((instances, tall, HD), jnp.bfloat16),
            pltpu.VMEM((heads_kv, instances * rows, HD), jnp.bfloat16),
            pltpu.VMEM((heads_kv, instances * rows, 2 * HD), jnp.bfloat16),
        ],
        compiler_params=pltpu.CompilerParams(vmem_limit_bytes=24 << 20),
        name="attend",
    )(me, *[got[k] for k in (0, *order)], keys, values, k_far, v_far, beside, both)


def on_device(queries, keys, values, query_owner, cache_owner):
    instances = lax.axis_size("seq")
    rows = queries.shape[0]
    capacity = 3 * rows // (2 * instances)
    heads = queries.shape[1] // HD
    whole_tiles = instances == 4 and capacity % 16 == 0 and rows == HD and heads % 2 == 0
    form = few_instances if whole_tiles else many_instances
    return form(queries, keys, values, query_owner, cache_owner)


def solution(mesh):
    return jax.shard_map(
        on_device,
        mesh=mesh,
        in_specs=(
            P(("groups", "seq"), ("tp", "rep")),
            P(("groups", "seq"), ("tp", "rep")),
            P(("groups", "seq"), ("tp", "rep")),
            P(("groups", "seq"), None),
            P(("groups", "seq"), None),
        ),
        out_specs=(
            P(("groups", "seq"), ("tp", "rep")),
            P(("groups", "seq"), ("tp", "rep")),
            P(("groups", "seq"), ("tp", "rep")),
        ),
        check_vma=False,
    )
```

```python
import functools
import math

import jax
import jax.numpy as jnp
from jax import lax
from jax.experimental import pallas as pl
from jax.experimental.pallas import tpu as pltpu
from jax.sharding import PartitionSpec as P

HD = 128


neg_big = -1e30


def slot_select(owner_list, instances, capacity):
    owners = owner_list[:, 0]
    onehot = (owners[:, None] == jnp.arange(instances, dtype=jnp.int32)[None, :]).astype(jnp.int32)
    earlier = jnp.cumsum(onehot, axis=0) - onehot
    ranking = jnp.sum(earlier * onehot, axis=1)
    target = owners * capacity + ranking
    return target[None, :] == jnp.arange(instances * capacity, dtype=jnp.int32)[:, None]


def pack_rows(select, table_rows, instances):
    selected = jnp.dot(
        select.astype(table_rows.dtype), table_rows, preferred_element_type=jnp.float32
    )
    return selected.astype(table_rows.dtype).reshape(instances, -1, table_rows.shape[1])


def start_state(heads_kv, per_group, slot_count):
    running_max = jnp.full((heads_kv, per_group, slot_count), neg_big, jnp.float32)
    running_sum = jnp.zeros((heads_kv, per_group, slot_count), jnp.float32)
    weighted = jnp.zeros((heads_kv, per_group, slot_count, HD), jnp.float32)
    return (running_max, running_sum, weighted)


def key_block(current, grouped, query_pos, key_piece, value_piece, key_start):
    running_max, running_sum, weighted = current
    key_count = key_piece.shape[0]
    heads_kv = grouped.shape[1]
    key_heads = key_piece.reshape(key_count, heads_kv, HD)
    value_heads = value_piece.reshape(key_count, heads_kv, HD)
    scores = jnp.einsum("rkgd,nkd->kgrn", grouped, key_heads, preferred_element_type=jnp.float32)
    scores = scores * (1.0 / math.sqrt(HD))
    key_pos = key_start + jnp.arange(key_count, dtype=jnp.int32)
    allowed = key_pos[None, :] <= query_pos[:, None]
    scores = jnp.where(allowed, scores, neg_big)
    new_max = jnp.maximum(running_max, jnp.max(scores, axis=-1))
    weights = jnp.where(allowed, jnp.exp(scores - new_max[..., None]), 0.0).astype(jnp.bfloat16)
    rescale = jnp.exp(running_max - new_max)
    running_sum = running_sum * rescale + jnp.sum(weights, axis=-1, dtype=jnp.float32)
    weighted = weighted * rescale[..., None] + jnp.einsum(
        "kgrn,nkd->kgrd", weights, value_heads, preferred_element_type=jnp.float32
    )
    return (new_max, running_sum, weighted)


def folder(grouped, query_pos, current, pieces):
    last_pos = jnp.max(query_pos)
    key_part, value_part = pieces
    key_count = key_part.shape[0]
    block_rows = math.gcd(512, key_count)
    block_count = key_count // block_rows
    key_blocks = key_part.reshape(block_count, block_rows, key_part.shape[1])
    value_blocks = value_part.reshape(block_count, block_rows, value_part.shape[1])

    def visit(carried, block_item):
        block_index, key_piece, value_piece = block_item
        key_start = block_index * block_rows
        updated = lax.cond(
            key_start <= last_pos,
            lambda inner: key_block(inner, grouped, query_pos, key_piece, value_piece, key_start),
            lambda inner: inner,
            carried,
        )
        return (updated, None)

    current, _ = lax.scan(
        visit, current, (jnp.arange(block_count, dtype=jnp.int32), key_blocks, value_blocks)
    )
    return current


def finish(current, slot_count):
    running_max, running_sum, weighted = current
    denominator = jnp.where(running_sum > 0.0, running_sum, 1.0)
    averaged = weighted / denominator[..., None]
    return jnp.transpose(averaged, (2, 0, 1, 3)).reshape(slot_count, -1).astype(jnp.bfloat16)


def many_instances(queries, keys, values, query_owner, cache_owner):
    instances = lax.axis_size("seq")
    own_index = lax.axis_index("seq")
    local_rows = queries.shape[0]
    capacity = 3 * local_rows // (2 * instances)
    slot_count = instances * capacity
    heads_kv = keys.shape[1] // HD
    per_group = queries.shape[1] // keys.shape[1]
    positions = own_index * local_rows + jnp.arange(local_rows, dtype=jnp.int32)
    cache_pick = slot_select(cache_owner, instances, capacity)
    key_slots = pack_rows(cache_pick, keys, instances)
    value_slots = pack_rows(cache_pick, values, instances)
    query_pick = slot_select(query_owner, instances, capacity)
    query_slots = pack_rows(query_pick, queries, instances)
    slot_pos = jnp.max(jnp.where(query_pick, positions[None, :], -1), axis=1).reshape(
        instances, capacity
    )
    query_got, pos_got, key_got, value_got = (
        lax.all_to_all(query_slots, "seq", split_axis=0, concat_axis=0, tiled=True),
        lax.all_to_all(slot_pos, "seq", split_axis=0, concat_axis=0, tiled=True),
        lax.all_to_all(key_slots, "seq", split_axis=0, concat_axis=0, tiled=True),
        lax.all_to_all(value_slots, "seq", split_axis=0, concat_axis=0, tiled=True),
    )
    arrived = query_got.reshape(slot_count, -1)
    arrived_pos = pos_got.reshape(slot_count)
    grouped = arrived.reshape(slot_count, heads_kv, per_group, HD)
    final_state = folder(
        grouped,
        arrived_pos,
        start_state(heads_kv, per_group, slot_count),
        (
            lax.all_gather(keys, "seq", axis=0, tiled=True),
            lax.all_gather(values, "seq", axis=0, tiled=True),
        ),
    )
    attended = finish(final_state, slot_count)
    key_cache = key_got.reshape(slot_count, -1)
    value_cache = value_got.reshape(slot_count, -1)
    return (attended, key_cache, value_cache)


def before(rows):
    r = lax.broadcasted_iota(jnp.int32, (rows, rows), 0)
    u = lax.broadcasted_iota(jnp.int32, (rows, rows), 1)
    return (r < u).astype(jnp.bfloat16)


def picks(marks, earlier, capacity):
    rows = marks.shape[1]
    slot = lax.broadcasted_iota(jnp.int32, (capacity, rows), 0).astype(jnp.float32)
    chosen = jnp.where(marks > 0.5, earlier, -1.0)
    return (chosen == slot).astype(jnp.bfloat16)


def pack_kernel(instances, capacity, me_ref, q_hbm, qo_ref, co_ref, *rest):
    sends, (q_ref, arrived) = rest[:instances], rest[instances:]
    rows = q_ref.shape[0]
    heads = q_ref.shape[1] // HD
    fetch = pltpu.make_async_copy(q_hbm, q_ref, arrived)
    fetch.start()
    me = me_ref[0]
    owners = qo_ref[...]
    lane = lax.broadcasted_iota(jnp.int32, (16, rows), 0)
    dest = jnp.bitwise_xor(lane, me)
    marks = (jnp.broadcast_to(owners, (16, rows)) == dest).astype(jnp.bfloat16)
    earlier = jnp.dot(marks, before(rows), preferred_element_type=jnp.float32)
    wide = marks.astype(jnp.float32)
    select = jnp.concatenate(
        [picks(wide[k : k + 1], earlier[k : k + 1], capacity) for k in range(instances)], axis=0
    )
    lists = jnp.concatenate(
        [owners, co_ref[...], jnp.full((14, rows), -1, jnp.int32)], axis=0
    ).astype(jnp.float32).astype(jnp.bfloat16)
    for k in range(instances):
        sends[k][heads * capacity : heads * capacity + 16, :] = lists
    fetch.wait()
    for pair in range(heads // 2):
        packed = jnp.dot(
            select,
            q_ref[:, pair * 2 * HD : (pair + 1) * 2 * HD],
            preferred_element_type=jnp.float32,
        ).astype(jnp.bfloat16)
        for k in range(instances):
            for half in range(2):
                at = (2 * pair + half) * capacity
                sends[k][at : at + capacity, :] = packed[
                    k * capacity : (k + 1) * capacity, half * HD : (half + 1) * HD
                ]


def gate_kernel(tall, heads_kv, k_ref, v_ref, *rest):
    beside, copied = rest[-2:]
    rows = k_ref.shape[0]
    copies = []
    for index, source in enumerate((k_ref, v_ref)):
        for g in range(heads_kv):
            place = index * heads_kv + g
            copies.append(
                pltpu.make_async_copy(
                    source.at[:, g * HD : (g + 1) * HD],
                    beside.at[tall + place * rows : tall + (place + 1) * rows, :],
                    copied.at[place],
                )
            )
    for copy in copies:
        copy.start()
    for copy in copies:
        copy.wait()


def attend_kernel(instances, capacity, heads, heads_kv, me_ref, *rest):
    got, rest = rest[:instances], rest[instances:]
    k_own, v_own, k_near, v_near, k_far, v_far = rest[:6]
    att_ref, kc_ref, vc_ref, wanted_ref, keys, vals = rest[6:]
    rows = HD
    per_group = heads // heads_kv
    tail = heads * capacity
    me = me_ref[0]
    direct = ((k_own, v_own), (k_near, v_near), (k_far, v_far))
    for k in range(instances):
        source = jnp.bitwise_xor(me, k)
        wanted_ref[source] = got[k][: tail + 16, :]
        at = pl.ds(pl.multiple_of(source * rows, rows), rows)
        for g in range(heads_kv):
            if k < len(direct):
                keys[g, at, :] = direct[k][0][:, g * HD : (g + 1) * HD]
                vals[g, at, :HD] = direct[k][1][:, g * HD : (g + 1) * HD]
            else:
                start = tail + 16 + g * rows
                keys[g, at, :] = got[1][start : start + rows, :]
                start = start + heads_kv * rows
                vals[g, at, :HD] = got[1][start : start + rows, :]
        vals[:, k * rows : (k + 1) * rows, HD:] = jnp.ones((heads_kv, rows, HD), jnp.bfloat16)
    lists = jnp.concatenate([wanted_ref[s, tail : tail + 16, :] for s in range(instances)], axis=0)
    wide = (lists.astype(jnp.float32) == me.astype(jnp.float32)).astype(jnp.float32)
    earlier = jnp.dot(wide.astype(jnp.bfloat16), before(rows), preferred_element_type=jnp.float32)
    r = lax.broadcasted_iota(jnp.int32, (rows, 2 * rows), 0)
    u = lax.broadcasted_iota(jnp.int32, (rows, 2 * rows), 1)
    reach = ((u <= r) | (u >= rows)).astype(jnp.bfloat16)
    scale = math.log2(math.e) / math.sqrt(HD)
    for s in range(instances):
        q_at, c_at = 16 * s, 16 * s + 1
        cache_pick = picks(wide[c_at : c_at + 1], earlier[c_at : c_at + 1], capacity)
        query_pick = picks(wide[q_at : q_at + 1], earlier[q_at : q_at + 1], capacity)
        slots = slice(s * capacity, (s + 1) * capacity)
        block = slice(s * rows, (s + 1) * rows)
        for g in range(heads_kv):
            columns = slice(g * HD, (g + 1) * HD)
            both = jnp.concatenate([keys[g, block, :], vals[g, block, :HD]], axis=1)
            cached = jnp.dot(cache_pick, both, preferred_element_type=jnp.float32).astype(jnp.bfloat16)
            kc_ref[slots, columns] = cached[:, :HD]
            vc_ref[slots, columns] = cached[:, HD:]
        allowed = jnp.dot(query_pick, reach, preferred_element_type=jnp.float32)
        near = jnp.concatenate([allowed[:, :rows]] * per_group, axis=0) > 0.5
        valid = jnp.concatenate([allowed[:, rows:]] * per_group, axis=0) > 0.5
        for g in range(heads_kv):
            wanted = wanted_ref[s, g * per_group * capacity : (g + 1) * per_group * capacity, :]
            scores = lax.dot_general(
                wanted,
                keys[g, : (s + 1) * rows, :],
                (((1,), (1,)), ((), ())),
                preferred_element_type=jnp.float32,
            )
            last = jnp.where(near, scores[:, s * rows :], neg_big)
            scores = jnp.concatenate([scores[:, : s * rows], last], axis=1) if s else last
            top = jnp.max(scores, axis=1, keepdims=True)
            weights = jnp.exp2(scores * scale - top * scale).astype(jnp.bfloat16)
            mixed = jnp.dot(weights, vals[g, : (s + 1) * rows, :], preferred_element_type=jnp.float32)
            out = jnp.where(valid, mixed[:, :HD] / mixed[:, HD:], 0.0).astype(jnp.bfloat16)
            for h in range(per_group):
                column = (g * per_group + h) * HD
                att_ref[slots, column : column + HD] = out[h * capacity : (h + 1) * capacity, :]


def few_instances(queries, keys, values, query_owner, cache_owner):
    instances = lax.axis_size("seq")
    rows = queries.shape[0]
    capacity = 3 * rows // (2 * instances)
    heads, heads_kv = queries.shape[1] // HD, keys.shape[1] // HD

    def swap(array, k):
        return lax.ppermute(array, "seq", [(i, i ^ k) for i in range(instances)])

    tall = heads * capacity + 16
    vmem = pl.BlockSpec(memory_space=pltpu.VMEM)
    smem = pl.BlockSpec(memory_space=pltpu.SMEM)
    hbm = pl.BlockSpec(memory_space=pltpu.HBM)
    me = lax.axis_index("seq").astype(jnp.int32).reshape(1)
    k_far, v_far = swap(keys, 2), swap(values, 2)
    k_near, v_near = swap(keys, 1), swap(values, 1)
    kv_tall = 2 * heads_kv * rows
    sends = pl.pallas_call(
        functools.partial(pack_kernel, instances, capacity),
        out_shape=tuple(
            jax.ShapeDtypeStruct((tall + kv_tall * (k == 1), HD), jnp.bfloat16)
            for k in range(instances)
        ),
        in_specs=[smem, hbm, vmem, vmem],
        out_specs=(vmem,) * instances,
        scratch_shapes=[pltpu.VMEM(queries.shape, jnp.bfloat16), pltpu.SemaphoreType.DMA],
        compiler_params=pltpu.CompilerParams(vmem_limit_bytes=16 << 20),
        cost_estimate=pl.CostEstimate(flops=1 << 27, bytes_accessed=2 << 20, transcendentals=0),
        name="pack",
    )(me, queries, query_owner.reshape(1, rows), cache_owner.reshape(1, rows))
    anyspace = pl.BlockSpec(memory_space=pl.ANY)
    through = [sends[2], sends[3], k_near, v_near, sends[1]]
    through = pl.pallas_call(
        functools.partial(gate_kernel, tall, heads_kv),
        out_shape=tuple(jax.ShapeDtypeStruct(x.shape, x.dtype) for x in through),
        in_specs=[anyspace] * (len(through) + 2),
        out_specs=(anyspace,) * len(through),
        input_output_aliases={2 + i: i for i in range(len(through))},
        scratch_shapes=[pltpu.SemaphoreType.DMA((2 * heads_kv,))],
        cost_estimate=pl.CostEstimate(flops=0, bytes_accessed=1 << 18, transcendentals=0),
        name="gate",
    )(k_far, v_far, *through)
    k_near, v_near = through[2:4]
    got = (sends[0], swap(through[4], 1), swap(through[0], 2), swap(through[1], 3))
    slots = instances * capacity
    return pl.pallas_call(
        functools.partial(attend_kernel, instances, capacity, heads, heads_kv),
        out_shape=(
            jax.ShapeDtypeStruct((slots, heads * HD), jnp.bfloat16),
            jax.ShapeDtypeStruct((slots, heads_kv * HD), jnp.bfloat16),
            jax.ShapeDtypeStruct((slots, heads_kv * HD), jnp.bfloat16),
        ),
        in_specs=[smem] + [vmem] * (instances + 6),
        out_specs=(vmem, vmem, vmem),
        scratch_shapes=[
            pltpu.VMEM((instances, tall, HD), jnp.bfloat16),
            pltpu.VMEM((heads_kv, instances * rows, HD), jnp.bfloat16),
            pltpu.VMEM((heads_kv, instances * rows, 2 * HD), jnp.bfloat16),
        ],
        compiler_params=pltpu.CompilerParams(vmem_limit_bytes=24 << 20),
        name="attend",
    )(me, *[got[k] for k in range(instances)], keys, values, k_near, v_near, k_far, v_far)


def on_device(queries, keys, values, query_owner, cache_owner):
    instances = lax.axis_size("seq")
    rows = queries.shape[0]
    capacity = 3 * rows // (2 * instances)
    heads = queries.shape[1] // HD
    whole_tiles = instances == 4 and capacity % 16 == 0 and rows == HD and heads % 2 == 0
    form = few_instances if whole_tiles else many_instances
    return form(queries, keys, values, query_owner, cache_owner)


def solution(mesh):
    return jax.shard_map(
        on_device,
        mesh=mesh,
        in_specs=(
            P(("groups", "seq"), ("tp", "rep")),
            P(("groups", "seq"), ("tp", "rep")),
            P(("groups", "seq"), ("tp", "rep")),
            P(("groups", "seq"), None),
            P(("groups", "seq"), None),
        ),
        out_specs=(
            P(("groups", "seq"), ("tp", "rep")),
            P(("groups", "seq"), ("tp", "rep")),
            P(("groups", "seq"), ("tp", "rep")),
        ),
        check_vma=False,
    )
```

```python
import functools
import math

import jax
import jax.numpy as jnp
from jax import lax
from jax.experimental import pallas as pl
from jax.experimental.pallas import tpu as pltpu
from jax.sharding import PartitionSpec as P

HD = 128


neg_big = -1e30
DISTANCES = (0, 1, 2, 3)


def slot_select(owner_list, instances, capacity):
    owners = owner_list[:, 0]
    onehot = (owners[:, None] == jnp.arange(instances, dtype=jnp.int32)[None, :]).astype(jnp.int32)
    earlier = jnp.cumsum(onehot, axis=0) - onehot
    ranking = jnp.sum(earlier * onehot, axis=1)
    target = owners * capacity + ranking
    return target[None, :] == jnp.arange(instances * capacity, dtype=jnp.int32)[:, None]


def pack_rows(select, table_rows, instances):
    selected = jnp.dot(
        select.astype(table_rows.dtype), table_rows, preferred_element_type=jnp.float32
    )
    return selected.astype(table_rows.dtype).reshape(instances, -1, table_rows.shape[1])


def start_state(heads_kv, per_group, slot_count):
    running_max = jnp.full((heads_kv, per_group, slot_count), neg_big, jnp.float32)
    running_sum = jnp.zeros((heads_kv, per_group, slot_count), jnp.float32)
    weighted = jnp.zeros((heads_kv, per_group, slot_count, HD), jnp.float32)
    return (running_max, running_sum, weighted)


def key_block(current, grouped, query_pos, key_piece, value_piece, key_start):
    running_max, running_sum, weighted = current
    key_count = key_piece.shape[0]
    heads_kv = grouped.shape[1]
    key_heads = key_piece.reshape(key_count, heads_kv, HD)
    value_heads = value_piece.reshape(key_count, heads_kv, HD)
    scores = jnp.einsum("rkgd,nkd->kgrn", grouped, key_heads, preferred_element_type=jnp.float32)
    scores = scores * (1.0 / math.sqrt(HD))
    key_pos = key_start + jnp.arange(key_count, dtype=jnp.int32)
    allowed = key_pos[None, :] <= query_pos[:, None]
    scores = jnp.where(allowed, scores, neg_big)
    new_max = jnp.maximum(running_max, jnp.max(scores, axis=-1))
    weights = jnp.where(allowed, jnp.exp(scores - new_max[..., None]), 0.0).astype(jnp.bfloat16)
    rescale = jnp.exp(running_max - new_max)
    running_sum = running_sum * rescale + jnp.sum(weights, axis=-1, dtype=jnp.float32)
    weighted = weighted * rescale[..., None] + jnp.einsum(
        "kgrn,nkd->kgrd", weights, value_heads, preferred_element_type=jnp.float32
    )
    return (new_max, running_sum, weighted)


def folder(grouped, query_pos, current, pieces):
    last_pos = jnp.max(query_pos)
    key_part, value_part = pieces
    key_count = key_part.shape[0]
    block_rows = math.gcd(512, key_count)
    block_count = key_count // block_rows
    key_blocks = key_part.reshape(block_count, block_rows, key_part.shape[1])
    value_blocks = value_part.reshape(block_count, block_rows, value_part.shape[1])

    def visit(carried, block_item):
        block_index, key_piece, value_piece = block_item
        key_start = block_index * block_rows
        updated = lax.cond(
            key_start <= last_pos,
            lambda inner: key_block(inner, grouped, query_pos, key_piece, value_piece, key_start),
            lambda inner: inner,
            carried,
        )
        return (updated, None)

    current, _ = lax.scan(
        visit, current, (jnp.arange(block_count, dtype=jnp.int32), key_blocks, value_blocks)
    )
    return current


def finish(current, slot_count):
    running_max, running_sum, weighted = current
    denominator = jnp.where(running_sum > 0.0, running_sum, 1.0)
    averaged = weighted / denominator[..., None]
    return jnp.transpose(averaged, (2, 0, 1, 3)).reshape(slot_count, -1).astype(jnp.bfloat16)


def many_instances(queries, keys, values, query_owner, cache_owner):
    instances = lax.axis_size("seq")
    own_index = lax.axis_index("seq")
    local_rows = queries.shape[0]
    capacity = 3 * local_rows // (2 * instances)
    slot_count = instances * capacity
    heads_kv = keys.shape[1] // HD
    per_group = queries.shape[1] // keys.shape[1]
    positions = own_index * local_rows + jnp.arange(local_rows, dtype=jnp.int32)
    cache_pick = slot_select(cache_owner, instances, capacity)
    key_slots = pack_rows(cache_pick, keys, instances)
    value_slots = pack_rows(cache_pick, values, instances)
    query_pick = slot_select(query_owner, instances, capacity)
    query_slots = pack_rows(query_pick, queries, instances)
    slot_pos = jnp.max(jnp.where(query_pick, positions[None, :], -1), axis=1).reshape(
        instances, capacity
    )
    query_got, pos_got, key_got, value_got = (
        lax.all_to_all(query_slots, "seq", split_axis=0, concat_axis=0, tiled=True),
        lax.all_to_all(slot_pos, "seq", split_axis=0, concat_axis=0, tiled=True),
        lax.all_to_all(key_slots, "seq", split_axis=0, concat_axis=0, tiled=True),
        lax.all_to_all(value_slots, "seq", split_axis=0, concat_axis=0, tiled=True),
    )
    arrived = query_got.reshape(slot_count, -1)
    arrived_pos = pos_got.reshape(slot_count)
    grouped = arrived.reshape(slot_count, heads_kv, per_group, HD)
    final_state = folder(
        grouped,
        arrived_pos,
        start_state(heads_kv, per_group, slot_count),
        (
            lax.all_gather(keys, "seq", axis=0, tiled=True),
            lax.all_gather(values, "seq", axis=0, tiled=True),
        ),
    )
    attended = finish(final_state, slot_count)
    key_cache = key_got.reshape(slot_count, -1)
    value_cache = value_got.reshape(slot_count, -1)
    return (attended, key_cache, value_cache)


def before(rows):
    r = lax.broadcasted_iota(jnp.int32, (rows, rows), 0)
    u = lax.broadcasted_iota(jnp.int32, (rows, rows), 1)
    return (r < u).astype(jnp.bfloat16)


def picks(marks, earlier, capacity):
    rows = marks.shape[1]
    slot = lax.broadcasted_iota(jnp.int32, (capacity, rows), 0).astype(jnp.float32)
    chosen = jnp.where(marks > 0.5, earlier, -1.0)
    return (chosen == slot).astype(jnp.bfloat16)


def pack_kernel(instances, capacity, me_ref, q_hbm, qo_ref, co_ref, *rest):
    *sends, q_ref, arrived = rest
    groups = len(sends) // instances
    rows = q_ref.shape[0]
    heads = q_ref.shape[1] // HD
    fetch = pltpu.make_async_copy(q_hbm, q_ref, arrived)
    fetch.start()
    me = me_ref[0]
    owners = qo_ref[...]
    lane = lax.broadcasted_iota(jnp.int32, (16, rows), 0)
    dest = jnp.bitwise_xor(lane, me)
    marks = (jnp.broadcast_to(owners, (16, rows)) == dest).astype(jnp.bfloat16)
    earlier = jnp.dot(marks, before(rows), preferred_element_type=jnp.float32)
    wide = marks.astype(jnp.float32)
    select = jnp.concatenate(
        [picks(wide[k : k + 1], earlier[k : k + 1], capacity) for k in range(instances)], axis=0
    )
    lists = jnp.concatenate(
        [owners, co_ref[...], jnp.full((14, rows), -1, jnp.int32)], axis=0
    ).astype(jnp.float32).astype(jnp.bfloat16)
    per_group = heads // groups
    for k in range(instances):
        sends[k * groups][per_group * capacity :, :] = lists
    fetch.wait()
    for pair in range(heads // 2):
        packed = jnp.dot(
            select,
            q_ref[:, pair * 2 * HD : (pair + 1) * 2 * HD],
            preferred_element_type=jnp.float32,
        ).astype(jnp.bfloat16)
        for k in range(instances):
            for half in range(2):
                g, h = divmod(2 * pair + half, per_group)
                sends[k * groups + g][h * capacity : (h + 1) * capacity, :] = packed[
                    k * capacity : (k + 1) * capacity, half * HD : (half + 1) * HD
                ]


def join_kernel(k_ref, v_ref, kv_ref):
    rows = k_ref.shape[0]
    at = 0
    for source in (k_ref, v_ref):
        for g in range(source.shape[1] // HD):
            kv_ref[at : at + rows, :] = source[:, g * HD : (g + 1) * HD]
            at += rows


def attend_kernel(instances, capacity, heads, heads_kv, me_ref, *rest):
    pieces = [(k, g) for g in range(heads_kv) for k in DISTANCES]
    got, rest = dict(zip(pieces, rest)), rest[len(pieces) :]
    got_kv, rest = rest[:instances], rest[instances:]
    att_ref, kc_ref, vc_ref, wanted_ref, keys, vals = rest
    rows = HD
    per_group = heads // heads_kv
    tall = per_group * capacity
    tail = heads * capacity
    me = me_ref[0]
    for k in range(instances):
        source = jnp.bitwise_xor(me, k)
        for g in range(heads_kv):
            wanted_ref[source, g * tall : (g + 1) * tall, :] = got[k, g][:tall, :]
        wanted_ref[source, tail:, :] = got[k, 0][tall:, :]
        at = pl.ds(pl.multiple_of(source * rows, rows), rows)
        for g in range(heads_kv):
            start = heads_kv * rows
            keys[g, at, :] = got_kv[k][g * rows : (g + 1) * rows, :]
            vals[g, at, :HD] = got_kv[k][start + g * rows : start + (g + 1) * rows, :]
        vals[:, k * rows : (k + 1) * rows, HD:] = jnp.ones((heads_kv, rows, HD), jnp.bfloat16)
    lists = jnp.concatenate([wanted_ref[s, tail : tail + 16, :] for s in range(instances)], axis=0)
    wide = (lists.astype(jnp.float32) == me.astype(jnp.float32)).astype(jnp.float32)
    earlier = jnp.dot(wide.astype(jnp.bfloat16), before(rows), preferred_element_type=jnp.float32)
    r = lax.broadcasted_iota(jnp.int32, (rows, 2 * rows), 0)
    u = lax.broadcasted_iota(jnp.int32, (rows, 2 * rows), 1)
    reach = ((u <= r) | (u >= rows)).astype(jnp.bfloat16)
    scale = math.log2(math.e) / math.sqrt(HD)
    for s in range(instances):
        q_at, c_at = 16 * s, 16 * s + 1
        cache_pick = picks(wide[c_at : c_at + 1], earlier[c_at : c_at + 1], capacity)
        query_pick = picks(wide[q_at : q_at + 1], earlier[q_at : q_at + 1], capacity)
        slots = slice(s * capacity, (s + 1) * capacity)
        block = slice(s * rows, (s + 1) * rows)
        for g in range(heads_kv):
            columns = slice(g * HD, (g + 1) * HD)
            both = jnp.concatenate([keys[g, block, :], vals[g, block, :HD]], axis=1)
            cached = jnp.dot(cache_pick, both, preferred_element_type=jnp.float32).astype(jnp.bfloat16)
            kc_ref[slots, columns] = cached[:, :HD]
            vc_ref[slots, columns] = cached[:, HD:]
        allowed = jnp.dot(query_pick, reach, preferred_element_type=jnp.float32)
        near = jnp.concatenate([allowed[:, :rows]] * per_group, axis=0) > 0.5
        valid = jnp.concatenate([allowed[:, rows:]] * per_group, axis=0) > 0.5
        for g in range(heads_kv):
            wanted = wanted_ref[s, g * per_group * capacity : (g + 1) * per_group * capacity, :]
            scores = lax.dot_general(
                wanted,
                keys[g, : (s + 1) * rows, :],
                (((1,), (1,)), ((), ())),
                preferred_element_type=jnp.float32,
            )
            last = jnp.where(near, scores[:, s * rows :], neg_big)
            scores = jnp.concatenate([scores[:, : s * rows], last], axis=1) if s else last
            top = jnp.max(scores, axis=1, keepdims=True)
            weights = jnp.exp2(scores * scale - top * scale).astype(jnp.bfloat16)
            mixed = jnp.dot(weights, vals[g, : (s + 1) * rows, :], preferred_element_type=jnp.float32)
            out = jnp.where(valid, mixed[:, :HD] / mixed[:, HD:], 0.0).astype(jnp.bfloat16)
            for h in range(per_group):
                column = (g * per_group + h) * HD
                att_ref[slots, column : column + HD] = out[h * capacity : (h + 1) * capacity, :]


def few_instances(queries, keys, values, query_owner, cache_owner):
    instances = lax.axis_size("seq")
    rows = queries.shape[0]
    capacity = 3 * rows // (2 * instances)
    heads, heads_kv = queries.shape[1] // HD, keys.shape[1] // HD

    def swap(array, k):
        return lax.ppermute(array, "seq", [(i, i ^ k) for i in range(instances)])

    tall = heads // heads_kv * capacity
    kv_tall = 2 * heads_kv * rows
    vmem = pl.BlockSpec(memory_space=pltpu.VMEM)
    smem = pl.BlockSpec(memory_space=pltpu.SMEM)
    hbm = pl.BlockSpec(memory_space=pltpu.HBM)
    me = lax.axis_index("seq").astype(jnp.int32).reshape(1)
    own_kv = pl.pallas_call(
        join_kernel,
        out_shape=jax.ShapeDtypeStruct((kv_tall, HD), jnp.bfloat16),
        in_specs=[vmem] * 2,
        out_specs=vmem,
        compiler_params=pltpu.CompilerParams(vmem_limit_bytes=16 << 20),
        cost_estimate=pl.CostEstimate(flops=0, bytes_accessed=1 << 18, transcendentals=0),
        name="join",
    )(keys, values)
    far_kv, near_kv = swap(own_kv, 2), swap(own_kv, 1)
    both_kv = swap(far_kv, 1)
    sends = pl.pallas_call(
        functools.partial(pack_kernel, instances, capacity),
        out_shape=tuple(
            jax.ShapeDtypeStruct((tall + 16 * (g == 0), HD), jnp.bfloat16)
            for k in range(instances)
            for g in range(heads_kv)
        ),
        in_specs=[smem, hbm, vmem, vmem],
        out_specs=(vmem,) * (instances * heads_kv),
        scratch_shapes=[pltpu.VMEM(queries.shape, jnp.bfloat16), pltpu.SemaphoreType.DMA],
        compiler_params=pltpu.CompilerParams(vmem_limit_bytes=16 << 20),
        cost_estimate=pl.CostEstimate(flops=1 << 27, bytes_accessed=2 << 20, transcendentals=0),
        name="pack",
    )(me, queries, query_owner.reshape(1, rows), cache_owner.reshape(1, rows))
    got = []
    for g in range(heads_kv):
        for k in DISTANCES:
            piece = sends[k * heads_kv + g]
            got.append(swap(piece, k) if k else piece)
    slots = instances * capacity
    return pl.pallas_call(
        functools.partial(attend_kernel, instances, capacity, heads, heads_kv),
        out_shape=(
            jax.ShapeDtypeStruct((slots, heads * HD), jnp.bfloat16),
            jax.ShapeDtypeStruct((slots, heads_kv * HD), jnp.bfloat16),
            jax.ShapeDtypeStruct((slots, heads_kv * HD), jnp.bfloat16),
        ),
        in_specs=[smem] + [vmem] * (len(got) + instances),
        out_specs=(vmem, vmem, vmem),
        scratch_shapes=[
            pltpu.VMEM((instances, heads * capacity + 16, HD), jnp.bfloat16),
            pltpu.VMEM((heads_kv, instances * rows, HD), jnp.bfloat16),
            pltpu.VMEM((heads_kv, instances * rows, 2 * HD), jnp.bfloat16),
        ],
        compiler_params=pltpu.CompilerParams(vmem_limit_bytes=24 << 20),
        name="attend",
    )(me, *got, own_kv, near_kv, far_kv, both_kv)


def on_device(queries, keys, values, query_owner, cache_owner):
    instances = lax.axis_size("seq")
    rows = queries.shape[0]
    capacity = 3 * rows // (2 * instances)
    heads = queries.shape[1] // HD
    whole_tiles = instances == 4 and capacity % 16 == 0 and rows == HD and heads % 2 == 0
    form = few_instances if whole_tiles else many_instances
    return form(queries, keys, values, query_owner, cache_owner)


def solution(mesh):
    return jax.shard_map(
        on_device,
        mesh=mesh,
        in_specs=(
            P(("groups", "seq"), ("tp", "rep")),
            P(("groups", "seq"), ("tp", "rep")),
            P(("groups", "seq"), ("tp", "rep")),
            P(("groups", "seq"), None),
            P(("groups", "seq"), None),
        ),
        out_specs=(
            P(("groups", "seq"), ("tp", "rep")),
            P(("groups", "seq"), ("tp", "rep")),
            P(("groups", "seq"), ("tp", "rep")),
        ),
        check_vma=False,
    )
```

```python
import functools
import math

import jax
import jax.numpy as jnp
from jax import lax
from jax.experimental import pallas as pl
from jax.experimental.pallas import tpu as pltpu
from jax.sharding import PartitionSpec as P

HD = 128


neg_big = -1e30


def slot_select(owner_list, instances, capacity):
    owners = owner_list[:, 0]
    onehot = (owners[:, None] == jnp.arange(instances, dtype=jnp.int32)[None, :]).astype(jnp.int32)
    earlier = jnp.cumsum(onehot, axis=0) - onehot
    ranking = jnp.sum(earlier * onehot, axis=1)
    target = owners * capacity + ranking
    return target[None, :] == jnp.arange(instances * capacity, dtype=jnp.int32)[:, None]


def pack_rows(select, table_rows, instances):
    selected = jnp.dot(
        select.astype(table_rows.dtype), table_rows, preferred_element_type=jnp.float32
    )
    return selected.astype(table_rows.dtype).reshape(instances, -1, table_rows.shape[1])


def start_state(heads_kv, per_group, slot_count):
    running_max = jnp.full((heads_kv, per_group, slot_count), neg_big, jnp.float32)
    running_sum = jnp.zeros((heads_kv, per_group, slot_count), jnp.float32)
    weighted = jnp.zeros((heads_kv, per_group, slot_count, HD), jnp.float32)
    return (running_max, running_sum, weighted)


def key_block(current, grouped, query_pos, key_piece, value_piece, key_start):
    running_max, running_sum, weighted = current
    key_count = key_piece.shape[0]
    heads_kv = grouped.shape[1]
    key_heads = key_piece.reshape(key_count, heads_kv, HD)
    value_heads = value_piece.reshape(key_count, heads_kv, HD)
    scores = jnp.einsum("rkgd,nkd->kgrn", grouped, key_heads, preferred_element_type=jnp.float32)
    scores = scores * (1.0 / math.sqrt(HD))
    key_pos = key_start + jnp.arange(key_count, dtype=jnp.int32)
    allowed = key_pos[None, :] <= query_pos[:, None]
    scores = jnp.where(allowed, scores, neg_big)
    new_max = jnp.maximum(running_max, jnp.max(scores, axis=-1))
    weights = jnp.where(allowed, jnp.exp(scores - new_max[..., None]), 0.0).astype(jnp.bfloat16)
    rescale = jnp.exp(running_max - new_max)
    running_sum = running_sum * rescale + jnp.sum(weights, axis=-1, dtype=jnp.float32)
    weighted = weighted * rescale[..., None] + jnp.einsum(
        "kgrn,nkd->kgrd", weights, value_heads, preferred_element_type=jnp.float32
    )
    return (new_max, running_sum, weighted)


def folder(grouped, query_pos, current, pieces):
    last_pos = jnp.max(query_pos)
    key_part, value_part = pieces
    key_count = key_part.shape[0]
    block_rows = math.gcd(512, key_count)
    block_count = key_count // block_rows
    key_blocks = key_part.reshape(block_count, block_rows, key_part.shape[1])
    value_blocks = value_part.reshape(block_count, block_rows, value_part.shape[1])

    def visit(carried, block_item):
        block_index, key_piece, value_piece = block_item
        key_start = block_index * block_rows
        updated = lax.cond(
            key_start <= last_pos,
            lambda inner: key_block(inner, grouped, query_pos, key_piece, value_piece, key_start),
            lambda inner: inner,
            carried,
        )
        return (updated, None)

    current, _ = lax.scan(
        visit, current, (jnp.arange(block_count, dtype=jnp.int32), key_blocks, value_blocks)
    )
    return current


def finish(current, slot_count):
    running_max, running_sum, weighted = current
    denominator = jnp.where(running_sum > 0.0, running_sum, 1.0)
    averaged = weighted / denominator[..., None]
    return jnp.transpose(averaged, (2, 0, 1, 3)).reshape(slot_count, -1).astype(jnp.bfloat16)


def many_instances(queries, keys, values, query_owner, cache_owner):
    instances = lax.axis_size("seq")
    own_index = lax.axis_index("seq")
    local_rows = queries.shape[0]
    capacity = 3 * local_rows // (2 * instances)
    slot_count = instances * capacity
    heads_kv = keys.shape[1] // HD
    per_group = queries.shape[1] // keys.shape[1]
    positions = own_index * local_rows + jnp.arange(local_rows, dtype=jnp.int32)
    cache_pick = slot_select(cache_owner, instances, capacity)
    key_slots = pack_rows(cache_pick, keys, instances)
    value_slots = pack_rows(cache_pick, values, instances)
    query_pick = slot_select(query_owner, instances, capacity)
    query_slots = pack_rows(query_pick, queries, instances)
    slot_pos = jnp.max(jnp.where(query_pick, positions[None, :], -1), axis=1).reshape(
        instances, capacity
    )
    query_got, pos_got, key_got, value_got = (
        lax.all_to_all(query_slots, "seq", split_axis=0, concat_axis=0, tiled=True),
        lax.all_to_all(slot_pos, "seq", split_axis=0, concat_axis=0, tiled=True),
        lax.all_to_all(key_slots, "seq", split_axis=0, concat_axis=0, tiled=True),
        lax.all_to_all(value_slots, "seq", split_axis=0, concat_axis=0, tiled=True),
    )
    arrived = query_got.reshape(slot_count, -1)
    arrived_pos = pos_got.reshape(slot_count)
    grouped = arrived.reshape(slot_count, heads_kv, per_group, HD)
    final_state = folder(
        grouped,
        arrived_pos,
        start_state(heads_kv, per_group, slot_count),
        (
            lax.all_gather(keys, "seq", axis=0, tiled=True),
            lax.all_gather(values, "seq", axis=0, tiled=True),
        ),
    )
    attended = finish(final_state, slot_count)
    key_cache = key_got.reshape(slot_count, -1)
    value_cache = value_got.reshape(slot_count, -1)
    return (attended, key_cache, value_cache)


def before(rows):
    r = lax.broadcasted_iota(jnp.int32, (rows, rows), 0)
    u = lax.broadcasted_iota(jnp.int32, (rows, rows), 1)
    return (r < u).astype(jnp.bfloat16)


def picks(marks, earlier, capacity):
    rows = marks.shape[1]
    slot = lax.broadcasted_iota(jnp.int32, (capacity, rows), 0).astype(jnp.float32)
    chosen = jnp.where(marks > 0.5, earlier, -1.0)
    return (chosen == slot).astype(jnp.bfloat16)


def pack_kernel(instances, capacity, me_ref, q_hbm, kv_ref, qo_ref, co_ref, *rest):
    lead, rest = rest[:instances], rest[instances:]
    sends, (q_ref, arrived) = (lead, rest[:instances]), rest[instances:]
    rows = q_ref.shape[0]
    heads = q_ref.shape[1] // HD
    fetch = pltpu.make_async_copy(q_hbm, q_ref, arrived)
    fetch.start()
    me = me_ref[0]
    owners = qo_ref[...]
    lane = lax.broadcasted_iota(jnp.int32, (16, rows), 0)
    dest = jnp.bitwise_xor(lane, me)
    marks = (jnp.broadcast_to(owners, (16, rows)) == dest).astype(jnp.bfloat16)
    earlier = jnp.dot(marks, before(rows), preferred_element_type=jnp.float32)
    wide = marks.astype(jnp.float32)
    select = jnp.concatenate(
        [picks(wide[k : k + 1], earlier[k : k + 1], capacity) for k in range(instances)], axis=0
    )
    lists = jnp.concatenate(
        [owners, co_ref[...], jnp.full((14, rows), -1, jnp.int32)], axis=0
    ).astype(jnp.float32).astype(jnp.bfloat16)
    per_group = heads // 2
    tall = per_group * capacity
    for k in range(instances):
        lead[k][tall : tall + 16, :] = lists
    for block in range(kv_ref.shape[1] // HD):
        at = tall + 16 + block * rows
        lead[1][at : at + rows, :] = kv_ref[:, block * HD : (block + 1) * HD]
    fetch.wait()
    for pair in range(heads // 2):
        packed = jnp.dot(
            select,
            q_ref[:, pair * 2 * HD : (pair + 1) * 2 * HD],
            preferred_element_type=jnp.float32,
        ).astype(jnp.bfloat16)
        for k in range(instances):
            for half in range(2):
                g, h = divmod(2 * pair + half, per_group)
                sends[g][k][h * capacity : (h + 1) * capacity, :] = packed[
                    k * capacity : (k + 1) * capacity, half * HD : (half + 1) * HD
                ]


def attend_head(instances, capacity, per_group, wanted_ref, keys, vals, allowed_ref, store):
    rows = HD
    tall = per_group * capacity
    scale = math.log2(math.e) / math.sqrt(HD)
    for s in reversed(range(instances)):
        slots = slice(s * capacity, (s + 1) * capacity)
        allowed = allowed_ref[slots, :].astype(jnp.float32)
        near = jnp.concatenate([allowed[:, :rows]] * per_group, axis=0) > 0.5
        valid = jnp.concatenate([allowed[:, rows:]] * per_group, axis=0) > 0.5
        scores = lax.dot_general(
            wanted_ref[s, :tall, :],
            keys[: (s + 1) * rows, :],
            (((1,), (1,)), ((), ())),
            preferred_element_type=jnp.float32,
        )
        last = jnp.where(near, scores[:, s * rows :], neg_big)
        scores = jnp.concatenate([scores[:, : s * rows], last], axis=1) if s else last
        top = jnp.max(scores, axis=1, keepdims=True)
        weights = jnp.exp2(scores * scale - top * scale).astype(jnp.bfloat16)
        mixed = jnp.dot(weights, vals[: (s + 1) * rows, :], preferred_element_type=jnp.float32)
        out = jnp.where(valid, mixed[:, :HD] / mixed[:, HD:], 0.0).astype(jnp.bfloat16)
        for h in range(per_group):
            store(s, slots, h, out[h * capacity : (h + 1) * capacity, :])


def lead_kernel(instances, capacity, per_group, me_ref, *rest):
    got, rest = rest[:instances], rest[instances:]
    own, far, both, half_ref, allowed_ref, keys_ref, vals_ref, kc_ref, vc_ref = rest[:9]
    wanted_ref, keys, vals = rest[9:]
    rows = HD
    tall = per_group * capacity
    me = me_ref[0]
    direct = {0: own, 2: far, 3: both}
    ones = jnp.ones((rows, HD), jnp.bfloat16)
    for k in range(instances):
        source = jnp.bitwise_xor(me, k)
        wanted_ref[source] = got[k][: tall + 16, :]
        at = pl.ds(pl.multiple_of(source * rows, rows), rows)
        blocks = []
        for block in range(4):
            if k in direct:
                blocks.append(direct[k][:, block * HD : (block + 1) * HD])
            else:
                start = tall + 16 + block * rows
                blocks.append(got[k][start : start + rows, :])
        keys[at, :] = blocks[0]
        keys_ref[at, :] = blocks[1]
        vals[at, :HD] = blocks[2]
        vals_ref[at, :HD] = blocks[3]
        vals[k * rows : (k + 1) * rows, HD:] = ones
        vals_ref[k * rows : (k + 1) * rows, HD:] = ones
    lists = jnp.concatenate([wanted_ref[s, tall : tall + 16, :] for s in range(instances)], axis=0)
    wide = (lists.astype(jnp.float32) == me.astype(jnp.float32)).astype(jnp.float32)
    earlier = jnp.dot(wide.astype(jnp.bfloat16), before(rows), preferred_element_type=jnp.float32)
    r = lax.broadcasted_iota(jnp.int32, (rows, 2 * rows), 0)
    u = lax.broadcasted_iota(jnp.int32, (rows, 2 * rows), 1)
    reach = ((u <= r) | (u >= rows)).astype(jnp.bfloat16)
    for s in range(instances):
        q_at, c_at = 16 * s, 16 * s + 1
        cache_pick = picks(wide[c_at : c_at + 1], earlier[c_at : c_at + 1], capacity)
        query_pick = picks(wide[q_at : q_at + 1], earlier[q_at : q_at + 1], capacity)
        slots = slice(s * capacity, (s + 1) * capacity)
        block = slice(s * rows, (s + 1) * rows)
        for g, (k_ref, v_ref) in enumerate(((keys, vals), (keys_ref, vals_ref))):
            columns = slice(g * HD, (g + 1) * HD)
            pair = jnp.concatenate([k_ref[block, :], v_ref[block, :HD]], axis=1)
            cached = jnp.dot(cache_pick, pair, preferred_element_type=jnp.float32).astype(jnp.bfloat16)
            kc_ref[slots, columns] = cached[:, :HD]
            vc_ref[slots, columns] = cached[:, HD:]
        allowed_ref[slots, :] = jnp.dot(query_pick, reach, preferred_element_type=jnp.float32).astype(
            jnp.bfloat16
        )

    def store(s, slots, h, value):
        half_ref[slots, h * HD : (h + 1) * HD] = value

    attend_head(instances, capacity, per_group, wanted_ref, keys, vals, allowed_ref, store)


def rest_kernel(instances, capacity, per_group, me_ref, *rest):
    got, rest = rest[:instances], rest[instances:]
    half_ref, allowed_ref, keys_ref, vals_ref, att_hbm, wanted_ref, mine_ref, sent = rest
    width = per_group * HD
    early = pltpu.make_async_copy(half_ref, att_hbm.at[:, :width], sent.at[instances])
    early.start()
    for k in range(instances):
        wanted_ref[jnp.bitwise_xor(me_ref[0], k)] = got[k][...]
    copies = []

    def store(s, slots, h, value):
        mine_ref[slots, h * HD : (h + 1) * HD] = value
        if h == per_group - 1:
            copy = pltpu.make_async_copy(
                mine_ref.at[slots, :], att_hbm.at[slots, width:], sent.at[s]
            )
            copy.start()
            copies.append(copy)

    attend_head(instances, capacity, per_group, wanted_ref, keys_ref, vals_ref, allowed_ref, store)
    for copy in [early, *copies]:
        copy.wait()


def few_instances(queries, keys, values, query_owner, cache_owner):
    instances = lax.axis_size("seq")
    rows = queries.shape[0]
    capacity = 3 * rows // (2 * instances)
    heads = queries.shape[1] // HD
    per_group = heads // 2
    tall = per_group * capacity
    slots = instances * capacity

    def swap(array, k):
        return lax.ppermute(array, "seq", [(i, i ^ k) for i in range(instances)])

    vmem = pl.BlockSpec(memory_space=pltpu.VMEM)
    smem = pl.BlockSpec(memory_space=pltpu.SMEM)
    hbm = pl.BlockSpec(memory_space=pltpu.HBM)
    shape = lambda *dims: jax.ShapeDtypeStruct(dims, jnp.bfloat16)
    me = lax.axis_index("seq").astype(jnp.int32).reshape(1)
    own_kv = jnp.concatenate([keys, values], axis=1)
    far_kv = swap(own_kv, 2)
    both_kv = swap(far_kv, 1)
    sends = pl.pallas_call(
        functools.partial(pack_kernel, instances, capacity),
        out_shape=tuple(shape(tall + 16 + 4 * rows * (k == 1), HD) for k in range(instances))
        + (shape(tall, HD),) * instances,
        in_specs=[smem, hbm, vmem, vmem, vmem],
        out_specs=(vmem,) * (2 * instances),
        scratch_shapes=[pltpu.VMEM(queries.shape, jnp.bfloat16), pltpu.SemaphoreType.DMA],
        compiler_params=pltpu.CompilerParams(vmem_limit_bytes=16 << 20),
        cost_estimate=pl.CostEstimate(flops=1 << 27, bytes_accessed=2 << 20, transcendentals=0),
        name="pack",
    )(me, queries, own_kv, query_owner.reshape(1, rows), cache_owner.reshape(1, rows))
    got = [swap(piece, i % instances) if i % instances else piece for i, piece in enumerate(sends)]
    half, allowed, keys_rest, vals_rest, key_cache, value_cache = pl.pallas_call(
        functools.partial(lead_kernel, instances, capacity, per_group),
        out_shape=(
            shape(slots, per_group * HD),
            shape(slots, 2 * rows),
            shape(instances * rows, HD),
            shape(instances * rows, 2 * HD),
            shape(slots, 2 * HD),
            shape(slots, 2 * HD),
        ),
        in_specs=[smem] + [vmem] * (instances + 3),
        out_specs=(vmem,) * 6,
        scratch_shapes=[
            pltpu.VMEM((instances, tall + 16, HD), jnp.bfloat16),
            pltpu.VMEM((instances * rows, HD), jnp.bfloat16),
            pltpu.VMEM((instances * rows, 2 * HD), jnp.bfloat16),
        ],
        compiler_params=pltpu.CompilerParams(vmem_limit_bytes=24 << 20),
        cost_estimate=pl.CostEstimate(flops=1 << 29, bytes_accessed=2 << 20, transcendentals=1 << 19),
        name="attend_lead",
    )(me, *got[:instances], own_kv, far_kv, both_kv)
    attended = pl.pallas_call(
        functools.partial(rest_kernel, instances, capacity, per_group),
        out_shape=shape(slots, heads * HD),
        in_specs=[smem] + [vmem] * (instances + 4),
        out_specs=hbm,
        scratch_shapes=[
            pltpu.VMEM((instances, tall, HD), jnp.bfloat16),
            pltpu.VMEM((slots, per_group * HD), jnp.bfloat16),
            pltpu.SemaphoreType.DMA((instances + 1,)),
        ],
        compiler_params=pltpu.CompilerParams(vmem_limit_bytes=24 << 20),
        cost_estimate=pl.CostEstimate(flops=1 << 29, bytes_accessed=2 << 20, transcendentals=1 << 19),
        name="attend_rest",
    )(me, *got[instances:], half, allowed, keys_rest, vals_rest)
    return (attended, key_cache, value_cache)


def on_device(queries, keys, values, query_owner, cache_owner):
    instances = lax.axis_size("seq")
    rows = queries.shape[0]
    capacity = 3 * rows // (2 * instances)
    heads = queries.shape[1] // HD
    whole_tiles = (
        instances == 4
        and capacity % 16 == 0
        and rows == HD
        and keys.shape[1] == 2 * HD
        and heads % 4 == 0
    )
    form = few_instances if whole_tiles else many_instances
    return form(queries, keys, values, query_owner, cache_owner)


def solution(mesh):
    return jax.shard_map(
        on_device,
        mesh=mesh,
        in_specs=(
            P(("groups", "seq"), ("tp", "rep")),
            P(("groups", "seq"), ("tp", "rep")),
            P(("groups", "seq"), ("tp", "rep")),
            P(("groups", "seq"), None),
            P(("groups", "seq"), None),
        ),
        out_specs=(
            P(("groups", "seq"), ("tp", "rep")),
            P(("groups", "seq"), ("tp", "rep")),
            P(("groups", "seq"), ("tp", "rep")),
        ),
        check_vma=False,
    )
```

```python
import functools
import math

import jax
import jax.numpy as jnp
from jax import lax
from jax.experimental import pallas as pl
from jax.experimental.pallas import tpu as pltpu
from jax.sharding import PartitionSpec as P

HD = 128


neg_big = -1e30
SECOND = (0, 2, 3, 1)


def slot_select(owner_list, instances, capacity):
    owners = owner_list[:, 0]
    onehot = (owners[:, None] == jnp.arange(instances, dtype=jnp.int32)[None, :]).astype(jnp.int32)
    earlier = jnp.cumsum(onehot, axis=0) - onehot
    ranking = jnp.sum(earlier * onehot, axis=1)
    target = owners * capacity + ranking
    return target[None, :] == jnp.arange(instances * capacity, dtype=jnp.int32)[:, None]


def pack_rows(select, table_rows, instances):
    selected = jnp.dot(
        select.astype(table_rows.dtype), table_rows, preferred_element_type=jnp.float32
    )
    return selected.astype(table_rows.dtype).reshape(instances, -1, table_rows.shape[1])


def start_state(heads_kv, per_group, slot_count):
    running_max = jnp.full((heads_kv, per_group, slot_count), neg_big, jnp.float32)
    running_sum = jnp.zeros((heads_kv, per_group, slot_count), jnp.float32)
    weighted = jnp.zeros((heads_kv, per_group, slot_count, HD), jnp.float32)
    return (running_max, running_sum, weighted)


def key_block(current, grouped, query_pos, key_piece, value_piece, key_start):
    running_max, running_sum, weighted = current
    key_count = key_piece.shape[0]
    heads_kv = grouped.shape[1]
    key_heads = key_piece.reshape(key_count, heads_kv, HD)
    value_heads = value_piece.reshape(key_count, heads_kv, HD)
    scores = jnp.einsum("rkgd,nkd->kgrn", grouped, key_heads, preferred_element_type=jnp.float32)
    scores = scores * (1.0 / math.sqrt(HD))
    key_pos = key_start + jnp.arange(key_count, dtype=jnp.int32)
    allowed = key_pos[None, :] <= query_pos[:, None]
    scores = jnp.where(allowed, scores, neg_big)
    new_max = jnp.maximum(running_max, jnp.max(scores, axis=-1))
    weights = jnp.where(allowed, jnp.exp(scores - new_max[..., None]), 0.0).astype(jnp.bfloat16)
    rescale = jnp.exp(running_max - new_max)
    running_sum = running_sum * rescale + jnp.sum(weights, axis=-1, dtype=jnp.float32)
    weighted = weighted * rescale[..., None] + jnp.einsum(
        "kgrn,nkd->kgrd", weights, value_heads, preferred_element_type=jnp.float32
    )
    return (new_max, running_sum, weighted)


def folder(grouped, query_pos, current, pieces):
    last_pos = jnp.max(query_pos)
    key_part, value_part = pieces
    key_count = key_part.shape[0]
    block_rows = math.gcd(512, key_count)
    block_count = key_count // block_rows
    key_blocks = key_part.reshape(block_count, block_rows, key_part.shape[1])
    value_blocks = value_part.reshape(block_count, block_rows, value_part.shape[1])

    def visit(carried, block_item):
        block_index, key_piece, value_piece = block_item
        key_start = block_index * block_rows
        updated = lax.cond(
            key_start <= last_pos,
            lambda inner: key_block(inner, grouped, query_pos, key_piece, value_piece, key_start),
            lambda inner: inner,
            carried,
        )
        return (updated, None)

    current, _ = lax.scan(
        visit, current, (jnp.arange(block_count, dtype=jnp.int32), key_blocks, value_blocks)
    )
    return current


def finish(current, slot_count):
    running_max, running_sum, weighted = current
    denominator = jnp.where(running_sum > 0.0, running_sum, 1.0)
    averaged = weighted / denominator[..., None]
    return jnp.transpose(averaged, (2, 0, 1, 3)).reshape(slot_count, -1).astype(jnp.bfloat16)


def many_instances(queries, keys, values, query_owner, cache_owner):
    instances = lax.axis_size("seq")
    own_index = lax.axis_index("seq")
    local_rows = queries.shape[0]
    capacity = 3 * local_rows // (2 * instances)
    slot_count = instances * capacity
    heads_kv = keys.shape[1] // HD
    per_group = queries.shape[1] // keys.shape[1]
    positions = own_index * local_rows + jnp.arange(local_rows, dtype=jnp.int32)
    cache_pick = slot_select(cache_owner, instances, capacity)
    key_slots = pack_rows(cache_pick, keys, instances)
    value_slots = pack_rows(cache_pick, values, instances)
    query_pick = slot_select(query_owner, instances, capacity)
    query_slots = pack_rows(query_pick, queries, instances)
    slot_pos = jnp.max(jnp.where(query_pick, positions[None, :], -1), axis=1).reshape(
        instances, capacity
    )
    query_got, pos_got, key_got, value_got = (
        lax.all_to_all(query_slots, "seq", split_axis=0, concat_axis=0, tiled=True),
        lax.all_to_all(slot_pos, "seq", split_axis=0, concat_axis=0, tiled=True),
        lax.all_to_all(key_slots, "seq", split_axis=0, concat_axis=0, tiled=True),
        lax.all_to_all(value_slots, "seq", split_axis=0, concat_axis=0, tiled=True),
    )
    arrived = query_got.reshape(slot_count, -1)
    arrived_pos = pos_got.reshape(slot_count)
    grouped = arrived.reshape(slot_count, heads_kv, per_group, HD)
    final_state = folder(
        grouped,
        arrived_pos,
        start_state(heads_kv, per_group, slot_count),
        (
            lax.all_gather(keys, "seq", axis=0, tiled=True),
            lax.all_gather(values, "seq", axis=0, tiled=True),
        ),
    )
    attended = finish(final_state, slot_count)
    key_cache = key_got.reshape(slot_count, -1)
    value_cache = value_got.reshape(slot_count, -1)
    return (attended, key_cache, value_cache)


def before(rows):
    r = lax.broadcasted_iota(jnp.int32, (rows, rows), 0)
    u = lax.broadcasted_iota(jnp.int32, (rows, rows), 1)
    return (r < u).astype(jnp.bfloat16)


def picks(marks, earlier, capacity):
    rows = marks.shape[1]
    slot = lax.broadcasted_iota(jnp.int32, (capacity, rows), 0).astype(jnp.float32)
    chosen = jnp.where(marks > 0.5, earlier, -1.0)
    return (chosen == slot).astype(jnp.bfloat16)


def pack_kernel(instances, capacity, me_ref, q_hbm, kv_ref, qo_ref, co_ref, *rest):
    lead, rest = rest[:instances], rest[instances:]
    second, (q_ref, arrived) = dict(zip(SECOND, rest)), rest[instances:]
    sends = (lead, second)
    rows = q_ref.shape[0]
    heads = q_ref.shape[1] // HD
    fetch = pltpu.make_async_copy(q_hbm, q_ref, arrived)
    fetch.start()
    me = me_ref[0]
    owners = qo_ref[...]
    lane = lax.broadcasted_iota(jnp.int32, (16, rows), 0)
    dest = jnp.bitwise_xor(lane, me)
    marks = (jnp.broadcast_to(owners, (16, rows)) == dest).astype(jnp.bfloat16)
    earlier = jnp.dot(marks, before(rows), preferred_element_type=jnp.float32)
    wide = marks.astype(jnp.float32)
    select = jnp.concatenate(
        [picks(wide[k : k + 1], earlier[k : k + 1], capacity) for k in range(instances)], axis=0
    )
    lists = jnp.concatenate(
        [owners, co_ref[...], jnp.full((14, rows), -1, jnp.int32)], axis=0
    ).astype(jnp.float32).astype(jnp.bfloat16)
    per_group = heads // 2
    tall = per_group * capacity
    for k in range(instances):
        lead[k][tall : tall + 16, :] = lists
    for block in range(kv_ref.shape[1] // HD):
        at = tall + 16 + block * rows
        lead[1][at : at + rows, :] = kv_ref[:, block * HD : (block + 1) * HD]
    fetch.wait()
    for pair in range(heads // 2):
        packed = jnp.dot(
            select,
            q_ref[:, pair * 2 * HD : (pair + 1) * 2 * HD],
            preferred_element_type=jnp.float32,
        ).astype(jnp.bfloat16)
        for k in range(instances):
            for half in range(2):
                g, h = divmod(2 * pair + half, per_group)
                sends[g][k][h * capacity : (h + 1) * capacity, :] = packed[
                    k * capacity : (k + 1) * capacity, half * HD : (half + 1) * HD
                ]


def attend_head(instances, capacity, per_group, wanted_ref, keys, vals, allowed_ref, store):
    rows = HD
    tall = per_group * capacity
    scale = math.log2(math.e) / math.sqrt(HD)
    for s in reversed(range(instances)):
        slots = slice(s * capacity, (s + 1) * capacity)
        allowed = allowed_ref[slots, :].astype(jnp.float32)
        near = jnp.concatenate([allowed[:, :rows]] * per_group, axis=0) > 0.5
        valid = jnp.concatenate([allowed[:, rows:]] * per_group, axis=0) > 0.5
        scores = lax.dot_general(
            wanted_ref[s, :tall, :],
            keys[: (s + 1) * rows, :],
            (((1,), (1,)), ((), ())),
            preferred_element_type=jnp.float32,
        )
        last = jnp.where(near, scores[:, s * rows :], neg_big)
        scores = jnp.concatenate([scores[:, : s * rows], last], axis=1) if s else last
        top = jnp.max(scores, axis=1, keepdims=True)
        weights = jnp.exp2(scores * scale - top * scale).astype(jnp.bfloat16)
        mixed = jnp.dot(weights, vals[: (s + 1) * rows, :], preferred_element_type=jnp.float32)
        out = jnp.where(valid, mixed[:, :HD] / mixed[:, HD:], 0.0).astype(jnp.bfloat16)
        for h in range(per_group):
            store(s, slots, h, out[h * capacity : (h + 1) * capacity, :])


def lead_kernel(instances, capacity, per_group, me_ref, *rest):
    got, rest = rest[:instances], rest[instances:]
    own, far, both, half_ref, allowed_ref, keys_ref, vals_ref, kc_ref, vc_ref = rest[:9]
    wanted_ref, keys, vals = rest[9:]
    rows = HD
    tall = per_group * capacity
    me = me_ref[0]
    direct = {0: own, 2: far, 3: both}
    ones = jnp.ones((rows, HD), jnp.bfloat16)
    for k in range(instances):
        source = jnp.bitwise_xor(me, k)
        wanted_ref[source] = got[k][: tall + 16, :]
        at = pl.ds(pl.multiple_of(source * rows, rows), rows)
        blocks = []
        for block in range(4):
            if k in direct:
                blocks.append(direct[k][:, block * HD : (block + 1) * HD])
            else:
                start = tall + 16 + block * rows
                blocks.append(got[k][start : start + rows, :])
        keys[at, :] = blocks[0]
        keys_ref[at, :] = blocks[1]
        vals[at, :HD] = blocks[2]
        vals_ref[at, :HD] = blocks[3]
        vals[k * rows : (k + 1) * rows, HD:] = ones
        vals_ref[k * rows : (k + 1) * rows, HD:] = ones
    lists = jnp.concatenate([wanted_ref[s, tall : tall + 16, :] for s in range(instances)], axis=0)
    wide = (lists.astype(jnp.float32) == me.astype(jnp.float32)).astype(jnp.float32)
    earlier = jnp.dot(wide.astype(jnp.bfloat16), before(rows), preferred_element_type=jnp.float32)
    r = lax.broadcasted_iota(jnp.int32, (rows, 2 * rows), 0)
    u = lax.broadcasted_iota(jnp.int32, (rows, 2 * rows), 1)
    reach = ((u <= r) | (u >= rows)).astype(jnp.bfloat16)
    for s in range(instances):
        q_at, c_at = 16 * s, 16 * s + 1
        cache_pick = picks(wide[c_at : c_at + 1], earlier[c_at : c_at + 1], capacity)
        query_pick = picks(wide[q_at : q_at + 1], earlier[q_at : q_at + 1], capacity)
        slots = slice(s * capacity, (s + 1) * capacity)
        block = slice(s * rows, (s + 1) * rows)
        for g, (k_ref, v_ref) in enumerate(((keys, vals), (keys_ref, vals_ref))):
            columns = slice(g * HD, (g + 1) * HD)
            pair = jnp.concatenate([k_ref[block, :], v_ref[block, :HD]], axis=1)
            cached = jnp.dot(cache_pick, pair, preferred_element_type=jnp.float32).astype(jnp.bfloat16)
            kc_ref[slots, columns] = cached[:, :HD]
            vc_ref[slots, columns] = cached[:, HD:]
        allowed_ref[slots, :] = jnp.dot(query_pick, reach, preferred_element_type=jnp.float32).astype(
            jnp.bfloat16
        )

    def store(s, slots, h, value):
        half_ref[slots, h * HD : (h + 1) * HD] = value

    attend_head(instances, capacity, per_group, wanted_ref, keys, vals, allowed_ref, store)


def rest_kernel(instances, capacity, per_group, me_ref, *rest):
    got, rest = rest[:instances], rest[instances:]
    half_ref, allowed_ref, keys_ref, vals_ref, att_hbm, wanted_ref, mine_ref, sent = rest
    width = per_group * HD
    early = pltpu.make_async_copy(half_ref, att_hbm.at[:, :width], sent.at[instances])
    early.start()
    for k, piece in zip(SECOND, got):
        wanted_ref[jnp.bitwise_xor(me_ref[0], k)] = piece[...]
    copies = []

    def store(s, slots, h, value):
        mine_ref[slots, h * HD : (h + 1) * HD] = value
        if h == per_group - 1:
            copy = pltpu.make_async_copy(
                mine_ref.at[slots, :], att_hbm.at[slots, width:], sent.at[s]
            )
            copy.start()
            copies.append(copy)

    attend_head(instances, capacity, per_group, wanted_ref, keys_ref, vals_ref, allowed_ref, store)
    for copy in [early, *copies]:
        copy.wait()


def few_instances(queries, keys, values, query_owner, cache_owner):
    instances = lax.axis_size("seq")
    rows = queries.shape[0]
    capacity = 3 * rows // (2 * instances)
    heads = queries.shape[1] // HD
    per_group = heads // 2
    tall = per_group * capacity
    slots = instances * capacity

    def swap(array, k):
        return lax.ppermute(array, "seq", [(i, i ^ k) for i in range(instances)])

    vmem = pl.BlockSpec(memory_space=pltpu.VMEM)
    smem = pl.BlockSpec(memory_space=pltpu.SMEM)
    hbm = pl.BlockSpec(memory_space=pltpu.HBM)
    shape = lambda *dims: jax.ShapeDtypeStruct(dims, jnp.bfloat16)
    me = lax.axis_index("seq").astype(jnp.int32).reshape(1)
    own_kv = jnp.concatenate([keys, values], axis=1)
    far_kv = swap(own_kv, 2)
    both_kv = swap(far_kv, 1)
    sends = pl.pallas_call(
        functools.partial(pack_kernel, instances, capacity),
        out_shape=tuple(shape(tall + 16 + 4 * rows * (k == 1), HD) for k in range(instances))
        + (shape(tall, HD),) * instances,
        in_specs=[smem, hbm, vmem, vmem, vmem],
        out_specs=(vmem,) * (2 * instances),
        scratch_shapes=[pltpu.VMEM(queries.shape, jnp.bfloat16), pltpu.SemaphoreType.DMA],
        compiler_params=pltpu.CompilerParams(vmem_limit_bytes=16 << 20),
        cost_estimate=pl.CostEstimate(flops=1 << 27, bytes_accessed=2 << 20, transcendentals=0),
        name="pack",
    )(me, queries, own_kv, query_owner.reshape(1, rows), cache_owner.reshape(1, rows))
    distances = (*range(instances), *SECOND)
    got = [swap(piece, k) if k else piece for k, piece in zip(distances, sends)]
    half, allowed, keys_rest, vals_rest, key_cache, value_cache = pl.pallas_call(
        functools.partial(lead_kernel, instances, capacity, per_group),
        out_shape=(
            shape(slots, per_group * HD),
            shape(slots, 2 * rows),
            shape(instances * rows, HD),
            shape(instances * rows, 2 * HD),
            shape(slots, 2 * HD),
            shape(slots, 2 * HD),
        ),
        in_specs=[smem] + [vmem] * (instances + 3),
        out_specs=(vmem,) * 6,
        scratch_shapes=[
            pltpu.VMEM((instances, tall + 16, HD), jnp.bfloat16),
            pltpu.VMEM((instances * rows, HD), jnp.bfloat16),
            pltpu.VMEM((instances * rows, 2 * HD), jnp.bfloat16),
        ],
        compiler_params=pltpu.CompilerParams(vmem_limit_bytes=24 << 20),
        cost_estimate=pl.CostEstimate(flops=1 << 29, bytes_accessed=2 << 20, transcendentals=1 << 19),
        name="attend_lead",
    )(me, *got[:instances], own_kv, far_kv, both_kv)
    attended = pl.pallas_call(
        functools.partial(rest_kernel, instances, capacity, per_group),
        out_shape=shape(slots, heads * HD),
        in_specs=[smem] + [vmem] * (instances + 4),
        out_specs=hbm,
        scratch_shapes=[
            pltpu.VMEM((instances, tall, HD), jnp.bfloat16),
            pltpu.VMEM((slots, per_group * HD), jnp.bfloat16),
            pltpu.SemaphoreType.DMA((instances + 1,)),
        ],
        compiler_params=pltpu.CompilerParams(vmem_limit_bytes=24 << 20),
        cost_estimate=pl.CostEstimate(flops=1 << 29, bytes_accessed=2 << 20, transcendentals=1 << 19),
        name="attend_rest",
    )(me, *got[instances:], half, allowed, keys_rest, vals_rest)
    return (attended, key_cache, value_cache)


def on_device(queries, keys, values, query_owner, cache_owner):
    instances = lax.axis_size("seq")
    rows = queries.shape[0]
    capacity = 3 * rows // (2 * instances)
    heads = queries.shape[1] // HD
    whole_tiles = (
        instances == 4
        and capacity % 16 == 0
        and rows == HD
        and keys.shape[1] == 2 * HD
        and heads % 4 == 0
    )
    form = few_instances if whole_tiles else many_instances
    return form(queries, keys, values, query_owner, cache_owner)


def solution(mesh):
    return jax.shard_map(
        on_device,
        mesh=mesh,
        in_specs=(
            P(("groups", "seq"), ("tp", "rep")),
            P(("groups", "seq"), ("tp", "rep")),
            P(("groups", "seq"), ("tp", "rep")),
            P(("groups", "seq"), None),
            P(("groups", "seq"), None),
        ),
        out_specs=(
            P(("groups", "seq"), ("tp", "rep")),
            P(("groups", "seq"), ("tp", "rep")),
            P(("groups", "seq"), ("tp", "rep")),
        ),
        check_vma=False,
    )
```

```python
import functools
import math

import jax
import jax.numpy as jnp
from jax import lax
from jax.experimental import pallas as pl
from jax.experimental.pallas import tpu as pltpu
from jax.sharding import PartitionSpec as P

HD = 128


neg_big = -1e30
SECOND = (2, 3)


def slot_select(owner_list, instances, capacity):
    owners = owner_list[:, 0]
    onehot = (owners[:, None] == jnp.arange(instances, dtype=jnp.int32)[None, :]).astype(jnp.int32)
    earlier = jnp.cumsum(onehot, axis=0) - onehot
    ranking = jnp.sum(earlier * onehot, axis=1)
    target = owners * capacity + ranking
    return target[None, :] == jnp.arange(instances * capacity, dtype=jnp.int32)[:, None]


def pack_rows(select, table_rows, instances):
    selected = jnp.dot(
        select.astype(table_rows.dtype), table_rows, preferred_element_type=jnp.float32
    )
    return selected.astype(table_rows.dtype).reshape(instances, -1, table_rows.shape[1])


def start_state(heads_kv, per_group, slot_count):
    running_max = jnp.full((heads_kv, per_group, slot_count), neg_big, jnp.float32)
    running_sum = jnp.zeros((heads_kv, per_group, slot_count), jnp.float32)
    weighted = jnp.zeros((heads_kv, per_group, slot_count, HD), jnp.float32)
    return (running_max, running_sum, weighted)


def key_block(current, grouped, query_pos, key_piece, value_piece, key_start):
    running_max, running_sum, weighted = current
    key_count = key_piece.shape[0]
    heads_kv = grouped.shape[1]
    key_heads = key_piece.reshape(key_count, heads_kv, HD)
    value_heads = value_piece.reshape(key_count, heads_kv, HD)
    scores = jnp.einsum("rkgd,nkd->kgrn", grouped, key_heads, preferred_element_type=jnp.float32)
    scores = scores * (1.0 / math.sqrt(HD))
    key_pos = key_start + jnp.arange(key_count, dtype=jnp.int32)
    allowed = key_pos[None, :] <= query_pos[:, None]
    scores = jnp.where(allowed, scores, neg_big)
    new_max = jnp.maximum(running_max, jnp.max(scores, axis=-1))
    weights = jnp.where(allowed, jnp.exp(scores - new_max[..., None]), 0.0).astype(jnp.bfloat16)
    rescale = jnp.exp(running_max - new_max)
    running_sum = running_sum * rescale + jnp.sum(weights, axis=-1, dtype=jnp.float32)
    weighted = weighted * rescale[..., None] + jnp.einsum(
        "kgrn,nkd->kgrd", weights, value_heads, preferred_element_type=jnp.float32
    )
    return (new_max, running_sum, weighted)


def folder(grouped, query_pos, current, pieces):
    last_pos = jnp.max(query_pos)
    key_part, value_part = pieces
    key_count = key_part.shape[0]
    block_rows = math.gcd(512, key_count)
    block_count = key_count // block_rows
    key_blocks = key_part.reshape(block_count, block_rows, key_part.shape[1])
    value_blocks = value_part.reshape(block_count, block_rows, value_part.shape[1])

    def visit(carried, block_item):
        block_index, key_piece, value_piece = block_item
        key_start = block_index * block_rows
        updated = lax.cond(
            key_start <= last_pos,
            lambda inner: key_block(inner, grouped, query_pos, key_piece, value_piece, key_start),
            lambda inner: inner,
            carried,
        )
        return (updated, None)

    current, _ = lax.scan(
        visit, current, (jnp.arange(block_count, dtype=jnp.int32), key_blocks, value_blocks)
    )
    return current


def finish(current, slot_count):
    running_max, running_sum, weighted = current
    denominator = jnp.where(running_sum > 0.0, running_sum, 1.0)
    averaged = weighted / denominator[..., None]
    return jnp.transpose(averaged, (2, 0, 1, 3)).reshape(slot_count, -1).astype(jnp.bfloat16)


def many_instances(queries, keys, values, query_owner, cache_owner):
    instances = lax.axis_size("seq")
    own_index = lax.axis_index("seq")
    local_rows = queries.shape[0]
    capacity = 3 * local_rows // (2 * instances)
    slot_count = instances * capacity
    heads_kv = keys.shape[1] // HD
    per_group = queries.shape[1] // keys.shape[1]
    positions = own_index * local_rows + jnp.arange(local_rows, dtype=jnp.int32)
    cache_pick = slot_select(cache_owner, instances, capacity)
    key_slots = pack_rows(cache_pick, keys, instances)
    value_slots = pack_rows(cache_pick, values, instances)
    query_pick = slot_select(query_owner, instances, capacity)
    query_slots = pack_rows(query_pick, queries, instances)
    slot_pos = jnp.max(jnp.where(query_pick, positions[None, :], -1), axis=1).reshape(
        instances, capacity
    )
    query_got, pos_got, key_got, value_got = (
        lax.all_to_all(query_slots, "seq", split_axis=0, concat_axis=0, tiled=True),
        lax.all_to_all(slot_pos, "seq", split_axis=0, concat_axis=0, tiled=True),
        lax.all_to_all(key_slots, "seq", split_axis=0, concat_axis=0, tiled=True),
        lax.all_to_all(value_slots, "seq", split_axis=0, concat_axis=0, tiled=True),
    )
    arrived = query_got.reshape(slot_count, -1)
    arrived_pos = pos_got.reshape(slot_count)
    grouped = arrived.reshape(slot_count, heads_kv, per_group, HD)
    final_state = folder(
        grouped,
        arrived_pos,
        start_state(heads_kv, per_group, slot_count),
        (
            lax.all_gather(keys, "seq", axis=0, tiled=True),
            lax.all_gather(values, "seq", axis=0, tiled=True),
        ),
    )
    attended = finish(final_state, slot_count)
    key_cache = key_got.reshape(slot_count, -1)
    value_cache = value_got.reshape(slot_count, -1)
    return (attended, key_cache, value_cache)


def before(rows):
    r = lax.broadcasted_iota(jnp.int32, (rows, rows), 0)
    u = lax.broadcasted_iota(jnp.int32, (rows, rows), 1)
    return (r < u).astype(jnp.bfloat16)


def picks(marks, earlier, capacity):
    rows = marks.shape[1]
    slot = lax.broadcasted_iota(jnp.int32, (capacity, rows), 0).astype(jnp.float32)
    chosen = jnp.where(marks > 0.5, earlier, -1.0)
    return (chosen == slot).astype(jnp.bfloat16)


def gate_kernel(near_ref, slots_ref, through_ref):
    pass


def pack_kernel(instances, capacity, me_ref, q_hbm, qo_ref, co_ref, *rest):
    lead, rest = rest[:instances], rest[instances:]
    second, (q_ref, arrived) = dict(zip(SECOND, rest)), rest[len(SECOND) :]
    rows = q_ref.shape[0]
    heads = q_ref.shape[1] // HD
    fetch = pltpu.make_async_copy(q_hbm, q_ref, arrived)
    fetch.start()
    me = me_ref[0]
    owners = qo_ref[...]
    lane = lax.broadcasted_iota(jnp.int32, (16, rows), 0)
    dest = jnp.bitwise_xor(lane, me)
    marks = (jnp.broadcast_to(owners, (16, rows)) == dest).astype(jnp.bfloat16)
    earlier = jnp.dot(marks, before(rows), preferred_element_type=jnp.float32)
    wide = marks.astype(jnp.float32)
    select = jnp.concatenate(
        [picks(wide[k : k + 1], earlier[k : k + 1], capacity) for k in range(instances)], axis=0
    )
    lists = jnp.concatenate(
        [owners, co_ref[...], jnp.full((14, rows), -1, jnp.int32)], axis=0
    ).astype(jnp.float32).astype(jnp.bfloat16)
    per_group = heads // 2
    tall = per_group * capacity
    for k in range(instances):
        lead[k][tall : tall + 16, :] = lists
    fetch.wait()
    for pair in range(heads // 2):
        packed = jnp.dot(
            select,
            q_ref[:, pair * 2 * HD : (pair + 1) * 2 * HD],
            preferred_element_type=jnp.float32,
        ).astype(jnp.bfloat16)
        for k in range(instances):
            for half in range(2):
                g, h = divmod(2 * pair + half, per_group)
                at = h * capacity + (tall + 16) * (g == 1 and k not in second)
                ref = second[k] if g == 1 and k in second else lead[k]
                ref[at : at + capacity, :] = packed[
                    k * capacity : (k + 1) * capacity, half * HD : (half + 1) * HD
                ]


def attend_head(instances, capacity, per_group, wanted_ref, keys, vals, allowed_ref, store):
    rows = HD
    tall = per_group * capacity
    scale = math.log2(math.e) / math.sqrt(HD)
    for s in reversed(range(instances)):
        slots = slice(s * capacity, (s + 1) * capacity)
        allowed = allowed_ref[slots, :].astype(jnp.float32)
        near = jnp.concatenate([allowed[:, :rows]] * per_group, axis=0) > 0.5
        valid = jnp.concatenate([allowed[:, rows:]] * per_group, axis=0) > 0.5
        scores = lax.dot_general(
            wanted_ref[s, :tall, :],
            keys[: (s + 1) * rows, :],
            (((1,), (1,)), ((), ())),
            preferred_element_type=jnp.float32,
        )
        last = jnp.where(near, scores[:, s * rows :], neg_big)
        scores = jnp.concatenate([scores[:, : s * rows], last], axis=1) if s else last
        top = jnp.max(scores, axis=1, keepdims=True)
        weights = jnp.exp2(scores * scale - top * scale).astype(jnp.bfloat16)
        mixed = jnp.dot(weights, vals[: (s + 1) * rows, :], preferred_element_type=jnp.float32)
        out = jnp.where(valid, mixed[:, :HD] / mixed[:, HD:], 0.0).astype(jnp.bfloat16)
        for h in range(per_group):
            store(s, slots, h, out[h * capacity : (h + 1) * capacity, :])


def lead_kernel(instances, capacity, per_group, me_ref, *rest):
    got, rest = rest[:instances], rest[instances:]
    blocks_of, rest = rest[:instances], rest[instances:]
    half_ref, allowed_ref, keys_ref, vals_ref, kc_ref, vc_ref, wanted_ref, keys, vals = rest
    rows = HD
    tall = per_group * capacity
    me = me_ref[0]
    ones = jnp.ones((rows, HD), jnp.bfloat16)
    for k in range(instances):
        source = jnp.bitwise_xor(me, k)
        wanted_ref[source] = got[k][: tall + 16, :]
        at = pl.ds(pl.multiple_of(source * rows, rows), rows)
        blocks = [blocks_of[k][:, block * HD : (block + 1) * HD] for block in range(4)]
        keys[at, :] = blocks[0]
        keys_ref[at, :] = blocks[1]
        vals[at, :HD] = blocks[2]
        vals_ref[at, :HD] = blocks[3]
        vals[k * rows : (k + 1) * rows, HD:] = ones
        vals_ref[k * rows : (k + 1) * rows, HD:] = ones
    lists = jnp.concatenate([wanted_ref[s, tall : tall + 16, :] for s in range(instances)], axis=0)
    wide = (lists.astype(jnp.float32) == me.astype(jnp.float32)).astype(jnp.float32)
    earlier = jnp.dot(wide.astype(jnp.bfloat16), before(rows), preferred_element_type=jnp.float32)
    r = lax.broadcasted_iota(jnp.int32, (rows, 2 * rows), 0)
    u = lax.broadcasted_iota(jnp.int32, (rows, 2 * rows), 1)
    reach = ((u <= r) | (u >= rows)).astype(jnp.bfloat16)
    for s in range(instances):
        q_at, c_at = 16 * s, 16 * s + 1
        cache_pick = picks(wide[c_at : c_at + 1], earlier[c_at : c_at + 1], capacity)
        query_pick = picks(wide[q_at : q_at + 1], earlier[q_at : q_at + 1], capacity)
        slots = slice(s * capacity, (s + 1) * capacity)
        block = slice(s * rows, (s + 1) * rows)
        for g, (k_ref, v_ref) in enumerate(((keys, vals), (keys_ref, vals_ref))):
            columns = slice(g * HD, (g + 1) * HD)
            pair = jnp.concatenate([k_ref[block, :], v_ref[block, :HD]], axis=1)
            cached = jnp.dot(cache_pick, pair, preferred_element_type=jnp.float32).astype(jnp.bfloat16)
            kc_ref[slots, columns] = cached[:, :HD]
            vc_ref[slots, columns] = cached[:, HD:]
        allowed_ref[slots, :] = jnp.dot(query_pick, reach, preferred_element_type=jnp.float32).astype(
            jnp.bfloat16
        )

    def store(s, slots, h, value):
        half_ref[slots, h * HD : (h + 1) * HD] = value

    attend_head(instances, capacity, per_group, wanted_ref, keys, vals, allowed_ref, store)


def rest_kernel(instances, capacity, per_group, me_ref, *rest):
    got, rest = rest[:instances], rest[instances:]
    half_ref, allowed_ref, keys_ref, vals_ref, att_hbm, wanted_ref, mine_ref, sent = rest
    width = per_group * HD
    early = pltpu.make_async_copy(half_ref, att_hbm.at[:, :width], sent.at[instances])
    early.start()
    tall = per_group * capacity
    for k, piece in zip((0, 1, *SECOND), got):
        start = 0 if k in SECOND else tall + 16
        wanted_ref[jnp.bitwise_xor(me_ref[0], k)] = piece[start : start + tall, :]
    copies = []

    def store(s, slots, h, value):
        mine_ref[slots, h * HD : (h + 1) * HD] = value
        if h == per_group - 1:
            copy = pltpu.make_async_copy(
                mine_ref.at[slots, :], att_hbm.at[slots, width:], sent.at[s]
            )
            copy.start()
            copies.append(copy)

    attend_head(instances, capacity, per_group, wanted_ref, keys_ref, vals_ref, allowed_ref, store)
    for copy in [early, *copies]:
        copy.wait()


def few_instances(queries, keys, values, query_owner, cache_owner):
    instances = lax.axis_size("seq")
    rows = queries.shape[0]
    capacity = 3 * rows // (2 * instances)
    heads = queries.shape[1] // HD
    per_group = heads // 2
    tall = per_group * capacity
    slots = instances * capacity

    def swap(array, k):
        return lax.ppermute(array, "seq", [(i, i ^ k) for i in range(instances)])

    vmem = pl.BlockSpec(memory_space=pltpu.VMEM)
    smem = pl.BlockSpec(memory_space=pltpu.SMEM)
    hbm = pl.BlockSpec(memory_space=pltpu.HBM)
    shape = lambda *dims: jax.ShapeDtypeStruct(dims, jnp.bfloat16)
    me = lax.axis_index("seq").astype(jnp.int32).reshape(1)
    own_kv = jnp.concatenate([keys, values], axis=1)
    far_kv, near_kv = swap(own_kv, 2), swap(own_kv, 1)
    both_kv = swap(far_kv, 1)
    distances = (*range(instances), *SECOND)
    sends = pl.pallas_call(
        functools.partial(pack_kernel, instances, capacity),
        out_shape=tuple(
            shape(tall + 16 + tall * (k not in SECOND), HD) for k in range(instances)
        )
        + (shape(tall, HD),) * len(SECOND),
        in_specs=[smem, hbm, vmem, vmem],
        out_specs=(vmem,) * len(distances),
        scratch_shapes=[pltpu.VMEM(queries.shape, jnp.bfloat16), pltpu.SemaphoreType.DMA],
        compiler_params=pltpu.CompilerParams(vmem_limit_bytes=16 << 20),
        cost_estimate=pl.CostEstimate(flops=1 << 27, bytes_accessed=2 << 20, transcendentals=0),
        name="pack",
    )(me, queries, query_owner.reshape(1, rows), cache_owner.reshape(1, rows))
    anyspace = pl.BlockSpec(memory_space=pl.ANY)
    beside = pl.pallas_call(
        gate_kernel,
        out_shape=shape(*sends[1].shape),
        in_specs=[anyspace] * 2,
        out_specs=anyspace,
        input_output_aliases={1: 0},
        compiler_params=pltpu.CompilerParams(vmem_limit_bytes=16 << 20),
        cost_estimate=pl.CostEstimate(flops=0, bytes_accessed=0, transcendentals=0),
        name="gate",
    )(near_kv, sends[1])
    sends = [sends[0], beside, *sends[2:]]
    got = [swap(piece, k) if k else piece for k, piece in zip(distances, sends)]
    half, allowed, keys_rest, vals_rest, key_cache, value_cache = pl.pallas_call(
        functools.partial(lead_kernel, instances, capacity, per_group),
        out_shape=(
            shape(slots, per_group * HD),
            shape(slots, 2 * rows),
            shape(instances * rows, HD),
            shape(instances * rows, 2 * HD),
            shape(slots, 2 * HD),
            shape(slots, 2 * HD),
        ),
        in_specs=[smem] + [vmem] * (2 * instances),
        out_specs=(vmem,) * 6,
        scratch_shapes=[
            pltpu.VMEM((instances, tall + 16, HD), jnp.bfloat16),
            pltpu.VMEM((instances * rows, HD), jnp.bfloat16),
            pltpu.VMEM((instances * rows, 2 * HD), jnp.bfloat16),
        ],
        compiler_params=pltpu.CompilerParams(vmem_limit_bytes=24 << 20),
        cost_estimate=pl.CostEstimate(flops=1 << 29, bytes_accessed=2 << 20, transcendentals=1 << 19),
        name="attend_lead",
    )(me, *got[:instances], own_kv, near_kv, far_kv, both_kv)
    attended = pl.pallas_call(
        functools.partial(rest_kernel, instances, capacity, per_group),
        out_shape=shape(slots, heads * HD),
        in_specs=[smem] + [vmem] * (instances + 4),
        out_specs=hbm,
        scratch_shapes=[
            pltpu.VMEM((instances, tall, HD), jnp.bfloat16),
            pltpu.VMEM((slots, per_group * HD), jnp.bfloat16),
            pltpu.SemaphoreType.DMA((instances + 1,)),
        ],
        compiler_params=pltpu.CompilerParams(vmem_limit_bytes=24 << 20),
        cost_estimate=pl.CostEstimate(flops=1 << 29, bytes_accessed=2 << 20, transcendentals=1 << 19),
        name="attend_rest",
    )(me, *got[:2], *got[instances:], half, allowed, keys_rest, vals_rest)
    return (attended, key_cache, value_cache)


def on_device(queries, keys, values, query_owner, cache_owner):
    instances = lax.axis_size("seq")
    rows = queries.shape[0]
    capacity = 3 * rows // (2 * instances)
    heads = queries.shape[1] // HD
    whole_tiles = (
        instances == 4
        and capacity % 16 == 0
        and rows == HD
        and keys.shape[1] == 2 * HD
        and heads % 4 == 0
    )
    form = few_instances if whole_tiles else many_instances
    return form(queries, keys, values, query_owner, cache_owner)


def solution(mesh):
    return jax.shard_map(
        on_device,
        mesh=mesh,
        in_specs=(
            P(("groups", "seq"), ("tp", "rep")),
            P(("groups", "seq"), ("tp", "rep")),
            P(("groups", "seq"), ("tp", "rep")),
            P(("groups", "seq"), None),
            P(("groups", "seq"), None),
        ),
        out_specs=(
            P(("groups", "seq"), ("tp", "rep")),
            P(("groups", "seq"), ("tp", "rep")),
            P(("groups", "seq"), ("tp", "rep")),
        ),
        check_vma=False,
    )
```

```python
import functools
import math

import jax
import jax.numpy as jnp
from jax import lax
from jax.experimental import pallas as pl
from jax.experimental.pallas import tpu as pltpu
from jax.sharding import PartitionSpec as P

HD = 128


neg_big = -1e30
SECOND = (2, 3)


def slot_select(owner_list, instances, capacity):
    owners = owner_list[:, 0]
    onehot = (owners[:, None] == jnp.arange(instances, dtype=jnp.int32)[None, :]).astype(jnp.int32)
    earlier = jnp.cumsum(onehot, axis=0) - onehot
    ranking = jnp.sum(earlier * onehot, axis=1)
    target = owners * capacity + ranking
    return target[None, :] == jnp.arange(instances * capacity, dtype=jnp.int32)[:, None]


def pack_rows(select, table_rows, instances):
    selected = jnp.dot(
        select.astype(table_rows.dtype), table_rows, preferred_element_type=jnp.float32
    )
    return selected.astype(table_rows.dtype).reshape(instances, -1, table_rows.shape[1])


def start_state(heads_kv, per_group, slot_count):
    running_max = jnp.full((heads_kv, per_group, slot_count), neg_big, jnp.float32)
    running_sum = jnp.zeros((heads_kv, per_group, slot_count), jnp.float32)
    weighted = jnp.zeros((heads_kv, per_group, slot_count, HD), jnp.float32)
    return (running_max, running_sum, weighted)


def key_block(current, grouped, query_pos, key_piece, value_piece, key_start):
    running_max, running_sum, weighted = current
    key_count = key_piece.shape[0]
    heads_kv = grouped.shape[1]
    key_heads = key_piece.reshape(key_count, heads_kv, HD)
    value_heads = value_piece.reshape(key_count, heads_kv, HD)
    scores = jnp.einsum("rkgd,nkd->kgrn", grouped, key_heads, preferred_element_type=jnp.float32)
    scores = scores * (1.0 / math.sqrt(HD))
    key_pos = key_start + jnp.arange(key_count, dtype=jnp.int32)
    allowed = key_pos[None, :] <= query_pos[:, None]
    scores = jnp.where(allowed, scores, neg_big)
    new_max = jnp.maximum(running_max, jnp.max(scores, axis=-1))
    weights = jnp.where(allowed, jnp.exp(scores - new_max[..., None]), 0.0).astype(jnp.bfloat16)
    rescale = jnp.exp(running_max - new_max)
    running_sum = running_sum * rescale + jnp.sum(weights, axis=-1, dtype=jnp.float32)
    weighted = weighted * rescale[..., None] + jnp.einsum(
        "kgrn,nkd->kgrd", weights, value_heads, preferred_element_type=jnp.float32
    )
    return (new_max, running_sum, weighted)


def folder(grouped, query_pos, current, pieces):
    last_pos = jnp.max(query_pos)
    key_part, value_part = pieces
    key_count = key_part.shape[0]
    block_rows = math.gcd(512, key_count)
    block_count = key_count // block_rows
    key_blocks = key_part.reshape(block_count, block_rows, key_part.shape[1])
    value_blocks = value_part.reshape(block_count, block_rows, value_part.shape[1])

    def visit(carried, block_item):
        block_index, key_piece, value_piece = block_item
        key_start = block_index * block_rows
        updated = lax.cond(
            key_start <= last_pos,
            lambda inner: key_block(inner, grouped, query_pos, key_piece, value_piece, key_start),
            lambda inner: inner,
            carried,
        )
        return (updated, None)

    current, _ = lax.scan(
        visit, current, (jnp.arange(block_count, dtype=jnp.int32), key_blocks, value_blocks)
    )
    return current


def finish(current, slot_count):
    running_max, running_sum, weighted = current
    denominator = jnp.where(running_sum > 0.0, running_sum, 1.0)
    averaged = weighted / denominator[..., None]
    return jnp.transpose(averaged, (2, 0, 1, 3)).reshape(slot_count, -1).astype(jnp.bfloat16)


def many_instances(queries, keys, values, query_owner, cache_owner):
    instances = lax.axis_size("seq")
    own_index = lax.axis_index("seq")
    local_rows = queries.shape[0]
    capacity = 3 * local_rows // (2 * instances)
    slot_count = instances * capacity
    heads_kv = keys.shape[1] // HD
    per_group = queries.shape[1] // keys.shape[1]
    positions = own_index * local_rows + jnp.arange(local_rows, dtype=jnp.int32)
    cache_pick = slot_select(cache_owner, instances, capacity)
    key_slots = pack_rows(cache_pick, keys, instances)
    value_slots = pack_rows(cache_pick, values, instances)
    query_pick = slot_select(query_owner, instances, capacity)
    query_slots = pack_rows(query_pick, queries, instances)
    slot_pos = jnp.max(jnp.where(query_pick, positions[None, :], -1), axis=1).reshape(
        instances, capacity
    )
    query_got, pos_got, key_got, value_got = (
        lax.all_to_all(query_slots, "seq", split_axis=0, concat_axis=0, tiled=True),
        lax.all_to_all(slot_pos, "seq", split_axis=0, concat_axis=0, tiled=True),
        lax.all_to_all(key_slots, "seq", split_axis=0, concat_axis=0, tiled=True),
        lax.all_to_all(value_slots, "seq", split_axis=0, concat_axis=0, tiled=True),
    )
    arrived = query_got.reshape(slot_count, -1)
    arrived_pos = pos_got.reshape(slot_count)
    grouped = arrived.reshape(slot_count, heads_kv, per_group, HD)
    final_state = folder(
        grouped,
        arrived_pos,
        start_state(heads_kv, per_group, slot_count),
        (
            lax.all_gather(keys, "seq", axis=0, tiled=True),
            lax.all_gather(values, "seq", axis=0, tiled=True),
        ),
    )
    attended = finish(final_state, slot_count)
    key_cache = key_got.reshape(slot_count, -1)
    value_cache = value_got.reshape(slot_count, -1)
    return (attended, key_cache, value_cache)


def before(rows):
    r = lax.broadcasted_iota(jnp.int32, (rows, rows), 0)
    u = lax.broadcasted_iota(jnp.int32, (rows, rows), 1)
    return (r < u).astype(jnp.bfloat16)


def picks(marks, earlier, capacity):
    rows = marks.shape[1]
    slot = lax.broadcasted_iota(jnp.int32, (capacity, rows), 0).astype(jnp.float32)
    chosen = jnp.where(marks > 0.5, earlier, -1.0)
    return (chosen == slot).astype(jnp.bfloat16)


def gate_kernel(near_ref, slots_ref, through_ref):
    pass


def pack_kernel(instances, capacity, me_ref, q_hbm, qo_ref, co_ref, *rest):
    lead, rest = rest[:instances], rest[instances:]
    second, (q_ref, arrived) = dict(zip(SECOND, rest)), rest[len(SECOND) :]
    rows = q_ref.shape[0]
    heads = q_ref.shape[1] // HD
    fetch = pltpu.make_async_copy(q_hbm, q_ref, arrived)
    fetch.start()
    me = me_ref[0]
    owners = qo_ref[...]
    lane = lax.broadcasted_iota(jnp.int32, (16, rows), 0)
    dest = jnp.bitwise_xor(lane, me)
    marks = (jnp.broadcast_to(owners, (16, rows)) == dest).astype(jnp.bfloat16)
    earlier = jnp.dot(marks, before(rows), preferred_element_type=jnp.float32)
    wide = marks.astype(jnp.float32)
    select = jnp.concatenate(
        [picks(wide[k : k + 1], earlier[k : k + 1], capacity) for k in range(instances)], axis=0
    )
    lists = jnp.concatenate(
        [owners, co_ref[...], jnp.full((14, rows), -1, jnp.int32)], axis=0
    ).astype(jnp.float32).astype(jnp.bfloat16)
    per_group = heads // 2
    tall = per_group * capacity
    for k in range(instances):
        lead[k][tall : tall + 16, :] = lists
    fetch.wait()
    for pair in range(heads // 2):
        packed = jnp.dot(
            select,
            q_ref[:, pair * 2 * HD : (pair + 1) * 2 * HD],
            preferred_element_type=jnp.float32,
        ).astype(jnp.bfloat16)
        for k in range(instances):
            for half in range(2):
                g, h = divmod(2 * pair + half, per_group)
                at = h * capacity + (tall + 16) * (g == 1 and k not in second)
                ref = second[k] if g == 1 and k in second else lead[k]
                ref[at : at + capacity, :] = packed[
                    k * capacity : (k + 1) * capacity, half * HD : (half + 1) * HD
                ]


def attend_head(instances, capacity, per_group, wanted_ref, keys, vals, allowed_ref, store):
    rows = HD
    tall = per_group * capacity
    scale = math.log2(math.e) / math.sqrt(HD)
    for s in reversed(range(instances)):
        slots = slice(s * capacity, (s + 1) * capacity)
        allowed = allowed_ref[slots, :].astype(jnp.float32)
        near = jnp.concatenate([allowed[:, :rows]] * per_group, axis=0) > 0.5
        valid = jnp.concatenate([allowed[:, rows:]] * per_group, axis=0) > 0.5
        scores = lax.dot_general(
            wanted_ref[s, :tall, :],
            keys[: (s + 1) * rows, :],
            (((1,), (1,)), ((), ())),
            preferred_element_type=jnp.float32,
        )
        last = jnp.where(near, scores[:, s * rows :], neg_big)
        scores = jnp.concatenate([scores[:, : s * rows], last], axis=1) if s else last
        top = jnp.max(scores, axis=1, keepdims=True)
        weights = jnp.exp2(scores * scale - top * scale).astype(jnp.bfloat16)
        mixed = jnp.dot(weights, vals[: (s + 1) * rows, :], preferred_element_type=jnp.float32)
        out = jnp.where(valid, mixed[:, :HD] / mixed[:, HD:], 0.0).astype(jnp.bfloat16)
        for h in range(per_group):
            store(s, slots, h, out[h * capacity : (h + 1) * capacity, :])


def lead_kernel(instances, capacity, per_group, me_ref, *rest):
    got, rest = rest[:instances], rest[instances:]
    blocks_of, rest = rest[:instances], rest[instances:]
    half_ref, allowed_ref, keys_ref, vals_ref, kc_ref, vc_ref, wanted_ref, keys, vals = rest
    rows = HD
    tall = per_group * capacity
    me = me_ref[0]
    ones = jnp.ones((rows, HD), jnp.bfloat16)
    for k in range(instances):
        source = jnp.bitwise_xor(me, k)
        wanted_ref[source] = got[k][: tall + 16, :]
        at = pl.ds(pl.multiple_of(source * rows, rows), rows)
        blocks = [blocks_of[k][:, block * HD : (block + 1) * HD] for block in range(4)]
        keys[at, :] = blocks[0]
        keys_ref[at, :] = blocks[1]
        vals[at, :HD] = blocks[2]
        vals_ref[at, :HD] = blocks[3]
        vals[k * rows : (k + 1) * rows, HD:] = ones
        vals_ref[k * rows : (k + 1) * rows, HD:] = ones
    lists = jnp.concatenate([wanted_ref[s, tall : tall + 16, :] for s in range(instances)], axis=0)
    wide = (lists.astype(jnp.float32) == me.astype(jnp.float32)).astype(jnp.float32)
    earlier = jnp.dot(wide.astype(jnp.bfloat16), before(rows), preferred_element_type=jnp.float32)
    r = lax.broadcasted_iota(jnp.int32, (rows, 2 * rows), 0)
    u = lax.broadcasted_iota(jnp.int32, (rows, 2 * rows), 1)
    reach = ((u <= r) | (u >= rows)).astype(jnp.bfloat16)
    for s in range(instances):
        q_at, c_at = 16 * s, 16 * s + 1
        cache_pick = picks(wide[c_at : c_at + 1], earlier[c_at : c_at + 1], capacity)
        query_pick = picks(wide[q_at : q_at + 1], earlier[q_at : q_at + 1], capacity)
        slots = slice(s * capacity, (s + 1) * capacity)
        block = slice(s * rows, (s + 1) * rows)
        for g, (k_ref, v_ref) in enumerate(((keys, vals), (keys_ref, vals_ref))):
            columns = slice(g * HD, (g + 1) * HD)
            pair = jnp.concatenate([k_ref[block, :], v_ref[block, :HD]], axis=1)
            cached = jnp.dot(cache_pick, pair, preferred_element_type=jnp.float32).astype(jnp.bfloat16)
            kc_ref[slots, columns] = cached[:, :HD]
            vc_ref[slots, columns] = cached[:, HD:]
        allowed_ref[slots, :] = jnp.dot(query_pick, reach, preferred_element_type=jnp.float32).astype(
            jnp.bfloat16
        )

    def store(s, slots, h, value):
        half_ref[slots, h * HD : (h + 1) * HD] = value

    attend_head(instances, capacity, per_group, wanted_ref, keys, vals, allowed_ref, store)


def rest_kernel(instances, capacity, per_group, me_ref, *rest):
    got, rest = rest[:instances], rest[instances:]
    half_ref, allowed_ref, keys_ref, vals_ref, att_hbm, wanted_ref, mine_ref, sent = rest
    width = per_group * HD
    early = pltpu.make_async_copy(half_ref, att_hbm.at[:, :width], sent.at[instances])
    early.start()
    tall = per_group * capacity
    for k, piece in zip((0, 1, *SECOND), got):
        start = 0 if k in SECOND else tall + 16
        wanted_ref[jnp.bitwise_xor(me_ref[0], k)] = piece[start : start + tall, :]
    copies = []

    def store(s, slots, h, value):
        mine_ref[slots, h * HD : (h + 1) * HD] = value
        if h == per_group - 1:
            copy = pltpu.make_async_copy(
                mine_ref.at[slots, :], att_hbm.at[slots, width:], sent.at[s]
            )
            copy.start()
            copies.append(copy)

    attend_head(instances, capacity, per_group, wanted_ref, keys_ref, vals_ref, allowed_ref, store)
    for copy in [early, *copies]:
        copy.wait()


def few_instances(queries, keys, values, query_owner, cache_owner):
    instances = lax.axis_size("seq")
    rows = queries.shape[0]
    capacity = 3 * rows // (2 * instances)
    heads = queries.shape[1] // HD
    per_group = heads // 2
    tall = per_group * capacity
    slots = instances * capacity

    def swap(array, k):
        return lax.ppermute(array, "seq", [(i, i ^ k) for i in range(instances)])

    vmem = pl.BlockSpec(memory_space=pltpu.VMEM)
    smem = pl.BlockSpec(memory_space=pltpu.SMEM)
    hbm = pl.BlockSpec(memory_space=pltpu.HBM)
    shape = lambda *dims: jax.ShapeDtypeStruct(dims, jnp.bfloat16)
    me = lax.axis_index("seq").astype(jnp.int32).reshape(1)
    own_kv = jnp.concatenate([keys, values], axis=1)
    far_kv, near_kv = swap(own_kv, 2), swap(own_kv, 1)
    both_kv = swap(far_kv, 1)
    distances = (*range(instances), *SECOND)
    sends = pl.pallas_call(
        functools.partial(pack_kernel, instances, capacity),
        out_shape=tuple(
            shape(tall + 16 + tall * (k not in SECOND), HD) for k in range(instances)
        )
        + (shape(tall, HD),) * len(SECOND),
        in_specs=[smem, hbm, vmem, vmem],
        out_specs=(vmem,) * len(distances),
        scratch_shapes=[pltpu.VMEM(queries.shape, jnp.bfloat16), pltpu.SemaphoreType.DMA],
        compiler_params=pltpu.CompilerParams(vmem_limit_bytes=16 << 20),
        cost_estimate=pl.CostEstimate(flops=1 << 27, bytes_accessed=2 << 20, transcendentals=0),
        name="pack",
    )(me, queries, query_owner.reshape(1, rows), cache_owner.reshape(1, rows))
    anyspace = pl.BlockSpec(memory_space=pl.ANY)
    opposite = pl.pallas_call(
        gate_kernel,
        out_shape=shape(*sends[2].shape),
        in_specs=[anyspace] * 2,
        out_specs=anyspace,
        input_output_aliases={1: 0},
        compiler_params=pltpu.CompilerParams(vmem_limit_bytes=16 << 20),
        cost_estimate=pl.CostEstimate(flops=0, bytes_accessed=0, transcendentals=0),
        name="gate",
    )(near_kv, sends[2])
    sends = [*sends[:2], opposite, *sends[3:]]
    got = [swap(piece, k) if k else piece for k, piece in zip(distances, sends)]
    half, allowed, keys_rest, vals_rest, key_cache, value_cache = pl.pallas_call(
        functools.partial(lead_kernel, instances, capacity, per_group),
        out_shape=(
            shape(slots, per_group * HD),
            shape(slots, 2 * rows),
            shape(instances * rows, HD),
            shape(instances * rows, 2 * HD),
            shape(slots, 2 * HD),
            shape(slots, 2 * HD),
        ),
        in_specs=[smem] + [vmem] * (2 * instances),
        out_specs=(vmem,) * 6,
        scratch_shapes=[
            pltpu.VMEM((instances, tall + 16, HD), jnp.bfloat16),
            pltpu.VMEM((instances * rows, HD), jnp.bfloat16),
            pltpu.VMEM((instances * rows, 2 * HD), jnp.bfloat16),
        ],
        compiler_params=pltpu.CompilerParams(vmem_limit_bytes=24 << 20),
        cost_estimate=pl.CostEstimate(flops=1 << 29, bytes_accessed=2 << 20, transcendentals=1 << 19),
        name="attend_lead",
    )(me, *got[:instances], own_kv, near_kv, far_kv, both_kv)
    attended = pl.pallas_call(
        functools.partial(rest_kernel, instances, capacity, per_group),
        out_shape=shape(slots, heads * HD),
        in_specs=[smem] + [vmem] * (instances + 4),
        out_specs=hbm,
        scratch_shapes=[
            pltpu.VMEM((instances, tall, HD), jnp.bfloat16),
            pltpu.VMEM((slots, per_group * HD), jnp.bfloat16),
            pltpu.SemaphoreType.DMA((instances + 1,)),
        ],
        compiler_params=pltpu.CompilerParams(vmem_limit_bytes=24 << 20),
        cost_estimate=pl.CostEstimate(flops=1 << 29, bytes_accessed=2 << 20, transcendentals=1 << 19),
        name="attend_rest",
    )(me, *got[:2], *got[instances:], half, allowed, keys_rest, vals_rest)
    return (attended, key_cache, value_cache)


def on_device(queries, keys, values, query_owner, cache_owner):
    instances = lax.axis_size("seq")
    rows = queries.shape[0]
    capacity = 3 * rows // (2 * instances)
    heads = queries.shape[1] // HD
    whole_tiles = (
        instances == 4
        and capacity % 16 == 0
        and rows == HD
        and keys.shape[1] == 2 * HD
        and heads % 4 == 0
    )
    form = few_instances if whole_tiles else many_instances
    return form(queries, keys, values, query_owner, cache_owner)


def solution(mesh):
    return jax.shard_map(
        on_device,
        mesh=mesh,
        in_specs=(
            P(("groups", "seq"), ("tp", "rep")),
            P(("groups", "seq"), ("tp", "rep")),
            P(("groups", "seq"), ("tp", "rep")),
            P(("groups", "seq"), None),
            P(("groups", "seq"), None),
        ),
        out_specs=(
            P(("groups", "seq"), ("tp", "rep")),
            P(("groups", "seq"), ("tp", "rep")),
            P(("groups", "seq"), ("tp", "rep")),
        ),
        check_vma=False,
    )
```

```python
import functools
import math

import jax
import jax.numpy as jnp
from jax import lax
from jax.experimental import pallas as pl
from jax.experimental.pallas import tpu as pltpu
from jax.sharding import PartitionSpec as P

HD = 128


neg_big = -1e30
SECOND = (2, 3)


def slot_select(owner_list, instances, capacity):
    owners = owner_list[:, 0]
    onehot = (owners[:, None] == jnp.arange(instances, dtype=jnp.int32)[None, :]).astype(jnp.int32)
    earlier = jnp.cumsum(onehot, axis=0) - onehot
    ranking = jnp.sum(earlier * onehot, axis=1)
    target = owners * capacity + ranking
    return target[None, :] == jnp.arange(instances * capacity, dtype=jnp.int32)[:, None]


def pack_rows(select, table_rows, instances):
    selected = jnp.dot(
        select.astype(table_rows.dtype), table_rows, preferred_element_type=jnp.float32
    )
    return selected.astype(table_rows.dtype).reshape(instances, -1, table_rows.shape[1])


def start_state(heads_kv, per_group, slot_count):
    running_max = jnp.full((heads_kv, per_group, slot_count), neg_big, jnp.float32)
    running_sum = jnp.zeros((heads_kv, per_group, slot_count), jnp.float32)
    weighted = jnp.zeros((heads_kv, per_group, slot_count, HD), jnp.float32)
    return (running_max, running_sum, weighted)


def key_block(current, grouped, query_pos, key_piece, value_piece, key_start):
    running_max, running_sum, weighted = current
    key_count = key_piece.shape[0]
    heads_kv = grouped.shape[1]
    key_heads = key_piece.reshape(key_count, heads_kv, HD)
    value_heads = value_piece.reshape(key_count, heads_kv, HD)
    scores = jnp.einsum("rkgd,nkd->kgrn", grouped, key_heads, preferred_element_type=jnp.float32)
    scores = scores * (1.0 / math.sqrt(HD))
    key_pos = key_start + jnp.arange(key_count, dtype=jnp.int32)
    allowed = key_pos[None, :] <= query_pos[:, None]
    scores = jnp.where(allowed, scores, neg_big)
    new_max = jnp.maximum(running_max, jnp.max(scores, axis=-1))
    weights = jnp.where(allowed, jnp.exp(scores - new_max[..., None]), 0.0).astype(jnp.bfloat16)
    rescale = jnp.exp(running_max - new_max)
    running_sum = running_sum * rescale + jnp.sum(weights, axis=-1, dtype=jnp.float32)
    weighted = weighted * rescale[..., None] + jnp.einsum(
        "kgrn,nkd->kgrd", weights, value_heads, preferred_element_type=jnp.float32
    )
    return (new_max, running_sum, weighted)


def folder(grouped, query_pos, current, pieces):
    last_pos = jnp.max(query_pos)
    key_part, value_part = pieces
    key_count = key_part.shape[0]
    block_rows = math.gcd(512, key_count)
    block_count = key_count // block_rows
    key_blocks = key_part.reshape(block_count, block_rows, key_part.shape[1])
    value_blocks = value_part.reshape(block_count, block_rows, value_part.shape[1])

    def visit(carried, block_item):
        block_index, key_piece, value_piece = block_item
        key_start = block_index * block_rows
        updated = lax.cond(
            key_start <= last_pos,
            lambda inner: key_block(inner, grouped, query_pos, key_piece, value_piece, key_start),
            lambda inner: inner,
            carried,
        )
        return (updated, None)

    current, _ = lax.scan(
        visit, current, (jnp.arange(block_count, dtype=jnp.int32), key_blocks, value_blocks)
    )
    return current


def finish(current, slot_count):
    running_max, running_sum, weighted = current
    denominator = jnp.where(running_sum > 0.0, running_sum, 1.0)
    averaged = weighted / denominator[..., None]
    return jnp.transpose(averaged, (2, 0, 1, 3)).reshape(slot_count, -1).astype(jnp.bfloat16)


def many_instances(queries, keys, values, query_owner, cache_owner):
    instances = lax.axis_size("seq")
    own_index = lax.axis_index("seq")
    local_rows = queries.shape[0]
    capacity = 3 * local_rows // (2 * instances)
    slot_count = instances * capacity
    heads_kv = keys.shape[1] // HD
    per_group = queries.shape[1] // keys.shape[1]
    positions = own_index * local_rows + jnp.arange(local_rows, dtype=jnp.int32)
    cache_pick = slot_select(cache_owner, instances, capacity)
    key_slots = pack_rows(cache_pick, keys, instances)
    value_slots = pack_rows(cache_pick, values, instances)
    query_pick = slot_select(query_owner, instances, capacity)
    query_slots = pack_rows(query_pick, queries, instances)
    slot_pos = jnp.max(jnp.where(query_pick, positions[None, :], -1), axis=1).reshape(
        instances, capacity
    )
    query_got, pos_got, key_got, value_got = (
        lax.all_to_all(query_slots, "seq", split_axis=0, concat_axis=0, tiled=True),
        lax.all_to_all(slot_pos, "seq", split_axis=0, concat_axis=0, tiled=True),
        lax.all_to_all(key_slots, "seq", split_axis=0, concat_axis=0, tiled=True),
        lax.all_to_all(value_slots, "seq", split_axis=0, concat_axis=0, tiled=True),
    )
    arrived = query_got.reshape(slot_count, -1)
    arrived_pos = pos_got.reshape(slot_count)
    grouped = arrived.reshape(slot_count, heads_kv, per_group, HD)
    final_state = folder(
        grouped,
        arrived_pos,
        start_state(heads_kv, per_group, slot_count),
        (
            lax.all_gather(keys, "seq", axis=0, tiled=True),
            lax.all_gather(values, "seq", axis=0, tiled=True),
        ),
    )
    attended = finish(final_state, slot_count)
    key_cache = key_got.reshape(slot_count, -1)
    value_cache = value_got.reshape(slot_count, -1)
    return (attended, key_cache, value_cache)


def before(rows):
    r = lax.broadcasted_iota(jnp.int32, (rows, rows), 0)
    u = lax.broadcasted_iota(jnp.int32, (rows, rows), 1)
    return (r < u).astype(jnp.bfloat16)


def picks(marks, earlier, capacity):
    rows = marks.shape[1]
    slot = lax.broadcasted_iota(jnp.int32, (capacity, rows), 0).astype(jnp.float32)
    chosen = jnp.where(marks > 0.5, earlier, -1.0)
    return (chosen == slot).astype(jnp.bfloat16)


def lead_heads(heads):
    return heads // 2 + 3 * heads // 16


def gate_kernel(near_ref, far_ref, through_ref):
    pass


def pack_kernel(instances, capacity, me_ref, q_hbm, qo_ref, co_ref, *rest):
    lead, rest = rest[:instances], rest[instances:]
    second, (q_ref, arrived) = dict(zip(SECOND, rest)), rest[len(SECOND) :]
    rows = q_ref.shape[0]
    heads = q_ref.shape[1] // HD
    fetch = pltpu.make_async_copy(q_hbm, q_ref, arrived)
    fetch.start()
    me = me_ref[0]
    owners = qo_ref[...]
    lane = lax.broadcasted_iota(jnp.int32, (16, rows), 0)
    dest = jnp.bitwise_xor(lane, me)
    marks = (jnp.broadcast_to(owners, (16, rows)) == dest).astype(jnp.bfloat16)
    earlier = jnp.dot(marks, before(rows), preferred_element_type=jnp.float32)
    wide = marks.astype(jnp.float32)
    select = jnp.concatenate(
        [picks(wide[k : k + 1], earlier[k : k + 1], capacity) for k in range(instances)], axis=0
    )
    lists = jnp.concatenate(
        [owners, co_ref[...], jnp.full((14, rows), -1, jnp.int32)], axis=0
    ).astype(jnp.float32).astype(jnp.bfloat16)
    first = lead_heads(heads)
    tall = first * capacity
    for k in range(instances):
        lead[k][tall : tall + 16, :] = lists
    fetch.wait()
    for pair in range(heads // 2):
        packed = jnp.dot(
            select,
            q_ref[:, pair * 2 * HD : (pair + 1) * 2 * HD],
            preferred_element_type=jnp.float32,
        ).astype(jnp.bfloat16)
        for k in range(instances):
            for half in range(2):
                h = 2 * pair + half
                ref, at = lead[k], h * capacity
                if h >= first:
                    ref, at = (second[k], at - tall) if k in second else (ref, at + 16)
                ref[at : at + capacity, :] = packed[
                    k * capacity : (k + 1) * capacity, half * HD : (half + 1) * HD
                ]


def attend_head(instances, capacity, span, wanted_ref, keys, vals, allowed_ref, store):
    rows = HD
    count = span.stop - span.start
    scale = math.log2(math.e) / math.sqrt(HD)
    for s in reversed(range(instances)):
        slots = slice(s * capacity, (s + 1) * capacity)
        allowed = allowed_ref[slots, :].astype(jnp.float32)
        near = jnp.concatenate([allowed[:, :rows]] * count, axis=0) > 0.5
        valid = jnp.concatenate([allowed[:, rows:]] * count, axis=0) > 0.5
        scores = lax.dot_general(
            wanted_ref[s, span.start * capacity : span.stop * capacity, :],
            keys[: (s + 1) * rows, :],
            (((1,), (1,)), ((), ())),
            preferred_element_type=jnp.float32,
        )
        last = jnp.where(near, scores[:, s * rows :], neg_big)
        scores = jnp.concatenate([scores[:, : s * rows], last], axis=1) if s else last
        top = jnp.max(scores, axis=1, keepdims=True)
        weights = jnp.exp2(scores * scale - top * scale).astype(jnp.bfloat16)
        mixed = jnp.dot(weights, vals[: (s + 1) * rows, :], preferred_element_type=jnp.float32)
        out = jnp.where(valid, mixed[:, :HD] / mixed[:, HD:], 0.0).astype(jnp.bfloat16)
        for h in range(count):
            store(s, slots, span.start + h, out[h * capacity : (h + 1) * capacity, :])


def lead_kernel(instances, capacity, heads, me_ref, *rest):
    got, rest = rest[:instances], rest[instances:]
    blocks_of, rest = rest[:instances], rest[instances:]
    half_ref, allowed_ref, keys_ref, vals_ref, kc_ref, vc_ref, wanted_ref, keys, vals = rest
    rows = HD
    tall = lead_heads(heads) * capacity
    me = me_ref[0]
    ones = jnp.ones((rows, HD), jnp.bfloat16)
    for k in range(instances):
        source = jnp.bitwise_xor(me, k)
        wanted_ref[source] = got[k][: tall + 16, :]
        at = pl.ds(pl.multiple_of(source * rows, rows), rows)
        blocks = [blocks_of[k][:, block * HD : (block + 1) * HD] for block in range(4)]
        keys[at, :] = blocks[0]
        keys_ref[at, :] = blocks[1]
        vals[at, :HD] = blocks[2]
        vals_ref[at, :HD] = blocks[3]
        vals[k * rows : (k + 1) * rows, HD:] = ones
        vals_ref[k * rows : (k + 1) * rows, HD:] = ones
    lists = jnp.concatenate([wanted_ref[s, tall : tall + 16, :] for s in range(instances)], axis=0)
    wide = (lists.astype(jnp.float32) == me.astype(jnp.float32)).astype(jnp.float32)
    earlier = jnp.dot(wide.astype(jnp.bfloat16), before(rows), preferred_element_type=jnp.float32)
    r = lax.broadcasted_iota(jnp.int32, (rows, 2 * rows), 0)
    u = lax.broadcasted_iota(jnp.int32, (rows, 2 * rows), 1)
    reach = ((u <= r) | (u >= rows)).astype(jnp.bfloat16)
    for s in range(instances):
        q_at, c_at = 16 * s, 16 * s + 1
        cache_pick = picks(wide[c_at : c_at + 1], earlier[c_at : c_at + 1], capacity)
        query_pick = picks(wide[q_at : q_at + 1], earlier[q_at : q_at + 1], capacity)
        slots = slice(s * capacity, (s + 1) * capacity)
        block = slice(s * rows, (s + 1) * rows)
        for g, (k_ref, v_ref) in enumerate(((keys, vals), (keys_ref, vals_ref))):
            columns = slice(g * HD, (g + 1) * HD)
            pair = jnp.concatenate([k_ref[block, :], v_ref[block, :HD]], axis=1)
            cached = jnp.dot(cache_pick, pair, preferred_element_type=jnp.float32).astype(jnp.bfloat16)
            kc_ref[slots, columns] = cached[:, :HD]
            vc_ref[slots, columns] = cached[:, HD:]
        allowed_ref[slots, :] = jnp.dot(query_pick, reach, preferred_element_type=jnp.float32).astype(
            jnp.bfloat16
        )

    def store(s, slots, h, value):
        half_ref[slots, h * HD : (h + 1) * HD] = value

    halves = (slice(0, heads // 2), keys, vals), (slice(heads // 2, lead_heads(heads)), keys_ref, vals_ref)
    for span, k_ref, v_ref in halves:
        attend_head(instances, capacity, span, wanted_ref, k_ref, v_ref, allowed_ref, store)


def rest_kernel(instances, capacity, heads, me_ref, *rest):
    got, rest = rest[:instances], rest[instances:]
    half_ref, allowed_ref, keys_ref, vals_ref, att_hbm, wanted_ref, mine_ref, sent = rest
    first = lead_heads(heads)
    count = heads - first
    early = pltpu.make_async_copy(half_ref, att_hbm.at[:, : first * HD], sent.at[instances])
    early.start()
    for k, piece in zip((0, 1, *SECOND), got):
        start = 0 if k in SECOND else first * capacity + 16
        wanted_ref[jnp.bitwise_xor(me_ref[0], k)] = piece[start : start + count * capacity, :]
    copies = []

    def store(s, slots, h, value):
        mine_ref[slots, h * HD : (h + 1) * HD] = value
        if h == count - 1:
            copy = pltpu.make_async_copy(
                mine_ref.at[slots, :], att_hbm.at[slots, first * HD :], sent.at[s]
            )
            copy.start()
            copies.append(copy)

    attend_head(
        instances, capacity, slice(0, count), wanted_ref, keys_ref, vals_ref, allowed_ref, store
    )
    for copy in [early, *copies]:
        copy.wait()


def few_instances(queries, keys, values, query_owner, cache_owner):
    instances = lax.axis_size("seq")
    rows = queries.shape[0]
    capacity = 3 * rows // (2 * instances)
    heads = queries.shape[1] // HD
    first = lead_heads(heads)
    tall, short = first * capacity, (heads - first) * capacity
    slots = instances * capacity

    def swap(array, k):
        return lax.ppermute(array, "seq", [(i, i ^ k) for i in range(instances)])

    vmem = pl.BlockSpec(memory_space=pltpu.VMEM)
    smem = pl.BlockSpec(memory_space=pltpu.SMEM)
    hbm = pl.BlockSpec(memory_space=pltpu.HBM)
    shape = lambda *dims: jax.ShapeDtypeStruct(dims, jnp.bfloat16)
    me = lax.axis_index("seq").astype(jnp.int32).reshape(1)
    own_kv = jnp.concatenate([keys, values], axis=1)
    far_kv, near_kv = swap(own_kv, 2), swap(own_kv, 1)
    distances = (*range(instances), *SECOND)
    sends = pl.pallas_call(
        functools.partial(pack_kernel, instances, capacity),
        out_shape=tuple(
            shape(tall + 16 + short * (k not in SECOND), HD) for k in range(instances)
        )
        + (shape(short, HD),) * len(SECOND),
        in_specs=[smem, hbm, vmem, vmem],
        out_specs=(vmem,) * len(distances),
        scratch_shapes=[pltpu.VMEM(queries.shape, jnp.bfloat16), pltpu.SemaphoreType.DMA],
        compiler_params=pltpu.CompilerParams(vmem_limit_bytes=16 << 20),
        cost_estimate=pl.CostEstimate(flops=1 << 27, bytes_accessed=2 << 20, transcendentals=0),
        name="pack",
    )(me, queries, query_owner.reshape(1, rows), cache_owner.reshape(1, rows))
    anyspace = pl.BlockSpec(memory_space=pl.ANY)
    passed_kv = pl.pallas_call(
        gate_kernel,
        out_shape=shape(*far_kv.shape),
        in_specs=[anyspace] * 2,
        out_specs=anyspace,
        input_output_aliases={1: 0},
        compiler_params=pltpu.CompilerParams(vmem_limit_bytes=16 << 20),
        cost_estimate=pl.CostEstimate(flops=0, bytes_accessed=0, transcendentals=0),
        name="gate",
    )(near_kv, far_kv)
    both_kv = swap(passed_kv, 1)
    got = [swap(piece, k) if k else piece for k, piece in zip(distances, sends)]
    half, allowed, keys_rest, vals_rest, key_cache, value_cache = pl.pallas_call(
        functools.partial(lead_kernel, instances, capacity, heads),
        out_shape=(
            shape(slots, first * HD),
            shape(slots, 2 * rows),
            shape(instances * rows, HD),
            shape(instances * rows, 2 * HD),
            shape(slots, 2 * HD),
            shape(slots, 2 * HD),
        ),
        in_specs=[smem] + [vmem] * (2 * instances),
        out_specs=(vmem,) * 6,
        scratch_shapes=[
            pltpu.VMEM((instances, tall + 16, HD), jnp.bfloat16),
            pltpu.VMEM((instances * rows, HD), jnp.bfloat16),
            pltpu.VMEM((instances * rows, 2 * HD), jnp.bfloat16),
        ],
        compiler_params=pltpu.CompilerParams(vmem_limit_bytes=24 << 20),
        cost_estimate=pl.CostEstimate(flops=1 << 29, bytes_accessed=2 << 20, transcendentals=1 << 19),
        name="attend_lead",
    )(me, *got[:instances], own_kv, near_kv, passed_kv, both_kv)
    attended = pl.pallas_call(
        functools.partial(rest_kernel, instances, capacity, heads),
        out_shape=shape(slots, heads * HD),
        in_specs=[smem] + [vmem] * (instances + 4),
        out_specs=hbm,
        scratch_shapes=[
            pltpu.VMEM((instances, short, HD), jnp.bfloat16),
            pltpu.VMEM((slots, (heads - first) * HD), jnp.bfloat16),
            pltpu.SemaphoreType.DMA((instances + 1,)),
        ],
        compiler_params=pltpu.CompilerParams(vmem_limit_bytes=24 << 20),
        cost_estimate=pl.CostEstimate(flops=1 << 29, bytes_accessed=2 << 20, transcendentals=1 << 19),
        name="attend_rest",
    )(me, *got[:2], *got[instances:], half, allowed, keys_rest, vals_rest)
    return (attended, key_cache, value_cache)


def on_device(queries, keys, values, query_owner, cache_owner):
    instances = lax.axis_size("seq")
    rows = queries.shape[0]
    capacity = 3 * rows // (2 * instances)
    heads = queries.shape[1] // HD
    whole_tiles = (
        instances == 4
        and capacity % 16 == 0
        and rows == HD
        and keys.shape[1] == 2 * HD
        and heads % 16 == 0
    )
    form = few_instances if whole_tiles else many_instances
    return form(queries, keys, values, query_owner, cache_owner)


def solution(mesh):
    return jax.shard_map(
        on_device,
        mesh=mesh,
        in_specs=(
            P(("groups", "seq"), ("tp", "rep")),
            P(("groups", "seq"), ("tp", "rep")),
            P(("groups", "seq"), ("tp", "rep")),
            P(("groups", "seq"), None),
            P(("groups", "seq"), None),
        ),
        out_specs=(
            P(("groups", "seq"), ("tp", "rep")),
            P(("groups", "seq"), ("tp", "rep")),
            P(("groups", "seq"), ("tp", "rep")),
        ),
        check_vma=False,
    )
```

```python
import functools
import math

import jax
import jax.numpy as jnp
from jax import lax
from jax.experimental import pallas as pl
from jax.experimental.pallas import tpu as pltpu
from jax.sharding import PartitionSpec as P

HD = 128


neg_big = -1e30
SECOND = (2, 3)


def slot_select(owner_list, instances, capacity):
    owners = owner_list[:, 0]
    onehot = (owners[:, None] == jnp.arange(instances, dtype=jnp.int32)[None, :]).astype(jnp.int32)
    earlier = jnp.cumsum(onehot, axis=0) - onehot
    ranking = jnp.sum(earlier * onehot, axis=1)
    target = owners * capacity + ranking
    return target[None, :] == jnp.arange(instances * capacity, dtype=jnp.int32)[:, None]


def pack_rows(select, table_rows, instances):
    selected = jnp.dot(
        select.astype(table_rows.dtype), table_rows, preferred_element_type=jnp.float32
    )
    return selected.astype(table_rows.dtype).reshape(instances, -1, table_rows.shape[1])


def start_state(heads_kv, per_group, slot_count):
    running_max = jnp.full((heads_kv, per_group, slot_count), neg_big, jnp.float32)
    running_sum = jnp.zeros((heads_kv, per_group, slot_count), jnp.float32)
    weighted = jnp.zeros((heads_kv, per_group, slot_count, HD), jnp.float32)
    return (running_max, running_sum, weighted)


def key_block(current, grouped, query_pos, key_piece, value_piece, key_start):
    running_max, running_sum, weighted = current
    key_count = key_piece.shape[0]
    heads_kv = grouped.shape[1]
    key_heads = key_piece.reshape(key_count, heads_kv, HD)
    value_heads = value_piece.reshape(key_count, heads_kv, HD)
    scores = jnp.einsum("rkgd,nkd->kgrn", grouped, key_heads, preferred_element_type=jnp.float32)
    scores = scores * (1.0 / math.sqrt(HD))
    key_pos = key_start + jnp.arange(key_count, dtype=jnp.int32)
    allowed = key_pos[None, :] <= query_pos[:, None]
    scores = jnp.where(allowed, scores, neg_big)
    new_max = jnp.maximum(running_max, jnp.max(scores, axis=-1))
    weights = jnp.where(allowed, jnp.exp(scores - new_max[..., None]), 0.0).astype(jnp.bfloat16)
    rescale = jnp.exp(running_max - new_max)
    running_sum = running_sum * rescale + jnp.sum(weights, axis=-1, dtype=jnp.float32)
    weighted = weighted * rescale[..., None] + jnp.einsum(
        "kgrn,nkd->kgrd", weights, value_heads, preferred_element_type=jnp.float32
    )
    return (new_max, running_sum, weighted)


def folder(grouped, query_pos, current, pieces):
    last_pos = jnp.max(query_pos)
    key_part, value_part = pieces
    key_count = key_part.shape[0]
    block_rows = math.gcd(512, key_count)
    block_count = key_count // block_rows
    key_blocks = key_part.reshape(block_count, block_rows, key_part.shape[1])
    value_blocks = value_part.reshape(block_count, block_rows, value_part.shape[1])

    def visit(carried, block_item):
        block_index, key_piece, value_piece = block_item
        key_start = block_index * block_rows
        updated = lax.cond(
            key_start <= last_pos,
            lambda inner: key_block(inner, grouped, query_pos, key_piece, value_piece, key_start),
            lambda inner: inner,
            carried,
        )
        return (updated, None)

    current, _ = lax.scan(
        visit, current, (jnp.arange(block_count, dtype=jnp.int32), key_blocks, value_blocks)
    )
    return current


def finish(current, slot_count):
    running_max, running_sum, weighted = current
    denominator = jnp.where(running_sum > 0.0, running_sum, 1.0)
    averaged = weighted / denominator[..., None]
    return jnp.transpose(averaged, (2, 0, 1, 3)).reshape(slot_count, -1).astype(jnp.bfloat16)


def many_instances(queries, keys, values, query_owner, cache_owner):
    instances = lax.axis_size("seq")
    own_index = lax.axis_index("seq")
    local_rows = queries.shape[0]
    capacity = 3 * local_rows // (2 * instances)
    slot_count = instances * capacity
    heads_kv = keys.shape[1] // HD
    per_group = queries.shape[1] // keys.shape[1]
    positions = own_index * local_rows + jnp.arange(local_rows, dtype=jnp.int32)
    cache_pick = slot_select(cache_owner, instances, capacity)
    key_slots = pack_rows(cache_pick, keys, instances)
    value_slots = pack_rows(cache_pick, values, instances)
    query_pick = slot_select(query_owner, instances, capacity)
    query_slots = pack_rows(query_pick, queries, instances)
    slot_pos = jnp.max(jnp.where(query_pick, positions[None, :], -1), axis=1).reshape(
        instances, capacity
    )
    query_got, pos_got, key_got, value_got = (
        lax.all_to_all(query_slots, "seq", split_axis=0, concat_axis=0, tiled=True),
        lax.all_to_all(slot_pos, "seq", split_axis=0, concat_axis=0, tiled=True),
        lax.all_to_all(key_slots, "seq", split_axis=0, concat_axis=0, tiled=True),
        lax.all_to_all(value_slots, "seq", split_axis=0, concat_axis=0, tiled=True),
    )
    arrived = query_got.reshape(slot_count, -1)
    arrived_pos = pos_got.reshape(slot_count)
    grouped = arrived.reshape(slot_count, heads_kv, per_group, HD)
    final_state = folder(
        grouped,
        arrived_pos,
        start_state(heads_kv, per_group, slot_count),
        (
            lax.all_gather(keys, "seq", axis=0, tiled=True),
            lax.all_gather(values, "seq", axis=0, tiled=True),
        ),
    )
    attended = finish(final_state, slot_count)
    key_cache = key_got.reshape(slot_count, -1)
    value_cache = value_got.reshape(slot_count, -1)
    return (attended, key_cache, value_cache)


def before(rows):
    r = lax.broadcasted_iota(jnp.int32, (rows, rows), 0)
    u = lax.broadcasted_iota(jnp.int32, (rows, rows), 1)
    return (r < u).astype(jnp.bfloat16)


def picks(marks, earlier, capacity):
    rows = marks.shape[1]
    slot = lax.broadcasted_iota(jnp.int32, (capacity, rows), 0).astype(jnp.float32)
    chosen = jnp.where(marks > 0.5, earlier, -1.0)
    return (chosen == slot).astype(jnp.bfloat16)


def lead_heads(heads):
    return heads // 2 + 5 * heads // 16


def gate_kernel(near_ref, far_ref, through_ref):
    pass


def pack_kernel(instances, capacity, me_ref, q_hbm, qo_ref, co_ref, *rest):
    lead, rest = rest[:instances], rest[instances:]
    second, (q_ref, arrived) = dict(zip(SECOND, rest)), rest[len(SECOND) :]
    rows = q_ref.shape[0]
    heads = q_ref.shape[1] // HD
    fetch = pltpu.make_async_copy(q_hbm, q_ref, arrived)
    fetch.start()
    me = me_ref[0]
    owners = qo_ref[...]
    lane = lax.broadcasted_iota(jnp.int32, (16, rows), 0)
    dest = jnp.bitwise_xor(lane, me)
    marks = (jnp.broadcast_to(owners, (16, rows)) == dest).astype(jnp.bfloat16)
    earlier = jnp.dot(marks, before(rows), preferred_element_type=jnp.float32)
    wide = marks.astype(jnp.float32)
    select = jnp.concatenate(
        [picks(wide[k : k + 1], earlier[k : k + 1], capacity) for k in range(instances)], axis=0
    )
    lists = jnp.concatenate(
        [owners, co_ref[...], jnp.full((14, rows), -1, jnp.int32)], axis=0
    ).astype(jnp.float32).astype(jnp.bfloat16)
    first = lead_heads(heads)
    tall = first * capacity
    for k in range(instances):
        lead[k][tall : tall + 16, :] = lists
    fetch.wait()
    for pair in range(heads // 2):
        packed = jnp.dot(
            select,
            q_ref[:, pair * 2 * HD : (pair + 1) * 2 * HD],
            preferred_element_type=jnp.float32,
        ).astype(jnp.bfloat16)
        for k in range(instances):
            for half in range(2):
                h = 2 * pair + half
                ref, at = lead[k], h * capacity
                if h >= first:
                    ref, at = (second[k], at - tall) if k in second else (ref, at + 16)
                ref[at : at + capacity, :] = packed[
                    k * capacity : (k + 1) * capacity, half * HD : (half + 1) * HD
                ]


def attend_head(instances, capacity, span, wanted_ref, keys, vals, allowed_ref, store):
    rows = HD
    count = span.stop - span.start
    scale = math.log2(math.e) / math.sqrt(HD)
    for s in reversed(range(instances)):
        slots = slice(s * capacity, (s + 1) * capacity)
        allowed = allowed_ref[slots, :].astype(jnp.float32)
        near = jnp.concatenate([allowed[:, :rows]] * count, axis=0) > 0.5
        valid = jnp.concatenate([allowed[:, rows:]] * count, axis=0) > 0.5
        scores = lax.dot_general(
            wanted_ref[s, span.start * capacity : span.stop * capacity, :],
            keys[: (s + 1) * rows, :],
            (((1,), (1,)), ((), ())),
            preferred_element_type=jnp.float32,
        )
        last = jnp.where(near, scores[:, s * rows :], neg_big)
        scores = jnp.concatenate([scores[:, : s * rows], last], axis=1) if s else last
        top = jnp.max(scores, axis=1, keepdims=True)
        weights = jnp.exp2(scores * scale - top * scale).astype(jnp.bfloat16)
        mixed = jnp.dot(weights, vals[: (s + 1) * rows, :], preferred_element_type=jnp.float32)
        out = jnp.where(valid, mixed[:, :HD] / mixed[:, HD:], 0.0).astype(jnp.bfloat16)
        for h in range(count):
            store(s, slots, span.start + h, out[h * capacity : (h + 1) * capacity, :])


def lead_kernel(instances, capacity, heads, me_ref, *rest):
    got, rest = rest[:instances], rest[instances:]
    blocks_of, rest = rest[:instances], rest[instances:]
    half_ref, allowed_ref, keys_ref, vals_ref, kc_ref, vc_ref, wanted_ref, keys, vals = rest
    rows = HD
    tall = lead_heads(heads) * capacity
    me = me_ref[0]
    ones = jnp.ones((rows, HD), jnp.bfloat16)
    for k in range(instances):
        source = jnp.bitwise_xor(me, k)
        wanted_ref[source] = got[k][: tall + 16, :]
        at = pl.ds(pl.multiple_of(source * rows, rows), rows)
        blocks = [blocks_of[k][:, block * HD : (block + 1) * HD] for block in range(4)]
        keys[at, :] = blocks[0]
        keys_ref[at, :] = blocks[1]
        vals[at, :HD] = blocks[2]
        vals_ref[at, :HD] = blocks[3]
        vals[k * rows : (k + 1) * rows, HD:] = ones
        vals_ref[k * rows : (k + 1) * rows, HD:] = ones
    lists = jnp.concatenate([wanted_ref[s, tall : tall + 16, :] for s in range(instances)], axis=0)
    wide = (lists.astype(jnp.float32) == me.astype(jnp.float32)).astype(jnp.float32)
    earlier = jnp.dot(wide.astype(jnp.bfloat16), before(rows), preferred_element_type=jnp.float32)
    r = lax.broadcasted_iota(jnp.int32, (rows, 2 * rows), 0)
    u = lax.broadcasted_iota(jnp.int32, (rows, 2 * rows), 1)
    reach = ((u <= r) | (u >= rows)).astype(jnp.bfloat16)
    for s in range(instances):
        q_at, c_at = 16 * s, 16 * s + 1
        cache_pick = picks(wide[c_at : c_at + 1], earlier[c_at : c_at + 1], capacity)
        query_pick = picks(wide[q_at : q_at + 1], earlier[q_at : q_at + 1], capacity)
        slots = slice(s * capacity, (s + 1) * capacity)
        block = slice(s * rows, (s + 1) * rows)
        for g, (k_ref, v_ref) in enumerate(((keys, vals), (keys_ref, vals_ref))):
            columns = slice(g * HD, (g + 1) * HD)
            pair = jnp.concatenate([k_ref[block, :], v_ref[block, :HD]], axis=1)
            cached = jnp.dot(cache_pick, pair, preferred_element_type=jnp.float32).astype(jnp.bfloat16)
            kc_ref[slots, columns] = cached[:, :HD]
            vc_ref[slots, columns] = cached[:, HD:]
        allowed_ref[slots, :] = jnp.dot(query_pick, reach, preferred_element_type=jnp.float32).astype(
            jnp.bfloat16
        )

    def store(s, slots, h, value):
        half_ref[slots, h * HD : (h + 1) * HD] = value

    halves = (slice(0, heads // 2), keys, vals), (slice(heads // 2, lead_heads(heads)), keys_ref, vals_ref)
    for span, k_ref, v_ref in halves:
        attend_head(instances, capacity, span, wanted_ref, k_ref, v_ref, allowed_ref, store)


def rest_kernel(instances, capacity, heads, me_ref, *rest):
    got, rest = rest[:instances], rest[instances:]
    half_ref, allowed_ref, keys_ref, vals_ref, att_hbm, wanted_ref, mine_ref, sent = rest
    first = lead_heads(heads)
    count = heads - first
    early = pltpu.make_async_copy(half_ref, att_hbm.at[:, : first * HD], sent.at[instances])
    early.start()
    for k, piece in zip((0, 1, *SECOND), got):
        start = 0 if k in SECOND else first * capacity + 16
        wanted_ref[jnp.bitwise_xor(me_ref[0], k)] = piece[start : start + count * capacity, :]
    copies = []

    def store(s, slots, h, value):
        mine_ref[slots, h * HD : (h + 1) * HD] = value
        if h == count - 1:
            copy = pltpu.make_async_copy(
                mine_ref.at[slots, :], att_hbm.at[slots, first * HD :], sent.at[s]
            )
            copy.start()
            copies.append(copy)

    attend_head(
        instances, capacity, slice(0, count), wanted_ref, keys_ref, vals_ref, allowed_ref, store
    )
    for copy in [early, *copies]:
        copy.wait()


def few_instances(queries, keys, values, query_owner, cache_owner):
    instances = lax.axis_size("seq")
    rows = queries.shape[0]
    capacity = 3 * rows // (2 * instances)
    heads = queries.shape[1] // HD
    first = lead_heads(heads)
    tall, short = first * capacity, (heads - first) * capacity
    slots = instances * capacity

    def swap(array, k):
        return lax.ppermute(array, "seq", [(i, i ^ k) for i in range(instances)])

    vmem = pl.BlockSpec(memory_space=pltpu.VMEM)
    smem = pl.BlockSpec(memory_space=pltpu.SMEM)
    hbm = pl.BlockSpec(memory_space=pltpu.HBM)
    shape = lambda *dims: jax.ShapeDtypeStruct(dims, jnp.bfloat16)
    me = lax.axis_index("seq").astype(jnp.int32).reshape(1)
    own_kv = jnp.concatenate([keys, values], axis=1)
    far_kv, near_kv = swap(own_kv, 2), swap(own_kv, 1)
    distances = (*range(instances), *SECOND)
    sends = pl.pallas_call(
        functools.partial(pack_kernel, instances, capacity),
        out_shape=tuple(
            shape(tall + 16 + short * (k not in SECOND), HD) for k in range(instances)
        )
        + (shape(short, HD),) * len(SECOND),
        in_specs=[smem, hbm, vmem, vmem],
        out_specs=(vmem,) * len(distances),
        scratch_shapes=[pltpu.VMEM(queries.shape, jnp.bfloat16), pltpu.SemaphoreType.DMA],
        compiler_params=pltpu.CompilerParams(vmem_limit_bytes=16 << 20),
        cost_estimate=pl.CostEstimate(flops=1 << 27, bytes_accessed=2 << 20, transcendentals=0),
        name="pack",
    )(me, queries, query_owner.reshape(1, rows), cache_owner.reshape(1, rows))
    anyspace = pl.BlockSpec(memory_space=pl.ANY)
    passed_kv = pl.pallas_call(
        gate_kernel,
        out_shape=shape(*far_kv.shape),
        in_specs=[anyspace] * 2,
        out_specs=anyspace,
        input_output_aliases={1: 0},
        compiler_params=pltpu.CompilerParams(vmem_limit_bytes=16 << 20),
        cost_estimate=pl.CostEstimate(flops=0, bytes_accessed=0, transcendentals=0),
        name="gate",
    )(near_kv, far_kv)
    both_kv = swap(passed_kv, 1)
    got = [swap(piece, k) if k else piece for k, piece in zip(distances, sends)]
    half, allowed, keys_rest, vals_rest, key_cache, value_cache = pl.pallas_call(
        functools.partial(lead_kernel, instances, capacity, heads),
        out_shape=(
            shape(slots, first * HD),
            shape(slots, 2 * rows),
            shape(instances * rows, HD),
            shape(instances * rows, 2 * HD),
            shape(slots, 2 * HD),
            shape(slots, 2 * HD),
        ),
        in_specs=[smem] + [vmem] * (2 * instances),
        out_specs=(vmem,) * 6,
        scratch_shapes=[
            pltpu.VMEM((instances, tall + 16, HD), jnp.bfloat16),
            pltpu.VMEM((instances * rows, HD), jnp.bfloat16),
            pltpu.VMEM((instances * rows, 2 * HD), jnp.bfloat16),
        ],
        compiler_params=pltpu.CompilerParams(vmem_limit_bytes=24 << 20),
        cost_estimate=pl.CostEstimate(flops=1 << 29, bytes_accessed=2 << 20, transcendentals=1 << 19),
        name="attend_lead",
    )(me, *got[:instances], own_kv, near_kv, passed_kv, both_kv)
    attended = pl.pallas_call(
        functools.partial(rest_kernel, instances, capacity, heads),
        out_shape=shape(slots, heads * HD),
        in_specs=[smem] + [vmem] * (instances + 4),
        out_specs=hbm,
        scratch_shapes=[
            pltpu.VMEM((instances, short, HD), jnp.bfloat16),
            pltpu.VMEM((slots, (heads - first) * HD), jnp.bfloat16),
            pltpu.SemaphoreType.DMA((instances + 1,)),
        ],
        compiler_params=pltpu.CompilerParams(vmem_limit_bytes=24 << 20),
        cost_estimate=pl.CostEstimate(flops=1 << 29, bytes_accessed=2 << 20, transcendentals=1 << 19),
        name="attend_rest",
    )(me, *got[:2], *got[instances:], half, allowed, keys_rest, vals_rest)
    return (attended, key_cache, value_cache)


def on_device(queries, keys, values, query_owner, cache_owner):
    instances = lax.axis_size("seq")
    rows = queries.shape[0]
    capacity = 3 * rows // (2 * instances)
    heads = queries.shape[1] // HD
    whole_tiles = (
        instances == 4
        and capacity % 16 == 0
        and rows == HD
        and keys.shape[1] == 2 * HD
        and heads % 16 == 0
    )
    form = few_instances if whole_tiles else many_instances
    return form(queries, keys, values, query_owner, cache_owner)


def solution(mesh):
    return jax.shard_map(
        on_device,
        mesh=mesh,
        in_specs=(
            P(("groups", "seq"), ("tp", "rep")),
            P(("groups", "seq"), ("tp", "rep")),
            P(("groups", "seq"), ("tp", "rep")),
            P(("groups", "seq"), None),
            P(("groups", "seq"), None),
        ),
        out_specs=(
            P(("groups", "seq"), ("tp", "rep")),
            P(("groups", "seq"), ("tp", "rep")),
            P(("groups", "seq"), ("tp", "rep")),
        ),
        check_vma=False,
    )
```

```python
import functools
import math

import jax
import jax.numpy as jnp
from jax import lax
from jax.experimental import pallas as pl
from jax.experimental.pallas import tpu as pltpu
from jax.sharding import PartitionSpec as P

HD = 128


neg_big = -1e30
SECOND = (2, 3)


def slot_select(owner_list, instances, capacity):
    owners = owner_list[:, 0]
    onehot = (owners[:, None] == jnp.arange(instances, dtype=jnp.int32)[None, :]).astype(jnp.int32)
    earlier = jnp.cumsum(onehot, axis=0) - onehot
    ranking = jnp.sum(earlier * onehot, axis=1)
    target = owners * capacity + ranking
    return target[None, :] == jnp.arange(instances * capacity, dtype=jnp.int32)[:, None]


def pack_rows(select, table_rows, instances):
    selected = jnp.dot(
        select.astype(table_rows.dtype), table_rows, preferred_element_type=jnp.float32
    )
    return selected.astype(table_rows.dtype).reshape(instances, -1, table_rows.shape[1])


def start_state(heads_kv, per_group, slot_count):
    running_max = jnp.full((heads_kv, per_group, slot_count), neg_big, jnp.float32)
    running_sum = jnp.zeros((heads_kv, per_group, slot_count), jnp.float32)
    weighted = jnp.zeros((heads_kv, per_group, slot_count, HD), jnp.float32)
    return (running_max, running_sum, weighted)


def key_block(current, grouped, query_pos, key_piece, value_piece, key_start):
    running_max, running_sum, weighted = current
    key_count = key_piece.shape[0]
    heads_kv = grouped.shape[1]
    key_heads = key_piece.reshape(key_count, heads_kv, HD)
    value_heads = value_piece.reshape(key_count, heads_kv, HD)
    scores = jnp.einsum("rkgd,nkd->kgrn", grouped, key_heads, preferred_element_type=jnp.float32)
    scores = scores * (1.0 / math.sqrt(HD))
    key_pos = key_start + jnp.arange(key_count, dtype=jnp.int32)
    allowed = key_pos[None, :] <= query_pos[:, None]
    scores = jnp.where(allowed, scores, neg_big)
    new_max = jnp.maximum(running_max, jnp.max(scores, axis=-1))
    weights = jnp.where(allowed, jnp.exp(scores - new_max[..., None]), 0.0).astype(jnp.bfloat16)
    rescale = jnp.exp(running_max - new_max)
    running_sum = running_sum * rescale + jnp.sum(weights, axis=-1, dtype=jnp.float32)
    weighted = weighted * rescale[..., None] + jnp.einsum(
        "kgrn,nkd->kgrd", weights, value_heads, preferred_element_type=jnp.float32
    )
    return (new_max, running_sum, weighted)


def folder(grouped, query_pos, current, pieces):
    last_pos = jnp.max(query_pos)
    key_part, value_part = pieces
    key_count = key_part.shape[0]
    block_rows = math.gcd(512, key_count)
    block_count = key_count // block_rows
    key_blocks = key_part.reshape(block_count, block_rows, key_part.shape[1])
    value_blocks = value_part.reshape(block_count, block_rows, value_part.shape[1])

    def visit(carried, block_item):
        block_index, key_piece, value_piece = block_item
        key_start = block_index * block_rows
        updated = lax.cond(
            key_start <= last_pos,
            lambda inner: key_block(inner, grouped, query_pos, key_piece, value_piece, key_start),
            lambda inner: inner,
            carried,
        )
        return (updated, None)

    current, _ = lax.scan(
        visit, current, (jnp.arange(block_count, dtype=jnp.int32), key_blocks, value_blocks)
    )
    return current


def finish(current, slot_count):
    running_max, running_sum, weighted = current
    denominator = jnp.where(running_sum > 0.0, running_sum, 1.0)
    averaged = weighted / denominator[..., None]
    return jnp.transpose(averaged, (2, 0, 1, 3)).reshape(slot_count, -1).astype(jnp.bfloat16)


def many_instances(queries, keys, values, query_owner, cache_owner):
    instances = lax.axis_size("seq")
    own_index = lax.axis_index("seq")
    local_rows = queries.shape[0]
    capacity = 3 * local_rows // (2 * instances)
    slot_count = instances * capacity
    heads_kv = keys.shape[1] // HD
    per_group = queries.shape[1] // keys.shape[1]
    positions = own_index * local_rows + jnp.arange(local_rows, dtype=jnp.int32)
    cache_pick = slot_select(cache_owner, instances, capacity)
    key_slots = pack_rows(cache_pick, keys, instances)
    value_slots = pack_rows(cache_pick, values, instances)
    query_pick = slot_select(query_owner, instances, capacity)
    query_slots = pack_rows(query_pick, queries, instances)
    slot_pos = jnp.max(jnp.where(query_pick, positions[None, :], -1), axis=1).reshape(
        instances, capacity
    )
    query_got, pos_got, key_got, value_got = (
        lax.all_to_all(query_slots, "seq", split_axis=0, concat_axis=0, tiled=True),
        lax.all_to_all(slot_pos, "seq", split_axis=0, concat_axis=0, tiled=True),
        lax.all_to_all(key_slots, "seq", split_axis=0, concat_axis=0, tiled=True),
        lax.all_to_all(value_slots, "seq", split_axis=0, concat_axis=0, tiled=True),
    )
    arrived = query_got.reshape(slot_count, -1)
    arrived_pos = pos_got.reshape(slot_count)
    grouped = arrived.reshape(slot_count, heads_kv, per_group, HD)
    final_state = folder(
        grouped,
        arrived_pos,
        start_state(heads_kv, per_group, slot_count),
        (
            lax.all_gather(keys, "seq", axis=0, tiled=True),
            lax.all_gather(values, "seq", axis=0, tiled=True),
        ),
    )
    attended = finish(final_state, slot_count)
    key_cache = key_got.reshape(slot_count, -1)
    value_cache = value_got.reshape(slot_count, -1)
    return (attended, key_cache, value_cache)


def before(rows):
    r = lax.broadcasted_iota(jnp.int32, (rows, rows), 0)
    u = lax.broadcasted_iota(jnp.int32, (rows, rows), 1)
    return (r < u).astype(jnp.bfloat16)


def picks(marks, earlier, capacity):
    rows = marks.shape[1]
    slot = lax.broadcasted_iota(jnp.int32, (capacity, rows), 0).astype(jnp.float32)
    chosen = jnp.where(marks > 0.5, earlier, -1.0)
    return (chosen == slot).astype(jnp.bfloat16)


def lead_heads(heads):
    return heads // 2 + 3 * heads // 16


def gate_kernel(near_ref, far_ref, through_ref):
    pass


def pack_kernel(instances, capacity, me_ref, q_hbm, qo_ref, co_ref, *rest):
    lead, rest = rest[:instances], rest[instances:]
    second, (q_ref, arrived) = dict(zip(SECOND, rest)), rest[len(SECOND) :]
    rows = q_ref.shape[0]
    heads = q_ref.shape[1] // HD
    fetch = pltpu.make_async_copy(q_hbm, q_ref, arrived)
    fetch.start()
    me = me_ref[0]
    owners = qo_ref[...]
    lane = lax.broadcasted_iota(jnp.int32, (16, rows), 0)
    dest = jnp.bitwise_xor(lane, me)
    marks = (jnp.broadcast_to(owners, (16, rows)) == dest).astype(jnp.bfloat16)
    earlier = jnp.dot(marks, before(rows), preferred_element_type=jnp.float32)
    wide = marks.astype(jnp.float32)
    select = jnp.concatenate(
        [picks(wide[k : k + 1], earlier[k : k + 1], capacity) for k in range(instances)], axis=0
    )
    lists = jnp.concatenate(
        [owners, co_ref[...], jnp.full((14, rows), -1, jnp.int32)], axis=0
    ).astype(jnp.float32).astype(jnp.bfloat16)
    first = lead_heads(heads)
    tall = first * capacity
    for k in range(instances):
        lead[k][tall : tall + 16, :] = lists
    fetch.wait()
    for pair in range(heads // 2):
        packed = jnp.dot(
            select,
            q_ref[:, pair * 2 * HD : (pair + 1) * 2 * HD],
            preferred_element_type=jnp.float32,
        ).astype(jnp.bfloat16)
        for k in range(instances):
            for half in range(2):
                h = 2 * pair + half
                ref, at = lead[k], h * capacity
                if h >= first:
                    ref, at = (second[k], at - tall) if k in second else (ref, at + 16)
                ref[at : at + capacity, :] = packed[
                    k * capacity : (k + 1) * capacity, half * HD : (half + 1) * HD
                ]


def attend_head(instances, capacity, span, wanted_ref, keys, vals, allowed_ref, store):
    rows = HD
    count = span.stop - span.start
    scale = math.log2(math.e) / math.sqrt(HD)
    for s in reversed(range(instances)):
        slots = slice(s * capacity, (s + 1) * capacity)
        allowed = allowed_ref[slots, :].astype(jnp.float32)
        near = jnp.concatenate([allowed[:, :rows]] * count, axis=0) > 0.5
        valid = jnp.concatenate([allowed[:, rows:]] * count, axis=0) > 0.5
        scores = lax.dot_general(
            wanted_ref[s, span.start * capacity : span.stop * capacity, :],
            keys[: (s + 1) * rows, :],
            (((1,), (1,)), ((), ())),
            preferred_element_type=jnp.float32,
        )
        last = jnp.where(near, scores[:, s * rows :], neg_big)
        scores = jnp.concatenate([scores[:, : s * rows], last], axis=1) if s else last
        top = jnp.max(scores, axis=1, keepdims=True)
        weights = jnp.exp2(scores * scale - top * scale).astype(jnp.bfloat16)
        mixed = jnp.dot(weights, vals[: (s + 1) * rows, :], preferred_element_type=jnp.float32)
        out = jnp.where(valid, mixed[:, :HD] / mixed[:, HD:], 0.0).astype(jnp.bfloat16)
        for h in range(count):
            store(s, slots, span.start + h, out[h * capacity : (h + 1) * capacity, :])


def lead_kernel(instances, capacity, heads, me_ref, *rest):
    got, rest = rest[:instances], rest[instances:]
    blocks_of, rest = rest[:instances], rest[instances:]
    att_hbm, allowed_ref, keys_ref, vals_ref, kc_ref, vc_ref, wanted_ref, keys, vals, half_ref, sent = rest
    rows = HD
    tall = lead_heads(heads) * capacity
    me = me_ref[0]
    ones = jnp.ones((rows, HD), jnp.bfloat16)
    for k in range(instances):
        source = jnp.bitwise_xor(me, k)
        wanted_ref[source] = got[k][: tall + 16, :]
        at = pl.ds(pl.multiple_of(source * rows, rows), rows)
        blocks = [blocks_of[k][:, block * HD : (block + 1) * HD] for block in range(4)]
        keys[at, :] = blocks[0]
        keys_ref[at, :] = blocks[1]
        vals[at, :HD] = blocks[2]
        vals_ref[at, :HD] = blocks[3]
        vals[k * rows : (k + 1) * rows, HD:] = ones
        vals_ref[k * rows : (k + 1) * rows, HD:] = ones
    lists = jnp.concatenate([wanted_ref[s, tall : tall + 16, :] for s in range(instances)], axis=0)
    wide = (lists.astype(jnp.float32) == me.astype(jnp.float32)).astype(jnp.float32)
    earlier = jnp.dot(wide.astype(jnp.bfloat16), before(rows), preferred_element_type=jnp.float32)
    r = lax.broadcasted_iota(jnp.int32, (rows, 2 * rows), 0)
    u = lax.broadcasted_iota(jnp.int32, (rows, 2 * rows), 1)
    reach = ((u <= r) | (u >= rows)).astype(jnp.bfloat16)
    for s in range(instances):
        q_at, c_at = 16 * s, 16 * s + 1
        cache_pick = picks(wide[c_at : c_at + 1], earlier[c_at : c_at + 1], capacity)
        query_pick = picks(wide[q_at : q_at + 1], earlier[q_at : q_at + 1], capacity)
        slots = slice(s * capacity, (s + 1) * capacity)
        block = slice(s * rows, (s + 1) * rows)
        for g, (k_ref, v_ref) in enumerate(((keys, vals), (keys_ref, vals_ref))):
            columns = slice(g * HD, (g + 1) * HD)
            pair = jnp.concatenate([k_ref[block, :], v_ref[block, :HD]], axis=1)
            cached = jnp.dot(cache_pick, pair, preferred_element_type=jnp.float32).astype(jnp.bfloat16)
            kc_ref[slots, columns] = cached[:, :HD]
            vc_ref[slots, columns] = cached[:, HD:]
        allowed_ref[slots, :] = jnp.dot(query_pick, reach, preferred_element_type=jnp.float32).astype(
            jnp.bfloat16
        )

    first = lead_heads(heads)
    copies = []

    def store(s, slots, h, value):
        half_ref[slots, h * HD : (h + 1) * HD] = value
        if h == first - 1:
            copy = pltpu.make_async_copy(
                half_ref.at[slots, :], att_hbm.at[slots, : first * HD], sent.at[s]
            )
            copy.start()
            copies.append(copy)

    halves = (slice(0, heads // 2), keys, vals), (slice(heads // 2, first), keys_ref, vals_ref)
    for span, k_ref, v_ref in halves:
        attend_head(instances, capacity, span, wanted_ref, k_ref, v_ref, allowed_ref, store)
    for copy in copies:
        copy.wait()


def rest_kernel(instances, capacity, heads, me_ref, *rest):
    got, rest = rest[:instances], rest[instances:]
    _, allowed_ref, keys_ref, vals_ref, att_hbm, wanted_ref, mine_ref, sent = rest
    first = lead_heads(heads)
    count = heads - first
    for k, piece in zip((0, 1, *SECOND), got):
        start = 0 if k in SECOND else first * capacity + 16
        wanted_ref[jnp.bitwise_xor(me_ref[0], k)] = piece[start : start + count * capacity, :]
    copies = []

    def store(s, slots, h, value):
        mine_ref[slots, h * HD : (h + 1) * HD] = value
        if h == count - 1:
            copy = pltpu.make_async_copy(
                mine_ref.at[slots, :], att_hbm.at[slots, first * HD :], sent.at[s]
            )
            copy.start()
            copies.append(copy)

    attend_head(
        instances, capacity, slice(0, count), wanted_ref, keys_ref, vals_ref, allowed_ref, store
    )
    for copy in copies:
        copy.wait()


def few_instances(queries, keys, values, query_owner, cache_owner):
    instances = lax.axis_size("seq")
    rows = queries.shape[0]
    capacity = 3 * rows // (2 * instances)
    heads = queries.shape[1] // HD
    first = lead_heads(heads)
    tall, short = first * capacity, (heads - first) * capacity
    slots = instances * capacity

    def swap(array, k):
        return lax.ppermute(array, "seq", [(i, i ^ k) for i in range(instances)])

    vmem = pl.BlockSpec(memory_space=pltpu.VMEM)
    smem = pl.BlockSpec(memory_space=pltpu.SMEM)
    hbm = pl.BlockSpec(memory_space=pltpu.HBM)
    shape = lambda *dims: jax.ShapeDtypeStruct(dims, jnp.bfloat16)
    me = lax.axis_index("seq").astype(jnp.int32).reshape(1)
    own_kv = jnp.concatenate([keys, values], axis=1)
    far_kv, near_kv = swap(own_kv, 2), swap(own_kv, 1)
    distances = (*range(instances), *SECOND)
    sends = pl.pallas_call(
        functools.partial(pack_kernel, instances, capacity),
        out_shape=tuple(
            shape(tall + 16 + short * (k not in SECOND), HD) for k in range(instances)
        )
        + (shape(short, HD),) * len(SECOND),
        in_specs=[smem, hbm, vmem, vmem],
        out_specs=(vmem,) * len(distances),
        scratch_shapes=[pltpu.VMEM(queries.shape, jnp.bfloat16), pltpu.SemaphoreType.DMA],
        compiler_params=pltpu.CompilerParams(vmem_limit_bytes=16 << 20),
        cost_estimate=pl.CostEstimate(flops=1 << 27, bytes_accessed=2 << 20, transcendentals=0),
        name="pack",
    )(me, queries, query_owner.reshape(1, rows), cache_owner.reshape(1, rows))
    anyspace = pl.BlockSpec(memory_space=pl.ANY)
    passed_kv = pl.pallas_call(
        gate_kernel,
        out_shape=shape(*far_kv.shape),
        in_specs=[anyspace] * 2,
        out_specs=anyspace,
        input_output_aliases={1: 0},
        compiler_params=pltpu.CompilerParams(vmem_limit_bytes=16 << 20),
        cost_estimate=pl.CostEstimate(flops=0, bytes_accessed=0, transcendentals=0),
        name="gate",
    )(near_kv, far_kv)
    both_kv = swap(passed_kv, 1)
    got = [swap(piece, k) if k else piece for k, piece in zip(distances, sends)]
    attended, allowed, keys_rest, vals_rest, key_cache, value_cache = pl.pallas_call(
        functools.partial(lead_kernel, instances, capacity, heads),
        out_shape=(
            shape(slots, heads * HD),
            shape(slots, 2 * rows),
            shape(instances * rows, HD),
            shape(instances * rows, 2 * HD),
            shape(slots, 2 * HD),
            shape(slots, 2 * HD),
        ),
        in_specs=[smem] + [vmem] * (2 * instances),
        out_specs=(hbm,) + (vmem,) * 5,
        scratch_shapes=[
            pltpu.VMEM((instances, tall + 16, HD), jnp.bfloat16),
            pltpu.VMEM((instances * rows, HD), jnp.bfloat16),
            pltpu.VMEM((instances * rows, 2 * HD), jnp.bfloat16),
            pltpu.VMEM((slots, first * HD), jnp.bfloat16),
            pltpu.SemaphoreType.DMA((instances,)),
        ],
        compiler_params=pltpu.CompilerParams(vmem_limit_bytes=24 << 20),
        cost_estimate=pl.CostEstimate(flops=1 << 29, bytes_accessed=2 << 20, transcendentals=1 << 19),
        name="attend_lead",
    )(me, *got[:instances], own_kv, near_kv, passed_kv, both_kv)
    attended = pl.pallas_call(
        functools.partial(rest_kernel, instances, capacity, heads),
        out_shape=shape(slots, heads * HD),
        in_specs=[smem] + [vmem] * instances + [hbm] + [vmem] * 3,
        out_specs=hbm,
        input_output_aliases={instances + 1: 0},
        scratch_shapes=[
            pltpu.VMEM((instances, short, HD), jnp.bfloat16),
            pltpu.VMEM((slots, (heads - first) * HD), jnp.bfloat16),
            pltpu.SemaphoreType.DMA((instances,)),
        ],
        compiler_params=pltpu.CompilerParams(vmem_limit_bytes=24 << 20),
        cost_estimate=pl.CostEstimate(flops=1 << 29, bytes_accessed=2 << 20, transcendentals=1 << 19),
        name="attend_rest",
    )(me, *got[:2], *got[instances:], attended, allowed, keys_rest, vals_rest)
    return (attended, key_cache, value_cache)


def on_device(queries, keys, values, query_owner, cache_owner):
    instances = lax.axis_size("seq")
    rows = queries.shape[0]
    capacity = 3 * rows // (2 * instances)
    heads = queries.shape[1] // HD
    whole_tiles = (
        instances == 4
        and capacity % 16 == 0
        and rows == HD
        and keys.shape[1] == 2 * HD
        and heads % 16 == 0
    )
    form = few_instances if whole_tiles else many_instances
    return form(queries, keys, values, query_owner, cache_owner)


def solution(mesh):
    return jax.shard_map(
        on_device,
        mesh=mesh,
        in_specs=(
            P(("groups", "seq"), ("tp", "rep")),
            P(("groups", "seq"), ("tp", "rep")),
            P(("groups", "seq"), ("tp", "rep")),
            P(("groups", "seq"), None),
            P(("groups", "seq"), None),
        ),
        out_specs=(
            P(("groups", "seq"), ("tp", "rep")),
            P(("groups", "seq"), ("tp", "rep")),
            P(("groups", "seq"), ("tp", "rep")),
        ),
        check_vma=False,
    )
```
